32 devices in a mesh: rep: 4 (over y, core), tp: 8 (over z, x).
Axes of the slice: x: 2, y: 2, z: 4, core: 2. Of those that a mesh axis runs over, the one named last changes fastest.
Arguments:
- tokens: bfloat16 [4096, 2048], P(('rep', 'tp')), may hold values from -6 to 6
- seg_ids: int32 [4096], replicated, may hold values from 0 to 15, never falling along the last dimension, each value on 1 to 1024 neighbouring positions
- expert_ids: int32 [4096, 8], P(('rep', 'tp')), may hold values from 0 to 31, all different within a row; in each aligned block of 128 rows (0 to 127, 128 to 255, ...) at most 48 rows name the same one
- gates: bfloat16 [4096, 8], P(('rep', 'tp')), may hold values from 0.099609375 to 0.59765625
- page_table: int32 [256], P(('rep', 'tp')), may hold values from 0 to 7, as said below
- attn_gain: float32 [2048], replicated, may hold values from 0.5 to 1.5
- q_gain: float32 [128], replicated, may hold values from 0.5 to 6, as said below
- key_norm_gain: float32 [128], replicated, may hold values from 0.5 to 6, as said below
- w_query: bfloat16 [2048, 4096], P(None, 'tp'), may hold values from -1 to 1
- w_keyval: bfloat16 [2048, 1024], replicated, may hold values from -1 to 1
- w_out: bfloat16 [4096, 2048], P('tp'), may hold values from -0.09375 to 0.09375
- moe_gain: float32 [2048], replicated, may hold values from 0.5 to 1.5
- w_gate_up: bfloat16 [32, 2048, 1536], P(('rep', 'tp')), may hold values from -0.125 to 0.125
- w_down: bfloat16 [32, 768, 2048], P(('rep', 'tp')), may hold values from -0.21875 to 0.21875
Outputs:
- hidden_out: bfloat16 [4096, 2048], P(('rep', 'tp'))
- cache: bfloat16 [256, 16, 1024], P(('rep', 'tp'))
The draws below stay inside these ranges and needn't reach their ends.
Inputs may be any that keep to these rules, and one draw needn't show every extreme that they name: `seg_ids`: never falling; each request has at most 1024 tokens and some request has exactly 1024. `expert_ids`: a token's 8 experts differ; in the rows of one device no expert appears more than 48 times. `page_table`: the 8 entries of each device name each of its slots once. `q_gain`: positive. `key_norm_gain`: positive.
All inputs are finite; a program needn't handle non-finite values.
Results may differ from the reference program's by a relative error of at most 0.022.
Values may be sent and summed in bfloat16 or wider, within the bound.
No kernel may reach another device: no remote copies, remote signals or barrier semaphores. Data moves between devices by JAX's collectives and lax.ppermute only.
A program may use at most 128 MiB of HBM per device.

```python
import math
import jax
import jax.numpy as jnp
import numpy as np
from jax import lax

MODEL_WIDTH = 2048
QUERY_HEADS = 32
KEY_VALUE_HEADS = 4
HEAD_SIZE = 128
FE = 768
TOP = 8
PAGE_TOKENS = 16
TOK_DEV = 128
TG = 1024
PACKED_TOKENS = 4096
EXPERTS = 32
CAP = 48
TOTAL_PAGES = 256
PAGES_DEV = 8
SEGS = 16
N_REP = 4
N_TP = 8


def query_offset(key):
    value_rows = jax.random.normal(jax.random.fold_in(key, 11), (MODEL_WIDTH, QUERY_HEADS * HEAD_SIZE), jnp.float32)
    return jnp.clip(value_rows, -6.0, 6.0) * MODEL_WIDTH ** (-0.5)


def draw_w_query(key, part):
    return query_offset(key).astype(jnp.bfloat16)


def draw_w_keyval(key, part):
    value_rows = jax.random.normal(jax.random.fold_in(key, 12), (MODEL_WIDTH, 2 * KEY_VALUE_HEADS * HEAD_SIZE), jnp.float32)
    value_rows = jnp.clip(value_rows, -6.0, 6.0) * MODEL_WIDTH ** (-0.5)
    return value_rows.astype(jnp.bfloat16)


def gain_draw(key, salt):
    value_rows = jax.random.normal(jax.random.fold_in(key, salt), (HEAD_SIZE,), jnp.float32)
    return 1.0 + 0.15 * jnp.clip(value_rows, -3.0, 3.0)


def draw_q_gain(key, part):
    return gain_draw(key, 21)


def draw_key_norm_gain(key, part):
    return gain_draw(key, 22)


def draw_page_table(key, part):
    key_list = jax.random.split(jax.random.fold_in(key, 31), PACKED_TOKENS // TOK_DEV)
    orders = jax.vmap(lambda single: jax.random.permutation(single, PAGES_DEV))(key_list)
    return orders.reshape(-1).astype(jnp.int32)


def steps_of(key, shape, cuts, least, high):
    def one(axis_at, parts):
        steps = jax.random.uniform(jax.random.fold_in(jax.random.fold_in(key, 6), axis_at), (parts,), jnp.float32, least / len(cuts), high / len(cuts))
        return jnp.repeat(jnp.exp(steps), shape[axis_at] // parts).reshape((-1,) + (1,) * (len(shape) - axis_at - 1))

    factor_of = one(*cuts[0])
    for cut in cuts[1:]:
        factor_of = factor_of * one(*cut)
    return factor_of


def split_up(count, total, reach, slope):
    portions = [(1 << 20) // math.isqrt(grade ** slope) + 1 for grade in range(2, count + 1)]
    spare, given = total - reach - (count - 1), [1] * (count - 1)
    while spare > 0:
        free = [i for i in range(count - 1) if given[i] < reach]
        mass, left = sum([portions[i] for i in free]), spare
        for i in free:
            extra = min(reach - given[i], max(1, left * portions[i] // mass), spare)
            given[i] = given[i] + extra
            spare = spare - extra
    return np.array([reach] + given)


def ragged(own_key, amount, total, bound, slope):
    if amount == 2:
        one = jax.random.randint(own_key, (), max(1, total - bound), min(bound, total - 1) + 1)
        return jnp.stack([one, total - one])
    sizes = jnp.asarray(split_up(amount, total, bound, slope), jnp.int32)
    twos = (amount - 1) // 2
    source_of, taker = sizes[1:1 + 2 * twos:2], sizes[2:2 + 2 * twos:2]
    room = jnp.minimum(source_of - 1, bound - taker)
    shifted = jax.random.randint(jax.random.fold_in(own_key, 1), (twos,), 0, 1 << 20) % (room + 1)
    sizes = sizes.at[1:1 + 2 * twos:2].set(source_of - shifted).at[2:2 + 2 * twos:2].set(taker + shifted)
    return sizes[jax.random.permutation(jax.random.fold_in(own_key, 2), amount)]


def routed_block(own_key, own, number, rows, number_of, top, bound, lean):
    order = jax.random.permutation(own_key, number_of)
    crowded, ordinary = portions_of(number_of, rows * top, bound, lean, True), portions_of(number_of, rows * top, bound, lean, False)
    places = jnp.arange(number_of)

    def named(sizes, rotation):
        used = int((sizes > 0).sum())
        fixed = max(1, used // 4)
        passed = fixed + (places - fixed + rotation * (used - fixed)) % max(1, number_of - fixed)
        return jnp.zeros((number_of,), jnp.int32).at[order[jnp.where(places < fixed, places, passed)]].set(jnp.asarray(sizes, jnp.int32))

    sizes = jnp.where(number % 4 == 0, named(crowded, number // 4), named(ordinary, number - number // 4 - 1))
    mixed = jax.random.permutation(jax.random.fold_in(own, 3), number_of)
    source_of, receiver = mixed[0:number_of // 2 * 2:2], mixed[1:number_of // 2 * 2:2]
    room = jnp.minimum(sizes[source_of] - 1, bound - sizes[receiver]) // 2
    room = jnp.where((source_of == order[0]) | (receiver == order[0]) | (sizes[receiver] == 0), 0, jnp.maximum(room, 0))
    passed = jax.random.randint(jax.random.fold_in(own, 4), (number_of // 2,), 0, 1 << 20) % (room + 1)
    sizes = sizes.at[source_of].add(-passed).at[receiver].add(passed)
    members = jnp.searchsorted(jnp.cumsum(sizes), jnp.arange(rows * top), side="right").astype(jnp.int32)
    listing = members.reshape(top, rows).T
    listing = listing[jax.random.permutation(jax.random.fold_in(own, 1), rows)]
    rotation = jax.random.randint(jax.random.fold_in(own, 2), (rows, 1), 0, top)
    return jnp.take_along_axis(listing, (jnp.arange(top)[None, :] + rotation) % top, axis=1)


def portions_of(amount, total, limit, skew, full):
    loads = [(1 << 20) // math.isqrt(standing ** skew) + 1 for standing in range(1, amount + 1)]
    largest = limit if full else min(limit, max(-(-total // amount), total * loads[0] // sum(loads)))
    least = 1 if total - largest >= amount - 1 else 0
    holding, spare = [largest] + [least] * (amount - 1), total - largest - least * (amount - 1)
    while spare > 0:
        candidates = [i for i in range(1, amount) if holding[i] < largest] or [i for i in range(1, amount) if holding[i] < limit]
        whole, budget = sum([loads[i] for i in candidates]), spare
        for i in candidates:
            addition = min(limit - holding[i], max(1, budget * loads[i] // whole), spare)
            holding[i] = holding[i] + addition
            spare = spare - addition
    return np.array(holding)


def bell_draw(own_key, extent, width, limit, cuts=(), kind=jnp.bfloat16):
    entries = jax.random.normal(own_key, extent, jnp.float32) * width
    if len(cuts) > 0:
        entries = steps_of(own_key, extent, cuts, -0.22, 0.18) * entries
    return jnp.clip(entries, min=-limit, max=limit).astype(kind)


def setup_inputs(seed: int = 0) -> dict:
    keys = jax.random.split(jax.random.key(seed), 15)
    tokens = bell_draw(keys[0], (PACKED_TOKENS, MODEL_WIDTH), 1.0, 6.0, ((0, 32),))
    seg_ids = jnp.searchsorted(jnp.cumsum(ragged(keys[1], SEGS, PACKED_TOKENS, TG, 2)), jnp.arange(PACKED_TOKENS), side="right").astype(jnp.int32)
    expert_ids_keys = jax.random.split(jax.random.fold_in(keys[2], 1), PACKED_TOKENS // TOK_DEV)
    expert_ids_turns = jax.random.permutation(jax.random.fold_in(keys[2], 3), PACKED_TOKENS // TOK_DEV)
    expert_ids = jax.vmap(lambda own, number: routed_block(jax.random.fold_in(keys[2], 2), own, number, TOK_DEV, EXPERTS, TOP, CAP, 1))(expert_ids_keys, expert_ids_turns).reshape((PACKED_TOKENS, TOP))
    gates = jnp.clip(0.099609375 + 0.49804688 * jax.random.uniform(keys[3], (PACKED_TOKENS, TOP), jnp.float32) ** steps_of(keys[3], (PACKED_TOKENS, TOP), ((0, 32),), -0.2, 0.2), 0.099609375, 0.59765625).astype(jnp.bfloat16)
    page_table = draw_page_table(jax.random.fold_in(keys[14], 71), 0)
    attn_gain = jnp.clip(1.0 + 0.1 * jax.random.normal(keys[5], (MODEL_WIDTH,), jnp.float32), 0.5, 1.5)
    q_gain = draw_q_gain(jax.random.fold_in(keys[14], 71), 0)
    key_norm_gain = draw_key_norm_gain(jax.random.fold_in(keys[14], 71), 0)
    w_query = draw_w_query(jax.random.fold_in(keys[14], 71), 0)
    w_keyval = draw_w_keyval(jax.random.fold_in(keys[14], 71), 0)
    w_out = bell_draw(keys[10], (QUERY_HEADS * HEAD_SIZE, MODEL_WIDTH), (QUERY_HEADS * HEAD_SIZE) ** -0.5, 0.09375, ((0, 8),))
    moe_gain = jnp.clip(1.0 + 0.1 * jax.random.normal(keys[11], (MODEL_WIDTH,), jnp.float32), 0.5, 1.5)
    w_gate_up = bell_draw(keys[12], (EXPERTS, MODEL_WIDTH, 2 * FE), MODEL_WIDTH ** -0.5, 0.125, ((0, 32),))
    w_down = bell_draw(keys[13], (EXPERTS, FE, MODEL_WIDTH), FE ** -0.5, 0.21875, ((0, 32),))
    return dict(tokens=tokens, seg_ids=seg_ids, expert_ids=expert_ids, gates=gates, page_table=page_table, attn_gain=attn_gain, q_gain=q_gain, key_norm_gain=key_norm_gain, w_query=w_query, w_keyval=w_keyval, w_out=w_out, moe_gain=moe_gain, w_gate_up=w_gate_up, w_down=w_down)


def root_mean_norm(value_rows, gain):
    return value_rows * lax.rsqrt(lax.optimization_barrier(jnp.mean(value_rows * value_rows, axis=-1, keepdims=True)) + 1e-06) * gain

def apply_rotary(value_rows, token_positions):
    half_dim = value_rows.shape[-1] // 2
    frequency = jnp.exp(jnp.arange(half_dim, dtype=jnp.float32) * (-2.0 * math.log(1000000.0) / value_rows.shape[-1]))
    angles = token_positions[:, None] * frequency[None, :]
    cosine = jnp.cos(angles)[:, None, :]
    sine_part = jnp.sin(angles)[:, None, :]
    first = value_rows[..., :half_dim]
    second = value_rows[..., half_dim:]
    return jnp.concatenate([first * cosine - second * sine_part, second * cosine + first * sine_part], axis=-1)

def reference(tokens, seg_ids, expert_ids, gates, page_table, attn_gain, q_gain, key_norm_gain, w_query, w_keyval, w_out, moe_gain, w_gate_up, w_down):
    token_positions = jnp.arange(PACKED_TOKENS, dtype=jnp.int32).astype(jnp.float32)
    normed = root_mean_norm(tokens.astype(jnp.float32), attn_gain).astype(jnp.bfloat16)
    query = jnp.dot(normed, w_query, preferred_element_type=jnp.float32).reshape(PACKED_TOKENS, QUERY_HEADS, HEAD_SIZE)
    query = apply_rotary(root_mean_norm(query, q_gain), token_positions).astype(jnp.bfloat16)
    key_value_rows = jnp.dot(normed, w_keyval, preferred_element_type=jnp.float32)
    rotary_output = apply_rotary(root_mean_norm(key_value_rows[:, :KEY_VALUE_HEADS * HEAD_SIZE].reshape(PACKED_TOKENS, KEY_VALUE_HEADS, HEAD_SIZE), key_norm_gain), token_positions)
    stored_cache = jnp.concatenate([rotary_output.reshape(PACKED_TOKENS, KEY_VALUE_HEADS * HEAD_SIZE), key_value_rows[:, KEY_VALUE_HEADS * HEAD_SIZE:]], axis=1).astype(jnp.bfloat16)
    cache_pages = stored_cache.reshape(TOTAL_PAGES, PAGE_TOKENS, 2 * KEY_VALUE_HEADS * HEAD_SIZE)
    slots = jnp.arange(TOTAL_PAGES, dtype=jnp.int32) // PAGES_DEV * PAGES_DEV + page_table.astype(jnp.int32)
    cache = jnp.zeros_like(cache_pages).at[slots].set(cache_pages)
    block_rows = min(512, TG)
    scale = HEAD_SIZE ** (-0.5)
    per_key_value = QUERY_HEADS // KEY_VALUE_HEADS
    results = []
    for group in range(N_REP):
        lower_row = max(group - 1, 0) * TG
        upper_row = (group + 1) * TG
        row_keys = stored_cache[lower_row:upper_row]
        key_seg = seg_ids[lower_row:upper_row]
        key_pos = jnp.arange(lower_row, upper_row, dtype=jnp.int32)
        query_group = query[group * TG:upper_row]
        query_seg = seg_ids[group * TG:upper_row].reshape(TG // block_rows, block_rows)
        query_pos = jnp.arange(group * TG, upper_row, dtype=jnp.int32).reshape(TG // block_rows, block_rows)

        def one_head(head):
            key_value_index = head // per_key_value
            head_keys = lax.dynamic_slice_in_dim(row_keys, key_value_index * HEAD_SIZE, HEAD_SIZE, 1)
            value_heads = lax.dynamic_slice_in_dim(row_keys, KEY_VALUE_HEADS * HEAD_SIZE + key_value_index * HEAD_SIZE, HEAD_SIZE, 1)
            head_query = lax.dynamic_index_in_dim(query_group, head, 1, keepdims=False).reshape(TG // block_rows, block_rows, HEAD_SIZE)

            def one_block(inputs):
                block_query, block_seg, block_pos = inputs
                scores = jnp.dot(block_query, head_keys.T, preferred_element_type=jnp.float32) * scale
                allowed = (key_seg[None, :] == block_seg[:, None]) & (key_pos[None, :] <= block_pos[:, None])
                scores = jnp.where(allowed, scores, -jnp.inf)
                largest = lax.optimization_barrier(jnp.max(scores, axis=-1, keepdims=True))
                weights = jnp.exp(scores - largest)
                totals = lax.optimization_barrier(jnp.sum(weights, axis=-1, keepdims=True))
                mixed = jnp.dot(weights.astype(jnp.bfloat16), value_heads, preferred_element_type=jnp.float32) / totals
                return mixed.astype(jnp.bfloat16)
            return lax.map(one_block, (head_query, query_seg, query_pos)).reshape(TG, HEAD_SIZE)
        heads_out = lax.map(one_head, jnp.arange(QUERY_HEADS, dtype=jnp.int32))
        results.append(jnp.transpose(heads_out, (1, 0, 2)).reshape(TG, QUERY_HEADS * HEAD_SIZE))
    attended = jnp.concatenate(results, axis=0)
    width_dev = QUERY_HEADS * HEAD_SIZE // N_TP

    def add_part(running, index):
        columns = lax.dynamic_slice_in_dim(attended, index * width_dev, width_dev, 1)
        rows = lax.dynamic_slice_in_dim(w_out, index * width_dev, width_dev, 0)
        term = jnp.dot(columns, rows, preferred_element_type=jnp.float32).astype(jnp.bfloat16)
        term = lax.optimization_barrier(term).astype(jnp.float32)
        return (running + term, None)
    mixed_sum, _ = lax.scan(add_part, jnp.zeros((PACKED_TOKENS, MODEL_WIDTH), jnp.float32), jnp.arange(N_TP, dtype=jnp.int32))
    residual = (tokens.astype(jnp.float32) + mixed_sum).astype(jnp.bfloat16)
    normed_moe = root_mean_norm(residual.astype(jnp.float32), moe_gain).astype(jnp.bfloat16)
    blocks = PACKED_TOKENS // TOK_DEV
    flat = expert_ids.reshape(blocks, TOK_DEV * TOP).astype(jnp.int32)
    onehot = (flat[:, :, None] == jnp.arange(EXPERTS, dtype=jnp.int32)[None, None, :]).astype(jnp.int32)
    rank = lax.optimization_barrier(jnp.sum((jnp.cumsum(onehot, axis=1) - 1) * onehot, axis=2)).astype(jnp.int32)
    block_index = jnp.broadcast_to(jnp.arange(blocks, dtype=jnp.int32)[:, None], flat.shape)
    token_index = block_index * TOK_DEV + jnp.broadcast_to(jnp.arange(TOK_DEV * TOP, dtype=jnp.int32)[None, :] // TOP, flat.shape)
    table = jnp.full((EXPERTS, blocks, CAP), PACKED_TOKENS, jnp.int32).at[flat, block_index, rank].set(token_index)
    weight_table = jnp.zeros((EXPERTS, blocks, CAP), jnp.float32).at[flat, block_index, rank].set(gates.reshape(blocks, TOK_DEV * TOP).astype(jnp.float32))
    padded = jnp.concatenate([normed_moe, jnp.zeros((1, MODEL_WIDTH), jnp.bfloat16)], axis=0)

    def expert_step(running, expert):
        indices = table[expert].reshape(-1)
        rows = padded[indices]
        gate_up = jnp.dot(rows, w_gate_up[expert], preferred_element_type=jnp.float32)
        act = (jax.nn.silu(gate_up[:, :FE]) * gate_up[:, FE:]).astype(jnp.bfloat16)
        expert_out = jnp.dot(act, w_down[expert], preferred_element_type=jnp.float32).astype(jnp.bfloat16)
        running = running.at[indices].add(weight_table[expert].reshape(-1)[:, None] * expert_out.astype(jnp.float32))
        return (running, None)
    moe_sum, _ = lax.scan(expert_step, jnp.zeros((PACKED_TOKENS + 1, MODEL_WIDTH), jnp.float32), jnp.arange(EXPERTS, dtype=jnp.int32))
    hidden_out = (residual.astype(jnp.float32) + moe_sum[:PACKED_TOKENS]).astype(jnp.bfloat16)
    return (hidden_out, cache)
```

```python
import functools
import math

import jax
import jax.numpy as jnp
from jax import lax
from jax.experimental import pallas as pl
from jax.experimental.pallas import tpu as pltpu
from jax.sharding import PartitionSpec as P


def passed_along(block, axis, distance):
    devices = range(lax.axis_size(axis))
    route = [(i - distance, i) for i in devices if i - distance in devices]
    return lax.ppermute(block, axis, route)


def root_mean_norm(value_rows, gain):
    return (
        value_rows
        * lax.rsqrt(jnp.mean(value_rows * value_rows, axis=-1, keepdims=True) + 1e-06)
        * gain
    )


def apply_rotary(value_rows, token_positions):
    half_dim = value_rows.shape[-1] // 2
    frequency = jnp.exp(
        jnp.arange(half_dim, dtype=jnp.float32)
        * (-2.0 * math.log(1000000.0) / value_rows.shape[-1])
    )
    angles = token_positions[:, None] * frequency[None, :]
    cosine = jnp.cos(angles)[:, None, :]
    sine_part = jnp.sin(angles)[:, None, :]
    first = value_rows[..., :half_dim]
    second = value_rows[..., half_dim:]
    return jnp.concatenate(
        [first * cosine - second * sine_part, second * cosine + first * sine_part], axis=-1
    )


def general_body(
    tokens,
    seg_ids,
    expert_ids,
    gates,
    page_table,
    attn_gain,
    q_gain,
    key_norm_gain,
    w_query,
    w_keyval,
    w_out,
    moe_gain,
    w_gate_up,
    w_down,
):
    tok_rows, width = tokens.shape
    tp_count = lax.axis_size("tp")
    rep_count = lax.axis_size("rep")
    rep_index = lax.axis_index("rep")
    tp_index = lax.axis_index("tp")
    group_rows = tok_rows * tp_count
    head_dim = q_gain.shape[0]
    q_width = w_query.shape[1]
    heads_here = q_width // head_dim
    kv_heads = w_keyval.shape[1] // (2 * head_dim)
    kv_width = kv_heads * head_dim
    per_key_value = heads_here * tp_count // kv_heads
    own_head = tp_index * heads_here // per_key_value
    first_row = (rep_index * tp_count + tp_index) * tok_rows
    local_pos = (first_row + jnp.arange(tok_rows, dtype=jnp.int32)).astype(jnp.float32)
    normed = root_mean_norm(tokens.astype(jnp.float32), attn_gain).astype(jnp.bfloat16)
    key_value_rows = jnp.dot(normed, w_keyval, preferred_element_type=jnp.float32)
    rotary_output = apply_rotary(
        root_mean_norm(
            key_value_rows[:, :kv_width].reshape(tok_rows, kv_heads, head_dim), key_norm_gain
        ),
        local_pos,
    )
    stored_cache = jnp.concatenate(
        [rotary_output.reshape(tok_rows, kv_width), key_value_rows[:, kv_width:]], axis=1
    ).astype(jnp.bfloat16)
    page_count = page_table.shape[0]
    placement_matrix = (
        page_table[None, :] == jnp.arange(page_count, dtype=jnp.int32)[:, None]
    ).astype(jnp.bfloat16)
    cache = jnp.dot(
        placement_matrix, stored_cache.reshape(page_count, -1), preferred_element_type=jnp.float32
    )
    cache = cache.astype(jnp.bfloat16).reshape(page_count, tok_rows // page_count, 2 * kv_width)
    projected = jnp.dot(
        lax.all_gather(normed, "tp", axis=0, tiled=True),
        w_query,
        preferred_element_type=jnp.float32,
    )
    group_start = rep_index * group_rows
    group_pos = group_start + jnp.arange(group_rows, dtype=jnp.int32)
    group_posf = group_pos.astype(jnp.float32)
    query = root_mean_norm(projected.reshape(group_rows, heads_here, head_dim), q_gain)
    query = apply_rotary(query, group_posf).astype(jnp.bfloat16)
    gathered = lax.all_gather(stored_cache, "tp", axis=0, tiled=True)
    own_keys = lax.dynamic_slice_in_dim(gathered, own_head * head_dim, head_dim, 1)
    own_values = lax.dynamic_slice_in_dim(gathered, kv_width + own_head * head_dim, head_dim, 1)
    earlier_keys, earlier_values = passed_along((own_keys, own_values), "rep", 1)
    own_seg = lax.dynamic_slice_in_dim(seg_ids, group_start, group_rows, 0)
    earlier_seg = lax.dynamic_slice_in_dim(
        seg_ids, jnp.maximum(group_start - group_rows, 0), group_rows, 0
    )
    earlier_seg = jnp.where(rep_index > 0, earlier_seg, -1)
    keys_all = jnp.concatenate([earlier_keys, own_keys], axis=0)
    values_all = jnp.concatenate([earlier_values, own_values], axis=0)
    key_seg = jnp.concatenate([earlier_seg, own_seg], axis=0)
    key_pos = group_start - group_rows + jnp.arange(2 * group_rows, dtype=jnp.int32)
    block_rows = min(512, group_rows)
    block_count = group_rows // block_rows
    scale = head_dim ** (-0.5)

    def attend(inputs):
        block_query, block_pos, block_seg = inputs
        scores = (
            jnp.einsum("bhd,kd->hbk", block_query, keys_all, preferred_element_type=jnp.float32)
            * scale
        )
        allowed = (key_seg[None, :] == block_seg[:, None]) & (
            key_pos[None, :] <= block_pos[:, None]
        )
        scores = jnp.where(allowed[None], scores, -jnp.inf)
        largest = jnp.max(scores, axis=-1, keepdims=True)
        weights = jnp.exp(scores - largest)
        totals = jnp.sum(weights, axis=-1, keepdims=True)
        mixed = (
            jnp.einsum(
                "hbk,kd->hbd",
                weights.astype(jnp.bfloat16),
                values_all,
                preferred_element_type=jnp.float32,
            )
            / totals
        )
        return jnp.transpose(mixed.astype(jnp.bfloat16), (1, 0, 2)).reshape(
            block_rows, heads_here * head_dim
        )

    attended = lax.map(
        attend,
        (
            query.reshape(block_count, block_rows, heads_here, head_dim),
            group_pos.reshape(block_count, block_rows),
            own_seg.reshape(block_count, block_rows),
        ),
    )
    attended = attended.reshape(group_rows, heads_here * head_dim)
    rows = attended
    term = jnp.dot(rows, w_out, preferred_element_type=jnp.float32).astype(jnp.bfloat16)
    mixed_sum = lax.psum_scatter(
        lax.optimization_barrier(term).astype(jnp.float32).astype(jnp.bfloat16),
        "tp",
        scatter_dimension=0,
        tiled=True,
    ).astype(jnp.float32)
    residual = (tokens.astype(jnp.float32) + mixed_sum).astype(jnp.bfloat16)
    normed_moe = root_mean_norm(residual.astype(jnp.float32), moe_gain).astype(jnp.bfloat16)
    expert_count = rep_count * tp_count * w_gate_up.shape[0]
    top_count = expert_ids.shape[1]
    capacity = max(2, 3 * tok_rows * top_count // (2 * expert_count))
    hidden_units = w_down.shape[1]
    flat = expert_ids.reshape(-1)
    onehot = (flat[:, None] == jnp.arange(expert_count, dtype=jnp.int32)[None, :]).astype(jnp.int32)
    rank = jnp.sum((jnp.cumsum(onehot, axis=0) - 1) * onehot, axis=1)
    target = (flat * capacity + rank).reshape(tok_rows, top_count)
    match = (
        target[:, :, None] == jnp.arange(expert_count * capacity, dtype=jnp.int32)[None, None, :]
    )
    dispatch = jnp.any(match, axis=1).astype(jnp.bfloat16)
    combine = jnp.sum(jnp.where(match, gates[:, :, None].astype(jnp.float32), 0.0), axis=1).astype(
        jnp.bfloat16
    )
    outgoing = lax.dot_general(
        dispatch, normed_moe, (((0,), (0,)), ((), ())), preferred_element_type=jnp.float32
    )
    outgoing = outgoing.astype(jnp.bfloat16).reshape(expert_count, capacity, width)
    received = lax.all_to_all(outgoing, ("rep", "tp"), split_axis=0, concat_axis=0, tiled=True)
    rows = received.reshape(-1, width)
    gate_up = jnp.dot(rows, w_gate_up[0], preferred_element_type=jnp.float32)
    act = (jax.nn.silu(gate_up[:, :hidden_units]) * gate_up[:, hidden_units:]).astype(jnp.bfloat16)
    result = jnp.dot(act, w_down[0], preferred_element_type=jnp.float32).astype(jnp.bfloat16)
    returned = lax.all_to_all(
        result.reshape(received.shape), ("rep", "tp"), split_axis=0, concat_axis=0, tiled=True
    )
    combined = jnp.dot(
        combine,
        returned.reshape(expert_count * capacity, width),
        preferred_element_type=jnp.float32,
    )
    hidden_out = (residual.astype(jnp.float32) + combined).astype(jnp.bfloat16)
    return (hidden_out, cache)


KEY_BLOCK = 256
MASKED = -1e30


def moved(block, change):
    route = []
    for y in range(2):
        for core in range(2):
            for z in range(4):
                for x in range(2):
                    to_y, to_core, to_z, to_x = change(y, core, z, x)
                    route.append(
                        ((y * 2 + core) * 8 + z * 2 + x, (to_y * 2 + to_core) * 8 + to_z * 2 + to_x)
                    )
    return lax.ppermute(block, ("rep", "tp"), route)


def other_x(block):
    return moved(block, lambda y, core, z, x: (y, core, z, 1 - x))


def other_y(block):
    return moved(block, lambda y, core, z, x: (1 - y, core, z, x))


def other_core(block):
    return moved(block, lambda y, core, z, x: (y, 1 - core, z, x))


def other_z(block, k):
    return moved(block, lambda y, core, z, x: (y, core, z ^ k, x))


def after(value, earlier):
    return lax.optimization_barrier((value, earlier))[0]


def attention_kernel(
    place, low, projected, gain, cosine, sine, start, kv_here, kv_side, kv_before, kv_before_side, out,
    keys, values, acc, peak, total,
):
    slot = pl.program_id(0)
    z, x = place[0], place[1]
    rows = projected.shape[0]
    head = gain.shape[0]
    heads = projected.shape[1] // head
    half = head // 2

    @pl.when(slot == 0)
    def _():
        for first, near, far in ((0, kv_before, kv_before_side), (8, kv_here, kv_side)):
            for k in range(4):
                at = jnp.bitwise_xor(z, k) * 2
                for source, shift in ((near, x), (far, 1 - x)):
                    row = pl.multiple_of((first + at + shift) * rows, rows)
                    keys[pl.ds(row, rows), :] = source[k, :, :head]
                    values[:, pl.ds(row, rows)] = source[k, :, head:].astype(jnp.float32).T.astype(jnp.bfloat16)

    turned = []
    for h in range(heads):
        q = projected[:, h * head : (h + 1) * head].T
        q = q * lax.rsqrt(jnp.mean(q * q, axis=0, keepdims=True) + 1e-06) * gain[...]
        first, second = q[:half], q[half:]
        turned.append(
            jnp.concatenate(
                [first * cosine[0] - second * sine[0], second * cosine[0] + first * sine[0]], axis=0
            )
        )
    query = (jnp.concatenate(turned, axis=1) * (head**-0.5 * math.log2(math.e))).astype(jnp.bfloat16)
    acc[...] = jnp.zeros_like(acc)
    total[...] = jnp.zeros_like(total)
    peak[...] = jnp.full_like(peak, MASKED)
    position = (8 + jnp.bitwise_xor(z, slot) * 2 + x) * rows
    own_position = position + lax.broadcasted_iota(jnp.int32, (KEY_BLOCK, rows), 1)
    own_start = start[0]

    def step(j, _):
        row = pl.multiple_of(j * KEY_BLOCK, KEY_BLOCK)
        scores = jnp.dot(keys[pl.ds(row, KEY_BLOCK), :], query, preferred_element_type=jnp.float32)
        key_position = row + lax.broadcasted_iota(jnp.int32, (KEY_BLOCK, rows), 0)
        allowed = (key_position >= own_start) & (key_position <= own_position)
        scores = jnp.concatenate(
            [jnp.where(allowed, scores[:, h * rows : (h + 1) * rows], MASKED) for h in range(heads)], axis=1
        )
        largest = jnp.maximum(peak[...], jnp.max(scores, axis=0, keepdims=True))
        fade = jnp.exp2(peak[...] - largest)
        weights = jnp.exp2(scores - largest)
        total[...] = total[...] * fade + jnp.sum(weights, axis=0, keepdims=True)
        acc[...] = acc[...] * fade + jnp.dot(
            values[:, pl.ds(row, KEY_BLOCK)], weights.astype(jnp.bfloat16), preferred_element_type=jnp.float32
        )
        peak[...] = largest
        return 0

    lax.fori_loop(low[slot], (position + rows - 1) // KEY_BLOCK + 1, step, 0)
    mixed = acc[...] / total[...]
    for h in range(heads):
        out[:, h * head : (h + 1) * head] = mixed[:, h * rows : (h + 1) * rows].T.astype(out.dtype)


def attend_slots(place, low, projected, q_gain, cosine, sine, start, kv):
    slots, rows = start.shape[0], start.shape[2]
    head = q_gain.shape[0]
    width = projected.shape[1]
    whole = lambda *shape: pl.BlockSpec(shape, lambda s, *_: (0,) * len(shape))
    return pl.pallas_call(
        attention_kernel,
        grid_spec=pltpu.PrefetchScalarGridSpec(
            num_scalar_prefetch=2,
            grid=(slots,),
            in_specs=[
                pl.BlockSpec((rows, width), lambda s, *_: (s, 0)),
                whole(head, 1),
                pl.BlockSpec((1, head // 2, rows), lambda s, *_: (s, 0, 0)),
                pl.BlockSpec((1, head // 2, rows), lambda s, *_: (s, 0, 0)),
                pl.BlockSpec((1, 1, rows), lambda s, *_: (s, 0, 0)),
            ]
            + [whole(*part.shape) for part in kv],
            out_specs=pl.BlockSpec((rows, width), lambda s, *_: (s, 0)),
            scratch_shapes=[
                pltpu.VMEM((16 * rows, head), jnp.bfloat16),
                pltpu.VMEM((head, 16 * rows), jnp.bfloat16),
                pltpu.VMEM((head, width // head * rows), jnp.float32),
                pltpu.VMEM((1, width // head * rows), jnp.float32),
                pltpu.VMEM((1, width // head * rows), jnp.float32),
            ],
        ),
        out_shape=jax.ShapeDtypeStruct((slots * rows, width), jnp.bfloat16),
        compiler_params=pltpu.CompilerParams(vmem_limit_bytes=40 * 2**20),
        cost_estimate=pl.CostEstimate(
            flops=4 * slots * rows * width * 4 * rows,
            bytes_accessed=8 * 2**20,
            transcendentals=slots * width * rows,
        ),
        name="attention",
    )(place, low, projected, q_gain.reshape(head, 1), cosine, sine, start, *kv)


def grid_body(
    tokens,
    seg_ids,
    expert_ids,
    gates,
    page_table,
    attn_gain,
    q_gain,
    key_norm_gain,
    w_query,
    w_keyval,
    w_out,
    moe_gain,
    w_gate_up,
    w_down,
):
    rows, width = tokens.shape
    head = q_gain.shape[0]
    kv_heads = w_keyval.shape[1] // (2 * head)
    kv_width = kv_heads * head
    rep, tp = lax.axis_index("rep"), lax.axis_index("tp")
    y, core, z, x = rep // 2, rep % 2, tp // 2, tp % 2
    group_rows = 8 * rows
    group_start = rep * group_rows
    slots = range(4)

    raw = [tokens] + [other_z(tokens, k) for k in (1, 2, 3)]
    half_heads = w_query.shape[1] // 2
    query_half = other_x(lax.dynamic_slice_in_dim(w_query, core * half_heads, half_heads, 1))
    query_rest = other_core(query_half)
    out_half = other_x(
        after(lax.dynamic_slice_in_dim(w_out, core * half_heads, half_heads, 0), query_half)
    )
    out_rest = other_core(out_half)

    routes = jnp.concatenate([expert_ids.T.astype(jnp.bfloat16), gates.T], axis=0)
    routes = lax.all_gather(routes, ("rep", "tp"), axis=0, tiled=True)

    normed = root_mean_norm(tokens.astype(jnp.float32), attn_gain).astype(jnp.bfloat16)
    own_position = (group_start + tp * rows + jnp.arange(rows, dtype=jnp.int32)).astype(jnp.float32)
    keyval = jnp.dot(normed, w_keyval, preferred_element_type=jnp.float32)
    rotated = apply_rotary(
        root_mean_norm(keyval[:, :kv_width].reshape(rows, kv_heads, head), key_norm_gain), own_position
    )
    stored = jnp.concatenate([rotated.reshape(rows, kv_width), keyval[:, kv_width:]], axis=1).astype(
        jnp.bfloat16
    )
    pages = page_table.shape[0]
    placing = (page_table[None, :] == jnp.arange(pages, dtype=jnp.int32)[:, None]).astype(jnp.bfloat16)
    cache = jnp.dot(placing, stored.reshape(pages, -1), preferred_element_type=jnp.float32)
    cache = cache.astype(jnp.bfloat16).reshape(pages, rows // pages, 2 * kv_width)

    by_head = jnp.transpose(stored.reshape(rows, 2, kv_heads, head), (2, 0, 1, 3))
    by_head = by_head.reshape(kv_heads, rows, 2 * head)
    pick = lambda h: lax.dynamic_index_in_dim(by_head, h, 0, keepdims=False)
    kv_here = jnp.stack([pick(z)] + [other_z(pick(z ^ k), k) for k in (1, 2, 3)])
    kv_before = passed_along(kv_here, "rep", 1)
    kv_side = other_x(kv_here)
    kv_before_side = other_x(kv_before)

    slot_z = jnp.stack([z ^ k for k in slots])
    slot_rows = ((slot_z * 2 + x) * rows)[:, None] + jnp.arange(rows, dtype=jnp.int32)[None, :]
    slot_position = group_start + slot_rows
    frequency = jnp.exp(
        jnp.arange(head // 2, dtype=jnp.float32) * (-2.0 * math.log(1000000.0) / head)
    )
    angles = frequency[None, :, None] * slot_position.astype(jnp.float32)[:, None, :]
    slot_seg = jnp.take(seg_ids, slot_position.reshape(-1), axis=0)
    starts = jnp.sum((seg_ids[None, :] < slot_seg[:, None]).astype(jnp.int32), axis=1)
    starts = (starts - (group_start - group_rows)).reshape(4, 1, rows)
    low = starts[:, 0, 0] // KEY_BLOCK
    lines = jnp.concatenate(raw, axis=0).astype(jnp.float32)
    normed_lines = root_mean_norm(lines, attn_gain).astype(jnp.bfloat16)
    w_query_wide = jnp.concatenate([w_query, query_half, query_rest], axis=1)
    projected = jnp.dot(normed_lines, w_query_wide, preferred_element_type=jnp.float32)
    attended = attend_slots(
        jnp.stack([z, x]),
        low,
        projected,
        q_gain,
        jnp.cos(angles),
        jnp.sin(angles),
        starts,
        (kv_here, kv_side, kv_before, kv_before_side),
    )
    w_out_wide = jnp.concatenate([w_out, out_half, out_rest], axis=0)
    term = jnp.dot(attended, w_out_wide, preferred_element_type=jnp.float32).astype(jnp.bfloat16)
    term = term.reshape(4, rows, width)
    mixed_sum = term[0].astype(jnp.float32)
    for k in (1, 2, 3):
        mixed_sum = mixed_sum + other_z(term[k], k).astype(jnp.float32)
    residual = (tokens.astype(jnp.float32) + mixed_sum).astype(jnp.bfloat16)
    normed_moe = root_mean_norm(residual.astype(jnp.float32), moe_gain).astype(jnp.bfloat16)

    top = expert_ids.shape[1]
    capacity = max(2, 3 * rows * top // (2 * 32))
    routes = routes.reshape(32, 2, top, rows)
    block_of = jnp.stack(
        [
            ((y ^ dy) * 2 + core) * 8 + (z ^ k) * 2 + (x ^ dx)
            for k in slots
            for dy, dx in ((0, 0), (0, 1), (1, 0), (1, 1))
        ]
    )
    routes = jnp.take(routes, block_of, axis=0)
    experts = jnp.stack([rep * 8 + tp, (rep ^ 1) * 8 + tp])
    hits = routes[:, 0][:, None] == experts.astype(jnp.bfloat16)[None, :, None, None]
    weight = jnp.sum(jnp.where(hits, routes[:, 1][:, None].astype(jnp.float32), 0.0), axis=2)
    hit = jnp.any(hits, axis=2)
    earlier = jnp.arange(rows)[:, None] < jnp.arange(rows)[None, :]
    place = jnp.dot(
        hit.reshape(-1, rows).astype(jnp.bfloat16),
        earlier.astype(jnp.bfloat16),
        preferred_element_type=jnp.float32,
    ).reshape(16, 2, rows)
    chosen = (
        place[:, :, None, :].astype(jnp.int32) == jnp.arange(capacity, dtype=jnp.int32)[None, None, :, None]
    ) & hit[:, :, None, :]
    weighted = jnp.where(chosen, weight[:, :, None, :], 0.0).astype(jnp.bfloat16)
    weighted = weighted.reshape(4, 4, 2, capacity, rows)
    chosen = chosen.astype(jnp.bfloat16).reshape(4, 4, 2 * capacity, rows)

    def experts_of(slot_rows_in):
        gate_up = jnp.dot(slot_rows_in, w_gate_up[0], preferred_element_type=jnp.float32)
        hidden = w_down.shape[1]
        act = (jax.nn.silu(gate_up[:, :hidden]) * gate_up[:, hidden:]).astype(jnp.bfloat16)
        return jnp.dot(act, w_down[0], preferred_element_type=jnp.float32).astype(jnp.bfloat16)

    half = rows // 2
    arrived = [normed_moe]
    for k in (1, 2, 3):
        arrived.append(other_z(after(normed_moe, arrived[-1]) if k > 1 else normed_moe, k))
    partial = []
    for k in slots:
        block = arrived[k]
        side_x, side_y = other_x(block), other_y(block)
        corner = jnp.concatenate([other_y(side_x[:half]), other_x(side_y[half:])], axis=0)
        blocks = jnp.stack([block, side_x, side_y, corner])
        picked = lax.dot_general(
            chosen[k], blocks, (((2,), (1,)), ((0,), (0,))), preferred_element_type=jnp.float32
        ).astype(jnp.bfloat16)
        kept = picked[:, :capacity].reshape(-1, width)
        traded = other_core(picked[:, capacity:].reshape(-1, width))
        result = experts_of(jnp.concatenate([kept, traded], axis=0))
        back = other_core(result[4 * capacity :])
        both = jnp.stack([result[: 4 * capacity], back]).reshape(2, 4, capacity, width)
        partial.append(
            lax.dot_general(
                weighted[k],
                jnp.transpose(both, (1, 0, 2, 3)),
                (((1, 2), (1, 2)), ((0,), (0,))),
                preferred_element_type=jnp.float32,
            ).astype(jnp.bfloat16)
        )
    combined = residual.astype(jnp.float32)
    for k in (1, 2, 3, 0):
        here, to_x, to_y, to_corner = (partial[k][v] for v in range(4))
        by_y, by_x = other_y(to_corner[:half]), other_x(to_corner[half:])
        add = lambda a, b: (a.astype(jnp.float32) + b.astype(jnp.float32)).astype(jnp.bfloat16)
        from_x = other_x(jnp.concatenate([add(to_x[:half], by_y), to_x[half:]], axis=0))
        from_y = other_y(jnp.concatenate([to_y[:half], add(to_y[half:], by_x)], axis=0))
        total = here.astype(jnp.float32) + from_x.astype(jnp.float32) + from_y.astype(jnp.float32)
        if k:
            total = other_z(total.astype(jnp.bfloat16), k).astype(jnp.float32)
        combined = combined + total
    return (combined.astype(jnp.bfloat16), cache)


def solution(mesh):
    in_specs = (
        P(("rep", "tp"), None),
        P(),
        P(("rep", "tp"), None),
        P(("rep", "tp"), None),
        P(("rep", "tp")),
        P(),
        P(),
        P(),
        P(None, "tp"),
        P(),
        P("tp", None),
        P(),
        P(("rep", "tp"), None, None),
        P(("rep", "tp"), None, None),
    )
    out_specs = (P(("rep", "tp"), None), P(("rep", "tp"), None, None))
    body = grid_body if (mesh.shape["rep"], mesh.shape["tp"]) == (4, 8) else general_body
    return jax.shard_map(body, mesh=mesh, in_specs=in_specs, out_specs=out_specs, check_vma=False)
```

```python
import functools
import math

import jax
import jax.numpy as jnp
from jax import lax
from jax.experimental import pallas as pl
from jax.experimental.pallas import tpu as pltpu
from jax.sharding import PartitionSpec as P


def passed_along(block, axis, distance):
    devices = range(lax.axis_size(axis))
    route = [(i - distance, i) for i in devices if i - distance in devices]
    return lax.ppermute(block, axis, route)


def root_mean_norm(value_rows, gain):
    return (
        value_rows
        * lax.rsqrt(jnp.mean(value_rows * value_rows, axis=-1, keepdims=True) + 1e-06)
        * gain
    )


def apply_rotary(value_rows, token_positions):
    half_dim = value_rows.shape[-1] // 2
    frequency = jnp.exp(
        jnp.arange(half_dim, dtype=jnp.float32)
        * (-2.0 * math.log(1000000.0) / value_rows.shape[-1])
    )
    angles = token_positions[:, None] * frequency[None, :]
    cosine = jnp.cos(angles)[:, None, :]
    sine_part = jnp.sin(angles)[:, None, :]
    first = value_rows[..., :half_dim]
    second = value_rows[..., half_dim:]
    return jnp.concatenate(
        [first * cosine - second * sine_part, second * cosine + first * sine_part], axis=-1
    )


def general_body(
    tokens,
    seg_ids,
    expert_ids,
    gates,
    page_table,
    attn_gain,
    q_gain,
    key_norm_gain,
    w_query,
    w_keyval,
    w_out,
    moe_gain,
    w_gate_up,
    w_down,
):
    tok_rows, width = tokens.shape
    tp_count = lax.axis_size("tp")
    rep_count = lax.axis_size("rep")
    rep_index = lax.axis_index("rep")
    tp_index = lax.axis_index("tp")
    group_rows = tok_rows * tp_count
    head_dim = q_gain.shape[0]
    q_width = w_query.shape[1]
    heads_here = q_width // head_dim
    kv_heads = w_keyval.shape[1] // (2 * head_dim)
    kv_width = kv_heads * head_dim
    per_key_value = heads_here * tp_count // kv_heads
    own_head = tp_index * heads_here // per_key_value
    first_row = (rep_index * tp_count + tp_index) * tok_rows
    local_pos = (first_row + jnp.arange(tok_rows, dtype=jnp.int32)).astype(jnp.float32)
    normed = root_mean_norm(tokens.astype(jnp.float32), attn_gain).astype(jnp.bfloat16)
    key_value_rows = jnp.dot(normed, w_keyval, preferred_element_type=jnp.float32)
    rotary_output = apply_rotary(
        root_mean_norm(
            key_value_rows[:, :kv_width].reshape(tok_rows, kv_heads, head_dim), key_norm_gain
        ),
        local_pos,
    )
    stored_cache = jnp.concatenate(
        [rotary_output.reshape(tok_rows, kv_width), key_value_rows[:, kv_width:]], axis=1
    ).astype(jnp.bfloat16)
    page_count = page_table.shape[0]
    placement_matrix = (
        page_table[None, :] == jnp.arange(page_count, dtype=jnp.int32)[:, None]
    ).astype(jnp.bfloat16)
    cache = jnp.dot(
        placement_matrix, stored_cache.reshape(page_count, -1), preferred_element_type=jnp.float32
    )
    cache = cache.astype(jnp.bfloat16).reshape(page_count, tok_rows // page_count, 2 * kv_width)
    projected = jnp.dot(
        lax.all_gather(normed, "tp", axis=0, tiled=True),
        w_query,
        preferred_element_type=jnp.float32,
    )
    group_start = rep_index * group_rows
    group_pos = group_start + jnp.arange(group_rows, dtype=jnp.int32)
    group_posf = group_pos.astype(jnp.float32)
    query = root_mean_norm(projected.reshape(group_rows, heads_here, head_dim), q_gain)
    query = apply_rotary(query, group_posf).astype(jnp.bfloat16)
    gathered = lax.all_gather(stored_cache, "tp", axis=0, tiled=True)
    own_keys = lax.dynamic_slice_in_dim(gathered, own_head * head_dim, head_dim, 1)
    own_values = lax.dynamic_slice_in_dim(gathered, kv_width + own_head * head_dim, head_dim, 1)
    earlier_keys, earlier_values = passed_along((own_keys, own_values), "rep", 1)
    own_seg = lax.dynamic_slice_in_dim(seg_ids, group_start, group_rows, 0)
    earlier_seg = lax.dynamic_slice_in_dim(
        seg_ids, jnp.maximum(group_start - group_rows, 0), group_rows, 0
    )
    earlier_seg = jnp.where(rep_index > 0, earlier_seg, -1)
    keys_all = jnp.concatenate([earlier_keys, own_keys], axis=0)
    values_all = jnp.concatenate([earlier_values, own_values], axis=0)
    key_seg = jnp.concatenate([earlier_seg, own_seg], axis=0)
    key_pos = group_start - group_rows + jnp.arange(2 * group_rows, dtype=jnp.int32)
    block_rows = min(512, group_rows)
    block_count = group_rows // block_rows
    scale = head_dim ** (-0.5)

    def attend(inputs):
        block_query, block_pos, block_seg = inputs
        scores = (
            jnp.einsum("bhd,kd->hbk", block_query, keys_all, preferred_element_type=jnp.float32)
            * scale
        )
        allowed = (key_seg[None, :] == block_seg[:, None]) & (
            key_pos[None, :] <= block_pos[:, None]
        )
        scores = jnp.where(allowed[None], scores, -jnp.inf)
        largest = jnp.max(scores, axis=-1, keepdims=True)
        weights = jnp.exp(scores - largest)
        totals = jnp.sum(weights, axis=-1, keepdims=True)
        mixed = (
            jnp.einsum(
                "hbk,kd->hbd",
                weights.astype(jnp.bfloat16),
                values_all,
                preferred_element_type=jnp.float32,
            )
            / totals
        )
        return jnp.transpose(mixed.astype(jnp.bfloat16), (1, 0, 2)).reshape(
            block_rows, heads_here * head_dim
        )

    attended = lax.map(
        attend,
        (
            query.reshape(block_count, block_rows, heads_here, head_dim),
            group_pos.reshape(block_count, block_rows),
            own_seg.reshape(block_count, block_rows),
        ),
    )
    attended = attended.reshape(group_rows, heads_here * head_dim)
    rows = attended
    term = jnp.dot(rows, w_out, preferred_element_type=jnp.float32).astype(jnp.bfloat16)
    mixed_sum = lax.psum_scatter(
        lax.optimization_barrier(term).astype(jnp.float32).astype(jnp.bfloat16),
        "tp",
        scatter_dimension=0,
        tiled=True,
    ).astype(jnp.float32)
    residual = (tokens.astype(jnp.float32) + mixed_sum).astype(jnp.bfloat16)
    normed_moe = root_mean_norm(residual.astype(jnp.float32), moe_gain).astype(jnp.bfloat16)
    expert_count = rep_count * tp_count * w_gate_up.shape[0]
    top_count = expert_ids.shape[1]
    capacity = max(2, 3 * tok_rows * top_count // (2 * expert_count))
    hidden_units = w_down.shape[1]
    flat = expert_ids.reshape(-1)
    onehot = (flat[:, None] == jnp.arange(expert_count, dtype=jnp.int32)[None, :]).astype(jnp.int32)
    rank = jnp.sum((jnp.cumsum(onehot, axis=0) - 1) * onehot, axis=1)
    target = (flat * capacity + rank).reshape(tok_rows, top_count)
    match = (
        target[:, :, None] == jnp.arange(expert_count * capacity, dtype=jnp.int32)[None, None, :]
    )
    dispatch = jnp.any(match, axis=1).astype(jnp.bfloat16)
    combine = jnp.sum(jnp.where(match, gates[:, :, None].astype(jnp.float32), 0.0), axis=1).astype(
        jnp.bfloat16
    )
    outgoing = lax.dot_general(
        dispatch, normed_moe, (((0,), (0,)), ((), ())), preferred_element_type=jnp.float32
    )
    outgoing = outgoing.astype(jnp.bfloat16).reshape(expert_count, capacity, width)
    received = lax.all_to_all(outgoing, ("rep", "tp"), split_axis=0, concat_axis=0, tiled=True)
    rows = received.reshape(-1, width)
    gate_up = jnp.dot(rows, w_gate_up[0], preferred_element_type=jnp.float32)
    act = (jax.nn.silu(gate_up[:, :hidden_units]) * gate_up[:, hidden_units:]).astype(jnp.bfloat16)
    result = jnp.dot(act, w_down[0], preferred_element_type=jnp.float32).astype(jnp.bfloat16)
    returned = lax.all_to_all(
        result.reshape(received.shape), ("rep", "tp"), split_axis=0, concat_axis=0, tiled=True
    )
    combined = jnp.dot(
        combine,
        returned.reshape(expert_count * capacity, width),
        preferred_element_type=jnp.float32,
    )
    hidden_out = (residual.astype(jnp.float32) + combined).astype(jnp.bfloat16)
    return (hidden_out, cache)


KEY_BLOCK = 256
MASKED = -1e30


def moved(block, change):
    route = []
    for y in range(2):
        for core in range(2):
            for z in range(4):
                for x in range(2):
                    to_y, to_core, to_z, to_x = change(y, core, z, x)
                    route.append(
                        ((y * 2 + core) * 8 + z * 2 + x, (to_y * 2 + to_core) * 8 + to_z * 2 + to_x)
                    )
    return lax.ppermute(block, ("rep", "tp"), route)


def other_x(block):
    return moved(block, lambda y, core, z, x: (y, core, z, 1 - x))


def other_y(block):
    return moved(block, lambda y, core, z, x: (1 - y, core, z, x))


def other_core(block):
    return moved(block, lambda y, core, z, x: (y, 1 - core, z, x))


def other_z(block, k):
    return moved(block, lambda y, core, z, x: (y, core, z ^ k, x))


def after(value, earlier):
    return lax.optimization_barrier((value, earlier))[0]


def attention_kernel(
    place, low, projected, gain, cosine, sine, start, kv_here, kv_side, kv_before, kv_before_side, out,
    keys, values, acc, peak, total,
):
    z, x, slot = place[0], place[1], place[2] + pl.program_id(0)
    rows = projected.shape[0]
    head = gain.shape[0]
    heads = projected.shape[1] // head
    half = head // 2

    @pl.when(pl.program_id(0) == 0)
    def _():
        for first, near, far in ((0, kv_before, kv_before_side), (8, kv_here, kv_side)):
            for k in range(4):
                at = jnp.bitwise_xor(z, k) * 2
                for source, shift in ((near, x), (far, 1 - x)):
                    row = pl.multiple_of((first + at + shift) * rows, rows)
                    keys[pl.ds(row, rows), :] = source[k, :, :head]
                    values[:, pl.ds(row, rows)] = source[k, :, head:].astype(jnp.float32).T.astype(jnp.bfloat16)

    turned = []
    for h in range(heads):
        q = projected[:, h * head : (h + 1) * head].T
        q = q * lax.rsqrt(jnp.mean(q * q, axis=0, keepdims=True) + 1e-06) * gain[...]
        first, second = q[:half], q[half:]
        turned.append(
            jnp.concatenate(
                [first * cosine[0] - second * sine[0], second * cosine[0] + first * sine[0]], axis=0
            )
        )
    query = (jnp.concatenate(turned, axis=1) * (head**-0.5 * math.log2(math.e))).astype(jnp.bfloat16)
    acc[...] = jnp.zeros_like(acc)
    total[...] = jnp.zeros_like(total)
    peak[...] = jnp.full_like(peak, MASKED)
    position = (8 + jnp.bitwise_xor(z, slot) * 2 + x) * rows
    own_position = position + lax.broadcasted_iota(jnp.int32, (KEY_BLOCK, rows), 1)
    own_start = start[0]

    def step(j, _):
        row = pl.multiple_of(j * KEY_BLOCK, KEY_BLOCK)
        scores = jnp.dot(keys[pl.ds(row, KEY_BLOCK), :], query, preferred_element_type=jnp.float32)
        key_position = row + lax.broadcasted_iota(jnp.int32, (KEY_BLOCK, rows), 0)
        allowed = (key_position >= own_start) & (key_position <= own_position)
        scores = jnp.concatenate(
            [jnp.where(allowed, scores[:, h * rows : (h + 1) * rows], MASKED) for h in range(heads)], axis=1
        )
        largest = jnp.maximum(peak[...], jnp.max(scores, axis=0, keepdims=True))
        fade = jnp.exp2(peak[...] - largest)
        weights = jnp.exp2(scores - largest)
        total[...] = total[...] * fade + jnp.sum(weights, axis=0, keepdims=True)
        acc[...] = acc[...] * fade + jnp.dot(
            values[:, pl.ds(row, KEY_BLOCK)], weights.astype(jnp.bfloat16), preferred_element_type=jnp.float32
        )
        peak[...] = largest
        return 0

    lax.fori_loop(low[pl.program_id(0)], (position + rows - 1) // KEY_BLOCK + 1, step, 0)
    mixed = acc[...] / total[...]
    for h in range(heads):
        out[:, h * head : (h + 1) * head] = mixed[:, h * rows : (h + 1) * rows].T.astype(out.dtype)


def attend_slots(place, low, projected, q_gain, cosine, sine, start, kv):
    slots, rows = start.shape[0], start.shape[2]
    head = q_gain.shape[0]
    width = projected.shape[1]
    whole = lambda *shape: pl.BlockSpec(shape, lambda s, *_: (0,) * len(shape))
    return pl.pallas_call(
        attention_kernel,
        grid_spec=pltpu.PrefetchScalarGridSpec(
            num_scalar_prefetch=2,
            grid=(slots,),
            in_specs=[
                pl.BlockSpec((rows, width), lambda s, *_: (s, 0)),
                whole(head, 1),
                pl.BlockSpec((1, head // 2, rows), lambda s, *_: (s, 0, 0)),
                pl.BlockSpec((1, head // 2, rows), lambda s, *_: (s, 0, 0)),
                pl.BlockSpec((1, 1, rows), lambda s, *_: (s, 0, 0)),
            ]
            + [whole(*part.shape) for part in kv],
            out_specs=pl.BlockSpec((rows, width), lambda s, *_: (s, 0)),
            scratch_shapes=[
                pltpu.VMEM((16 * rows, head), jnp.bfloat16),
                pltpu.VMEM((head, 16 * rows), jnp.bfloat16),
                pltpu.VMEM((head, width // head * rows), jnp.float32),
                pltpu.VMEM((1, width // head * rows), jnp.float32),
                pltpu.VMEM((1, width // head * rows), jnp.float32),
            ],
        ),
        out_shape=jax.ShapeDtypeStruct((slots * rows, width), jnp.bfloat16),
        compiler_params=pltpu.CompilerParams(vmem_limit_bytes=40 * 2**20),
        cost_estimate=pl.CostEstimate(
            flops=4 * slots * rows * width * 4 * rows,
            bytes_accessed=8 * 2**20,
            transcendentals=slots * width * rows,
        ),
        name="attention",
    )(place, low, projected, q_gain.reshape(head, 1), cosine, sine, start, *kv)


def keyval_kernel(tokens, gain, key_gain, cosine, sine, w_key, w_value, out, normed):
    @pl.when(pl.program_id(0) == 0)
    def _():
        normed[...] = root_mean_norm(tokens[...].astype(jnp.float32), gain[...]).astype(jnp.bfloat16)

    head = key_gain.shape[0]
    half = head // 2
    k = jnp.dot(normed[...], w_key[...], preferred_element_type=jnp.float32).T
    k = k * lax.rsqrt(jnp.mean(k * k, axis=0, keepdims=True) + 1e-06) * key_gain[...]
    first, second = k[:half], k[half:]
    k = jnp.concatenate(
        [first * cosine[0] - second * sine[0], second * cosine[0] + first * sine[0]], axis=0
    )
    out[0, :, :head] = k.T.astype(out.dtype)
    v = jnp.dot(normed[...], w_value[...], preferred_element_type=jnp.float32)
    out[0, :, head:] = v.astype(out.dtype)


def keyval_by_head(tokens, attn_gain, key_norm_gain, cosine, sine, w_keyval):
    rows, width = tokens.shape
    head = key_norm_gain.shape[0]
    heads = w_keyval.shape[1] // (2 * head)
    whole = lambda *shape: pl.BlockSpec(shape, lambda h: (0,) * len(shape))
    return pl.pallas_call(
        keyval_kernel,
        grid=(heads,),
        in_specs=[
            whole(rows, width),
            whole(1, width),
            whole(head, 1),
            whole(1, head // 2, rows),
            whole(1, head // 2, rows),
            pl.BlockSpec((width, head), lambda h: (0, h)),
            pl.BlockSpec((width, head), lambda h: (0, heads + h)),
        ],
        out_specs=pl.BlockSpec((1, rows, 2 * head), lambda h: (h, 0, 0)),
        out_shape=jax.ShapeDtypeStruct((heads, rows, 2 * head), jnp.bfloat16),
        scratch_shapes=[pltpu.VMEM((rows, width), jnp.bfloat16)],
        compiler_params=pltpu.CompilerParams(vmem_limit_bytes=32 * 2**20),
        cost_estimate=pl.CostEstimate(
            flops=2 * rows * width * w_keyval.shape[1], bytes_accessed=5 * 2**20, transcendentals=0
        ),
        name="keyval",
    )(tokens, attn_gain.reshape(1, width), key_norm_gain.reshape(head, 1), cosine, sine, w_keyval, w_keyval)


def grid_body(
    tokens,
    seg_ids,
    expert_ids,
    gates,
    page_table,
    attn_gain,
    q_gain,
    key_norm_gain,
    w_query,
    w_keyval,
    w_out,
    moe_gain,
    w_gate_up,
    w_down,
):
    rows, width = tokens.shape
    head = q_gain.shape[0]
    kv_heads = w_keyval.shape[1] // (2 * head)
    kv_width = kv_heads * head
    rep, tp = lax.axis_index("rep"), lax.axis_index("tp")
    y, core, z, x = rep // 2, rep % 2, tp // 2, tp % 2
    group_rows = 8 * rows
    group_start = rep * group_rows
    slots = range(4)

    raw = [tokens] + [other_z(tokens, k) for k in (1, 2, 3)]

    slot_z = jnp.stack([z ^ k for k in slots])
    slot_position = group_start + ((slot_z * 2 + x) * rows)[:, None] + jnp.arange(rows, dtype=jnp.int32)
    frequency = jnp.exp(
        jnp.arange(head // 2, dtype=jnp.float32) * (-2.0 * math.log(1000000.0) / head)
    )
    angles = frequency[None, :, None] * slot_position.astype(jnp.float32)[:, None, :]
    cosine, sine = jnp.cos(angles), jnp.sin(angles)

    by_head = keyval_by_head(tokens, attn_gain, key_norm_gain, cosine[:1], sine[:1], w_keyval)
    pick = lambda h: lax.dynamic_index_in_dim(by_head, h, 0, keepdims=False)
    kv_here = jnp.stack([pick(z)] + [other_z(pick(z ^ k), k) for k in (1, 2, 3)])
    kv_before = passed_along(kv_here, "rep", 1)
    kv_side = other_x(kv_here)
    kv_before_side = other_x(kv_before)

    half_heads = w_query.shape[1] // 2
    query_half = other_x(
        lax.dynamic_slice_in_dim(after(w_query, by_head), core * half_heads, half_heads, 1)
    )
    query_rest = other_core(query_half)
    out_half = other_x(
        lax.dynamic_slice_in_dim(after(w_out, query_half), core * half_heads, half_heads, 0)
    )
    out_rest = other_core(out_half)

    top = expert_ids.shape[1]
    routes = jnp.concatenate([expert_ids.T.astype(jnp.bfloat16), gates.T], axis=0)
    routes = after(routes, by_head)
    routes = jnp.stack([routes] + [other_z(routes, k) for k in (1, 2, 3)])
    routes = jnp.stack([routes, other_x(routes)], axis=1)
    routes = jnp.concatenate([routes, other_y(routes)], axis=1).reshape(16, 2, top, rows)

    pages = page_table.shape[0]
    stored = jnp.transpose(by_head.reshape(kv_heads, rows, 2, head), (1, 2, 0, 3))
    placing = (page_table[None, :] == jnp.arange(pages, dtype=jnp.int32)[:, None]).astype(jnp.bfloat16)
    cache = jnp.dot(placing, stored.reshape(pages, -1), preferred_element_type=jnp.float32)
    cache = cache.astype(jnp.bfloat16).reshape(pages, rows // pages, 2 * kv_width)

    slot_seg = jnp.take(seg_ids, slot_position.reshape(-1), axis=0)
    starts = jnp.sum((seg_ids[None, :] < slot_seg[:, None]).astype(jnp.int32), axis=1)
    starts = (starts - (group_start - group_rows)).reshape(4, 1, rows)
    low = starts[:, 0, 0] // KEY_BLOCK
    w_query_wide = jnp.concatenate([w_query, query_half, query_rest], axis=1)
    w_out_wide = jnp.concatenate([w_out, out_half, out_rest], axis=0)

    def attended(first):
        two = slice(first, first + 2)
        lines = jnp.concatenate(raw[two], axis=0).astype(jnp.float32)
        lines = root_mean_norm(lines, attn_gain).astype(jnp.bfloat16)
        projected = jnp.dot(lines, w_query_wide, preferred_element_type=jnp.float32)
        return attend_slots(
            jnp.stack([z, x, jnp.int32(first)]),
            low[two],
            projected,
            q_gain,
            cosine[two],
            sine[two],
            starts[two],
            (kv_here, kv_side, kv_before, kv_before_side),
        )

    def term_of(part):
        term = jnp.dot(part, w_out_wide, preferred_element_type=jnp.float32).astype(jnp.bfloat16)
        return term[:rows], term[rows:]

    early = attended(0)
    term_2, term_3 = term_of(attended(2))
    far = [other_z(term_2, 2), other_z(term_3, 3)]
    term_0, term_1 = term_of(after(early, term_3))
    mixed_sum = term_0.astype(jnp.float32)
    for part in [other_z(term_1, 1)] + far:
        mixed_sum = mixed_sum + part.astype(jnp.float32)
    residual = (tokens.astype(jnp.float32) + mixed_sum).astype(jnp.bfloat16)
    normed_moe = root_mean_norm(residual.astype(jnp.float32), moe_gain).astype(jnp.bfloat16)

    capacity = max(2, 3 * rows * top // (2 * 32))
    experts = jnp.stack([rep * 8 + tp, (rep ^ 1) * 8 + tp])
    hits = routes[:, 0][:, None] == experts.astype(jnp.bfloat16)[None, :, None, None]
    weight = jnp.sum(jnp.where(hits, routes[:, 1][:, None].astype(jnp.float32), 0.0), axis=2)
    hit = jnp.any(hits, axis=2)
    earlier = jnp.arange(rows)[:, None] < jnp.arange(rows)[None, :]
    place = jnp.dot(
        hit.reshape(-1, rows).astype(jnp.bfloat16),
        earlier.astype(jnp.bfloat16),
        preferred_element_type=jnp.float32,
    ).reshape(16, 2, rows)
    chosen = (
        place[:, :, None, :].astype(jnp.int32) == jnp.arange(capacity, dtype=jnp.int32)[None, None, :, None]
    ) & hit[:, :, None, :]
    weighted = jnp.where(chosen, weight[:, :, None, :], 0.0).astype(jnp.bfloat16)
    weighted = weighted.reshape(4, 4, 2, capacity, rows)
    chosen = chosen.astype(jnp.bfloat16).reshape(4, 4, 2 * capacity, rows)

    def experts_of(slot_rows_in):
        gate_up = jnp.dot(slot_rows_in, w_gate_up[0], preferred_element_type=jnp.float32)
        hidden = w_down.shape[1]
        act = (jax.nn.silu(gate_up[:, :hidden]) * gate_up[:, hidden:]).astype(jnp.bfloat16)
        return jnp.dot(act, w_down[0], preferred_element_type=jnp.float32).astype(jnp.bfloat16)

    half = rows // 2
    arrived = [normed_moe, other_z(normed_moe, 1)]
    arrived.append(other_z(after(normed_moe, arrived[1]), 2))
    arrived.append(other_z(after(normed_moe, arrived[2]), 3))
    partial = []
    turn = normed_moe
    for k in slots:
        block, turn = lax.optimization_barrier((arrived[k], turn))
        side_x, side_y = other_x(block), other_y(block)
        turn = side_x
        corner = jnp.concatenate([other_y(side_x[:half]), other_x(side_y[half:])], axis=0)
        blocks = jnp.stack([block, side_x, side_y, corner])
        picked = lax.dot_general(
            chosen[k], blocks, (((2,), (1,)), ((0,), (0,))), preferred_element_type=jnp.float32
        ).astype(jnp.bfloat16)
        kept = picked[:, :capacity].reshape(-1, width)
        traded = other_core(picked[:, capacity:].reshape(-1, width))
        result = experts_of(jnp.concatenate([kept, traded], axis=0))
        back = other_core(result[4 * capacity :])
        both = jnp.stack([result[: 4 * capacity], back]).reshape(2, 4, capacity, width)
        partial.append(
            lax.dot_general(
                weighted[k],
                jnp.transpose(both, (1, 0, 2, 3)),
                (((1, 2), (1, 2)), ((0,), (0,))),
                preferred_element_type=jnp.float32,
            ).astype(jnp.bfloat16)
        )
    combined = residual.astype(jnp.float32)
    add = lambda a, b: (a.astype(jnp.float32) + b.astype(jnp.float32)).astype(jnp.bfloat16)
    turn = partial[2]
    for k in (2, 3, 1, 0):
        partial_k, turn = lax.optimization_barrier((partial[k], turn))
        here, to_x, to_y, to_corner = (partial_k[v] for v in range(4))
        by_y, by_x = other_y(to_corner[:half]), other_x(to_corner[half:])
        turn = by_x
        from_x = other_x(jnp.concatenate([add(to_x[:half], by_y), to_x[half:]], axis=0))
        from_y = other_y(jnp.concatenate([to_y[:half], add(to_y[half:], by_x)], axis=0))
        total = here.astype(jnp.float32) + from_x.astype(jnp.float32) + from_y.astype(jnp.float32)
        if k:
            total = other_z(total.astype(jnp.bfloat16), k).astype(jnp.float32)
        combined = combined + total
    return (combined.astype(jnp.bfloat16), cache)


def solution(mesh):
    in_specs = (
        P(("rep", "tp"), None),
        P(),
        P(("rep", "tp"), None),
        P(("rep", "tp"), None),
        P(("rep", "tp")),
        P(),
        P(),
        P(),
        P(None, "tp"),
        P(),
        P("tp", None),
        P(),
        P(("rep", "tp"), None, None),
        P(("rep", "tp"), None, None),
    )
    out_specs = (P(("rep", "tp"), None), P(("rep", "tp"), None, None))
    body = grid_body if (mesh.shape["rep"], mesh.shape["tp"]) == (4, 8) else general_body
    return jax.shard_map(body, mesh=mesh, in_specs=in_specs, out_specs=out_specs, check_vma=False)
```

```python
import functools
import math

import jax
import jax.numpy as jnp
from jax import lax
from jax.experimental import pallas as pl
from jax.experimental.pallas import tpu as pltpu
from jax.sharding import PartitionSpec as P


def passed_along(block, axis, distance):
    devices = range(lax.axis_size(axis))
    route = [(i - distance, i) for i in devices if i - distance in devices]
    return lax.ppermute(block, axis, route)


def root_mean_norm(value_rows, gain):
    return (
        value_rows
        * lax.rsqrt(jnp.mean(value_rows * value_rows, axis=-1, keepdims=True) + 1e-06)
        * gain
    )


def apply_rotary(value_rows, token_positions):
    half_dim = value_rows.shape[-1] // 2
    frequency = jnp.exp(
        jnp.arange(half_dim, dtype=jnp.float32)
        * (-2.0 * math.log(1000000.0) / value_rows.shape[-1])
    )
    angles = token_positions[:, None] * frequency[None, :]
    cosine = jnp.cos(angles)[:, None, :]
    sine_part = jnp.sin(angles)[:, None, :]
    first = value_rows[..., :half_dim]
    second = value_rows[..., half_dim:]
    return jnp.concatenate(
        [first * cosine - second * sine_part, second * cosine + first * sine_part], axis=-1
    )


def general_body(
    tokens,
    seg_ids,
    expert_ids,
    gates,
    page_table,
    attn_gain,
    q_gain,
    key_norm_gain,
    w_query,
    w_keyval,
    w_out,
    moe_gain,
    w_gate_up,
    w_down,
):
    tok_rows, width = tokens.shape
    tp_count = lax.axis_size("tp")
    rep_count = lax.axis_size("rep")
    rep_index = lax.axis_index("rep")
    tp_index = lax.axis_index("tp")
    group_rows = tok_rows * tp_count
    head_dim = q_gain.shape[0]
    q_width = w_query.shape[1]
    heads_here = q_width // head_dim
    kv_heads = w_keyval.shape[1] // (2 * head_dim)
    kv_width = kv_heads * head_dim
    per_key_value = heads_here * tp_count // kv_heads
    own_head = tp_index * heads_here // per_key_value
    first_row = (rep_index * tp_count + tp_index) * tok_rows
    local_pos = (first_row + jnp.arange(tok_rows, dtype=jnp.int32)).astype(jnp.float32)
    normed = root_mean_norm(tokens.astype(jnp.float32), attn_gain).astype(jnp.bfloat16)
    key_value_rows = jnp.dot(normed, w_keyval, preferred_element_type=jnp.float32)
    rotary_output = apply_rotary(
        root_mean_norm(
            key_value_rows[:, :kv_width].reshape(tok_rows, kv_heads, head_dim), key_norm_gain
        ),
        local_pos,
    )
    stored_cache = jnp.concatenate(
        [rotary_output.reshape(tok_rows, kv_width), key_value_rows[:, kv_width:]], axis=1
    ).astype(jnp.bfloat16)
    page_count = page_table.shape[0]
    placement_matrix = (
        page_table[None, :] == jnp.arange(page_count, dtype=jnp.int32)[:, None]
    ).astype(jnp.bfloat16)
    cache = jnp.dot(
        placement_matrix, stored_cache.reshape(page_count, -1), preferred_element_type=jnp.float32
    )
    cache = cache.astype(jnp.bfloat16).reshape(page_count, tok_rows // page_count, 2 * kv_width)
    projected = jnp.dot(
        lax.all_gather(normed, "tp", axis=0, tiled=True),
        w_query,
        preferred_element_type=jnp.float32,
    )
    group_start = rep_index * group_rows
    group_pos = group_start + jnp.arange(group_rows, dtype=jnp.int32)
    group_posf = group_pos.astype(jnp.float32)
    query = root_mean_norm(projected.reshape(group_rows, heads_here, head_dim), q_gain)
    query = apply_rotary(query, group_posf).astype(jnp.bfloat16)
    gathered = lax.all_gather(stored_cache, "tp", axis=0, tiled=True)
    own_keys = lax.dynamic_slice_in_dim(gathered, own_head * head_dim, head_dim, 1)
    own_values = lax.dynamic_slice_in_dim(gathered, kv_width + own_head * head_dim, head_dim, 1)
    earlier_keys, earlier_values = passed_along((own_keys, own_values), "rep", 1)
    own_seg = lax.dynamic_slice_in_dim(seg_ids, group_start, group_rows, 0)
    earlier_seg = lax.dynamic_slice_in_dim(
        seg_ids, jnp.maximum(group_start - group_rows, 0), group_rows, 0
    )
    earlier_seg = jnp.where(rep_index > 0, earlier_seg, -1)
    keys_all = jnp.concatenate([earlier_keys, own_keys], axis=0)
    values_all = jnp.concatenate([earlier_values, own_values], axis=0)
    key_seg = jnp.concatenate([earlier_seg, own_seg], axis=0)
    key_pos = group_start - group_rows + jnp.arange(2 * group_rows, dtype=jnp.int32)
    block_rows = min(512, group_rows)
    block_count = group_rows // block_rows
    scale = head_dim ** (-0.5)

    def attend(inputs):
        block_query, block_pos, block_seg = inputs
        scores = (
            jnp.einsum("bhd,kd->hbk", block_query, keys_all, preferred_element_type=jnp.float32)
            * scale
        )
        allowed = (key_seg[None, :] == block_seg[:, None]) & (
            key_pos[None, :] <= block_pos[:, None]
        )
        scores = jnp.where(allowed[None], scores, -jnp.inf)
        largest = jnp.max(scores, axis=-1, keepdims=True)
        weights = jnp.exp(scores - largest)
        totals = jnp.sum(weights, axis=-1, keepdims=True)
        mixed = (
            jnp.einsum(
                "hbk,kd->hbd",
                weights.astype(jnp.bfloat16),
                values_all,
                preferred_element_type=jnp.float32,
            )
            / totals
        )
        return jnp.transpose(mixed.astype(jnp.bfloat16), (1, 0, 2)).reshape(
            block_rows, heads_here * head_dim
        )

    attended = lax.map(
        attend,
        (
            query.reshape(block_count, block_rows, heads_here, head_dim),
            group_pos.reshape(block_count, block_rows),
            own_seg.reshape(block_count, block_rows),
        ),
    )
    attended = attended.reshape(group_rows, heads_here * head_dim)
    rows = attended
    term = jnp.dot(rows, w_out, preferred_element_type=jnp.float32).astype(jnp.bfloat16)
    mixed_sum = lax.psum_scatter(
        lax.optimization_barrier(term).astype(jnp.float32).astype(jnp.bfloat16),
        "tp",
        scatter_dimension=0,
        tiled=True,
    ).astype(jnp.float32)
    residual = (tokens.astype(jnp.float32) + mixed_sum).astype(jnp.bfloat16)
    normed_moe = root_mean_norm(residual.astype(jnp.float32), moe_gain).astype(jnp.bfloat16)
    expert_count = rep_count * tp_count * w_gate_up.shape[0]
    top_count = expert_ids.shape[1]
    capacity = max(2, 3 * tok_rows * top_count // (2 * expert_count))
    hidden_units = w_down.shape[1]
    flat = expert_ids.reshape(-1)
    onehot = (flat[:, None] == jnp.arange(expert_count, dtype=jnp.int32)[None, :]).astype(jnp.int32)
    rank = jnp.sum((jnp.cumsum(onehot, axis=0) - 1) * onehot, axis=1)
    target = (flat * capacity + rank).reshape(tok_rows, top_count)
    match = (
        target[:, :, None] == jnp.arange(expert_count * capacity, dtype=jnp.int32)[None, None, :]
    )
    dispatch = jnp.any(match, axis=1).astype(jnp.bfloat16)
    combine = jnp.sum(jnp.where(match, gates[:, :, None].astype(jnp.float32), 0.0), axis=1).astype(
        jnp.bfloat16
    )
    outgoing = lax.dot_general(
        dispatch, normed_moe, (((0,), (0,)), ((), ())), preferred_element_type=jnp.float32
    )
    outgoing = outgoing.astype(jnp.bfloat16).reshape(expert_count, capacity, width)
    received = lax.all_to_all(outgoing, ("rep", "tp"), split_axis=0, concat_axis=0, tiled=True)
    rows = received.reshape(-1, width)
    gate_up = jnp.dot(rows, w_gate_up[0], preferred_element_type=jnp.float32)
    act = (jax.nn.silu(gate_up[:, :hidden_units]) * gate_up[:, hidden_units:]).astype(jnp.bfloat16)
    result = jnp.dot(act, w_down[0], preferred_element_type=jnp.float32).astype(jnp.bfloat16)
    returned = lax.all_to_all(
        result.reshape(received.shape), ("rep", "tp"), split_axis=0, concat_axis=0, tiled=True
    )
    combined = jnp.dot(
        combine,
        returned.reshape(expert_count * capacity, width),
        preferred_element_type=jnp.float32,
    )
    hidden_out = (residual.astype(jnp.float32) + combined).astype(jnp.bfloat16)
    return (hidden_out, cache)


KEY_BLOCK = 256
MASKED = -1e30


def moved(block, change):
    route = []
    for y in range(2):
        for core in range(2):
            for z in range(4):
                for x in range(2):
                    to_y, to_core, to_z, to_x = change(y, core, z, x)
                    route.append(
                        ((y * 2 + core) * 8 + z * 2 + x, (to_y * 2 + to_core) * 8 + to_z * 2 + to_x)
                    )
    return lax.ppermute(block, ("rep", "tp"), route)


def other_x(block):
    return moved(block, lambda y, core, z, x: (y, core, z, 1 - x))


def other_y(block):
    return moved(block, lambda y, core, z, x: (1 - y, core, z, x))


def other_core(block):
    return moved(block, lambda y, core, z, x: (y, 1 - core, z, x))


def other_z(block, k):
    return moved(block, lambda y, core, z, x: (y, core, z ^ k, x))


def sum_of(a, b):
    return (a.astype(jnp.float32) + b.astype(jnp.float32)).astype(jnp.bfloat16)


def after(value, earlier):
    return lax.optimization_barrier((value, earlier))[0]


def attention_kernel(
    place, low, projected, gain, cosine, sine, start, kv_here, kv_side, kv_before, kv_before_side, out,
    keys, values, acc, peak, total,
):
    z, x, slot = place[0], place[1], place[2] + pl.program_id(0)
    rows = projected.shape[0]
    head = gain.shape[0]
    heads = projected.shape[1] // head
    half = head // 2

    @pl.when(pl.program_id(0) == 0)
    def _():
        for first, near, far in ((0, kv_before, kv_before_side), (8, kv_here, kv_side)):
            for k in range(4):
                at = jnp.bitwise_xor(z, k) * 2
                for source, shift in ((near, x), (far, 1 - x)):
                    row = pl.multiple_of((first + at + shift) * rows, rows)
                    keys[pl.ds(row, rows), :] = source[k, :rows, :head]
                    values[:, pl.ds(row, rows)] = source[k, :rows, head:].astype(jnp.float32).T.astype(jnp.bfloat16)

    turned = []
    for h in range(heads):
        q = projected[:, h * head : (h + 1) * head].T
        q = q * lax.rsqrt(jnp.mean(q * q, axis=0, keepdims=True) + 1e-06) * gain[...]
        first, second = q[:half], q[half:]
        turned.append(
            jnp.concatenate(
                [first * cosine[0] - second * sine[0], second * cosine[0] + first * sine[0]], axis=0
            )
        )
    query = (jnp.concatenate(turned, axis=1) * (head**-0.5 * math.log2(math.e))).astype(jnp.bfloat16)
    acc[...] = jnp.zeros_like(acc)
    total[...] = jnp.zeros_like(total)
    peak[...] = jnp.full_like(peak, MASKED)
    position = (8 + jnp.bitwise_xor(z, slot) * 2 + x) * rows
    own_position = position + lax.broadcasted_iota(jnp.int32, (KEY_BLOCK, rows), 1)
    own_start = start[0]

    def step(j, _):
        row = pl.multiple_of(j * KEY_BLOCK, KEY_BLOCK)
        scores = jnp.dot(keys[pl.ds(row, KEY_BLOCK), :], query, preferred_element_type=jnp.float32)
        key_position = row + lax.broadcasted_iota(jnp.int32, (KEY_BLOCK, rows), 0)
        allowed = (key_position >= own_start) & (key_position <= own_position)
        scores = jnp.concatenate(
            [jnp.where(allowed, scores[:, h * rows : (h + 1) * rows], MASKED) for h in range(heads)], axis=1
        )
        largest = jnp.maximum(peak[...], jnp.max(scores, axis=0, keepdims=True))
        fade = jnp.exp2(peak[...] - largest)
        weights = jnp.exp2(scores - largest)
        total[...] = total[...] * fade + jnp.sum(weights, axis=0, keepdims=True)
        acc[...] = acc[...] * fade + jnp.dot(
            values[:, pl.ds(row, KEY_BLOCK)], weights.astype(jnp.bfloat16), preferred_element_type=jnp.float32
        )
        peak[...] = largest
        return 0

    lax.fori_loop(low[pl.program_id(0)], (position + rows - 1) // KEY_BLOCK + 1, step, 0)
    mixed = acc[...] / total[...]
    for h in range(heads):
        out[:, h * head : (h + 1) * head] = mixed[:, h * rows : (h + 1) * rows].T.astype(out.dtype)


def attend_slots(place, low, projected, q_gain, cosine, sine, start, kv):
    slots, rows = start.shape[0], start.shape[2]
    head = q_gain.shape[0]
    width = projected.shape[1]
    whole = lambda *shape: pl.BlockSpec(shape, lambda s, *_: (0,) * len(shape))
    return pl.pallas_call(
        attention_kernel,
        grid_spec=pltpu.PrefetchScalarGridSpec(
            num_scalar_prefetch=2,
            grid=(slots,),
            in_specs=[
                pl.BlockSpec((rows, width), lambda s, *_: (s, 0)),
                whole(head, 1),
                pl.BlockSpec((1, head // 2, rows), lambda s, *_: (s, 0, 0)),
                pl.BlockSpec((1, head // 2, rows), lambda s, *_: (s, 0, 0)),
                pl.BlockSpec((1, 1, rows), lambda s, *_: (s, 0, 0)),
            ]
            + [whole(*part.shape) for part in kv],
            out_specs=pl.BlockSpec((rows, width), lambda s, *_: (s, 0)),
            scratch_shapes=[
                pltpu.VMEM((16 * rows, head), jnp.bfloat16),
                pltpu.VMEM((head, 16 * rows), jnp.bfloat16),
                pltpu.VMEM((head, width // head * rows), jnp.float32),
                pltpu.VMEM((1, width // head * rows), jnp.float32),
                pltpu.VMEM((1, width // head * rows), jnp.float32),
            ],
        ),
        out_shape=jax.ShapeDtypeStruct((slots * rows, width), jnp.bfloat16),
        compiler_params=pltpu.CompilerParams(vmem_limit_bytes=40 * 2**20),
        cost_estimate=pl.CostEstimate(
            flops=4 * slots * rows * width * 4 * rows,
            bytes_accessed=8 * 2**20,
            transcendentals=slots * width * rows,
        ),
        name="attention",
    )(place, low, projected, q_gain.reshape(head, 1), cosine, sine, start, *kv)


def keyval_kernel(tokens, gain, key_gain, cosine, sine, w_key, w_value, out, normed):
    @pl.when(pl.program_id(0) == 0)
    def _():
        normed[...] = root_mean_norm(tokens[...].astype(jnp.float32), gain[...]).astype(jnp.bfloat16)

    head = key_gain.shape[0]
    half = head // 2
    k = jnp.dot(normed[...], w_key[...], preferred_element_type=jnp.float32).T
    k = k * lax.rsqrt(jnp.mean(k * k, axis=0, keepdims=True) + 1e-06) * key_gain[...]
    first, second = k[:half], k[half:]
    k = jnp.concatenate(
        [first * cosine[0] - second * sine[0], second * cosine[0] + first * sine[0]], axis=0
    )
    out[0, :, :head] = k.T.astype(out.dtype)
    v = jnp.dot(normed[...], w_value[...], preferred_element_type=jnp.float32)
    out[0, :, head:] = v.astype(out.dtype)


def keyval_by_head(tokens, attn_gain, key_norm_gain, cosine, sine, w_keyval):
    rows, width = tokens.shape
    head = key_norm_gain.shape[0]
    heads = w_keyval.shape[1] // (2 * head)
    whole = lambda *shape: pl.BlockSpec(shape, lambda h: (0,) * len(shape))
    return pl.pallas_call(
        keyval_kernel,
        grid=(heads,),
        in_specs=[
            whole(rows, width),
            whole(1, width),
            whole(head, 1),
            pl.BlockSpec((1, head // 2, rows), lambda h: (0, 0, 0)),
            pl.BlockSpec((1, head // 2, rows), lambda h: (0, 0, 0)),
            pl.BlockSpec((width, head), lambda h: (0, h)),
            pl.BlockSpec((width, head), lambda h: (0, heads + h)),
        ],
        out_specs=pl.BlockSpec((1, rows, 2 * head), lambda h: (h, 0, 0)),
        out_shape=jax.ShapeDtypeStruct((heads, rows, 2 * head), jnp.bfloat16),
        scratch_shapes=[pltpu.VMEM((rows, width), jnp.bfloat16)],
        compiler_params=pltpu.CompilerParams(vmem_limit_bytes=60 * 2**20),
        cost_estimate=pl.CostEstimate(
            flops=2 * rows * width * w_keyval.shape[1], bytes_accessed=5 * 2**20, transcendentals=0
        ),
        name="keyval",
    )(tokens, attn_gain.reshape(1, width), key_norm_gain.reshape(head, 1), cosine, sine, w_keyval, w_keyval)


def grid_body(
    tokens,
    seg_ids,
    expert_ids,
    gates,
    page_table,
    attn_gain,
    q_gain,
    key_norm_gain,
    w_query,
    w_keyval,
    w_out,
    moe_gain,
    w_gate_up,
    w_down,
):
    rows, width = tokens.shape
    head = q_gain.shape[0]
    kv_heads = w_keyval.shape[1] // (2 * head)
    kv_width = kv_heads * head
    rep, tp = lax.axis_index("rep"), lax.axis_index("tp")
    y, core, z, x = rep // 2, rep % 2, tp // 2, tp % 2
    group_rows = 8 * rows
    group_start = rep * group_rows
    slots = range(4)

    slot_start = [group_start + ((z ^ k) * 2 + x) * rows for k in slots]
    slot_position = jnp.stack([at + jnp.arange(rows, dtype=jnp.int32) for at in slot_start])
    frequency = jnp.exp(
        jnp.arange(head // 2, dtype=jnp.float32) * (-2.0 * math.log(1000000.0) / head)
    )
    angles = frequency[None, :, None] * slot_position.astype(jnp.float32)[:, None, :]
    cosine, sine = jnp.cos(angles), jnp.sin(angles)

    by_head = keyval_by_head(tokens, attn_gain, key_norm_gain, cosine, sine, w_keyval)
    part = w_query.shape[1] // 4
    quarter = y * 2 + core
    query_x = other_x(lax.dynamic_slice_in_dim(w_query, quarter * part, part, 1))
    by_head, query_x = lax.optimization_barrier((by_head, query_x))
    query_y = other_y(query_x)

    top = expert_ids.shape[1]
    routes = jnp.concatenate([expert_ids.T.astype(jnp.bfloat16), gates.T], axis=0)
    routes = jnp.pad(routes, ((0, 0), (0, 2 * head - rows)))
    pick = lambda h: jnp.concatenate(
        [lax.dynamic_index_in_dim(by_head, h, 0, keepdims=False), routes], axis=0
    )
    kv_here = jnp.stack([pick(z)] + [other_z(pick(z ^ k), k) for k in (1, 2, 3)])
    far = other_z(tokens, 2)
    kv_here, query_y, far, w_query, w_out = lax.optimization_barrier(
        (kv_here, query_y, far, w_query, w_out)
    )
    kv_before, kv_side = passed_along(kv_here, "rep", 1), other_x(kv_here)
    farther = other_z(far, 1)
    query_two = jnp.concatenate([query_x, query_y], axis=1)
    query_far = other_core(query_two)
    out_x = other_x(lax.dynamic_slice_in_dim(w_out, quarter * part, part, 0))
    kv_side, query_far = lax.optimization_barrier((kv_side, query_far))
    kv_before_side = passed_along(kv_side, "rep", 1)
    w_query_wide = jnp.concatenate([w_query, query_two, query_far], axis=1)
    kv_before, kv_before_side, out_x, farther = lax.optimization_barrier(
        (kv_before, kv_before_side, out_x, farther)
    )
    near = other_z(after(tokens, farther), 1)
    out_two = jnp.concatenate([out_x, other_y(out_x)], axis=0)
    w_out_wide = jnp.concatenate([w_out, out_two, other_core(out_two)], axis=0)
    raw = [tokens, near, far, farther]

    pages = page_table.shape[0]
    stored = jnp.transpose(by_head.reshape(kv_heads, rows, 2, head), (1, 2, 0, 3))
    placing = (page_table[None, :] == jnp.arange(pages, dtype=jnp.int32)[:, None]).astype(jnp.bfloat16)
    cache = jnp.dot(placing, stored.reshape(pages, -1), preferred_element_type=jnp.float32)
    cache = cache.astype(jnp.bfloat16).reshape(pages, rows // pages, 2 * kv_width)

    slot_seg = jnp.concatenate(
        [lax.dynamic_slice_in_dim(seg_ids, at, rows, 0) for at in slot_start]
    )
    starts = jnp.sum((seg_ids[None, :] < slot_seg[:, None]).astype(jnp.int32), axis=1)
    starts = (starts - (group_start - group_rows)).reshape(4, 1, rows)
    low = starts[:, 0, 0] // KEY_BLOCK

    def projection(first):
        lines = jnp.concatenate(raw[first : first + 2], axis=0).astype(jnp.float32)
        lines = root_mean_norm(lines, attn_gain).astype(jnp.bfloat16)
        return jnp.dot(lines, w_query_wide, preferred_element_type=jnp.float32)

    def attended(first, projected):
        two = slice(first, first + 2)
        return attend_slots(
            jnp.stack([z, x, jnp.int32(first)]),
            low[two],
            projected,
            q_gain,
            cosine[two],
            sine[two],
            starts[two],
            (kv_here, kv_side, kv_before, kv_before_side),
        )

    def term_of(part):
        term = jnp.dot(part, w_out_wide, preferred_element_type=jnp.float32).astype(jnp.bfloat16)
        return term[:rows], term[rows:]

    term_2, term_3 = term_of(attended(2, projection(2)))
    far_3 = other_z(term_3, 1)
    far = other_z(sum_of(term_2, far_3), 2)
    term_0, term_1 = term_of(attended(0, after(projection(0), term_3)))
    near = other_z(term_1, 1)
    mixed_sum = term_0.astype(jnp.float32) + near.astype(jnp.float32) + far.astype(jnp.float32)
    residual = (tokens.astype(jnp.float32) + mixed_sum).astype(jnp.bfloat16)
    normed_moe = root_mean_norm(residual.astype(jnp.float32), moe_gain).astype(jnp.bfloat16)

    turned = (False, True, False, True)
    routes = kv_here[:, rows:, :rows]
    over_x, over_y = kv_side[:, rows:, :rows], other_y(routes)
    routes = jnp.stack(
        [jnp.stack([routes[k], (over_y if turned[k] else over_x)[k]]) for k in slots]
    ).reshape(4, 2, 2, top, rows)
    capacity = max(2, 3 * rows * top // (2 * 32))
    mine = [rep * 8 + tp, (rep ^ 1) * 8 + tp]
    experts = jnp.stack(
        [jnp.stack(mine + [e ^ 1 if turned[k] else e ^ 16 for e in mine]) for k in slots]
    ).astype(jnp.bfloat16)
    hits = routes[:, :, 0][:, :, None] == experts[:, None, :, None, None]
    weight = jnp.sum(jnp.where(hits, routes[:, :, 1][:, :, None].astype(jnp.float32), 0.0), axis=3)
    hit = jnp.any(hits, axis=3)
    earlier = jnp.arange(rows)[:, None] < jnp.arange(rows)[None, :]
    place = jnp.dot(
        hit.reshape(-1, rows).astype(jnp.bfloat16),
        earlier.astype(jnp.bfloat16),
        preferred_element_type=jnp.float32,
    ).reshape(4, 2, 4, rows)
    chosen = (
        place[..., None, :].astype(jnp.int32) == jnp.arange(capacity, dtype=jnp.int32)[:, None]
    ) & hit[..., None, :]
    weighted = jnp.where(chosen, weight[..., None, :], 0.0).astype(jnp.bfloat16)
    weighted = weighted.reshape(4, 2, 4 * capacity, rows)
    chosen = chosen.astype(jnp.bfloat16).reshape(4, 2, 4 * capacity, rows)

    def experts_of(slot_rows_in):
        gate_up = jnp.dot(slot_rows_in, w_gate_up[0], preferred_element_type=jnp.float32)
        hidden = w_down.shape[1]
        act = (jax.nn.silu(gate_up[:, :hidden]) * gate_up[:, hidden:]).astype(jnp.bfloat16)
        return jnp.dot(act, w_down[0], preferred_element_type=jnp.float32).astype(jnp.bfloat16)

    pair = 2 * capacity
    together = lambda *values: lax.optimization_barrier(values)

    def picks(k, block, side):
        picked = lax.dot_general(
            chosen[k], jnp.stack([block, side]), (((2,), (1,)), ((0,), (0,))), preferred_element_type=jnp.float32
        ).astype(jnp.bfloat16)
        return picked[:, :pair], picked[:, pair:]

    def routed(mine, theirs):
        picked = jnp.concatenate([mine, theirs], axis=0)
        kept = picked[:, :capacity].reshape(-1, width)
        return jnp.concatenate([kept, other_core(picked[:, capacity:].reshape(-1, width))], axis=0)

    near, far = other_z(normed_moe, 1), other_z(normed_moe, 2)
    mine_0, theirs_0 = picks(0, normed_moe, other_x(normed_moe))
    theirs_0 = other_y(theirs_0)
    near, far, mine_0 = together(near, far, mine_0)
    side_1, side_2, farther = other_y(near), other_x(far), other_z(far, 1)
    side_2, farther, theirs_0 = together(side_2, farther, theirs_0)
    mine_2, theirs_2 = picks(2, far, side_2)
    side_3 = other_y(farther)
    side_1, mine_2, theirs_2 = together(side_1, mine_2, theirs_2)
    mine_1, theirs_1 = picks(1, near, side_1)
    theirs_1 = other_x(theirs_1)
    result_0 = experts_of(routed(mine_0, theirs_0))
    side_3, theirs_2, result_0 = together(side_3, theirs_2, result_0)
    mine_3, theirs_3 = picks(3, farther, side_3)
    theirs_2, theirs_3 = other_y(theirs_2), other_x(theirs_3)
    result_1 = experts_of(routed(mine_1, after(theirs_1, side_3)))
    theirs_2, result_1 = together(theirs_2, result_1)
    result_2 = experts_of(routed(mine_2, theirs_2))
    result_3 = experts_of(after(routed(mine_3, theirs_3), result_2))

    def back(result):
        traded = other_core(result[4 * capacity :])
        both = jnp.stack([result[: 4 * capacity], traded]).reshape(2, 4, capacity, width)
        both = jnp.transpose(both, (1, 0, 2, 3)).reshape(4, pair, width)
        return both[:2], both[2:]

    def summed(k, here, there):
        total = lax.dot_general(
            weighted[k],
            jnp.concatenate([here, there], axis=1),
            (((1,), (1,)), ((0,), (0,))),
            preferred_element_type=jnp.float32,
        ).astype(jnp.bfloat16)
        return total[0], total[1]

    (here_0, there_0), (here_1, there_1) = back(result_0), back(result_1)
    (here_2, there_2), (here_3, there_3) = back(result_2), back(result_3)
    there_2, there_3 = together(other_y(there_2), other_x(there_3))
    (own_2, side_2), (own_3, side_3) = summed(2, here_2, there_2), summed(3, here_3, there_3)
    side_2, side_3, there_0, there_1 = together(other_x(side_2), other_y(side_3), there_0, there_1)
    far_3 = other_z(sum_of(own_3, side_3), 1)
    there_0, there_1 = together(other_y(there_0), other_x(there_1))
    (own_0, side_0), (own_1, side_1) = summed(0, here_0, there_0), summed(1, here_1, there_1)
    far = own_2.astype(jnp.float32) + side_2.astype(jnp.float32) + far_3.astype(jnp.float32)
    far = other_z(far.astype(jnp.bfloat16), 2)
    side_0, side_1 = together(other_x(side_0), other_y(side_1))
    near = other_z(sum_of(own_1, side_1), 1)
    combined = residual.astype(jnp.float32)
    for value in (far, near, own_0, side_0):
        combined = combined + value.astype(jnp.float32)
    return (combined.astype(jnp.bfloat16), cache)


def solution(mesh):
    in_specs = (
        P(("rep", "tp"), None),
        P(),
        P(("rep", "tp"), None),
        P(("rep", "tp"), None),
        P(("rep", "tp")),
        P(),
        P(),
        P(),
        P(None, "tp"),
        P(),
        P("tp", None),
        P(),
        P(("rep", "tp"), None, None),
        P(("rep", "tp"), None, None),
    )
    out_specs = (P(("rep", "tp"), None), P(("rep", "tp"), None, None))
    body = grid_body if (mesh.shape["rep"], mesh.shape["tp"]) == (4, 8) else general_body
    return jax.shard_map(body, mesh=mesh, in_specs=in_specs, out_specs=out_specs, check_vma=False)
```

```python
import functools
import math

import jax
import jax.numpy as jnp
from jax import lax
from jax.experimental import pallas as pl
from jax.experimental.pallas import tpu as pltpu
from jax.sharding import PartitionSpec as P


def passed_along(block, axis, distance):
    devices = range(lax.axis_size(axis))
    route = [(i - distance, i) for i in devices if i - distance in devices]
    return lax.ppermute(block, axis, route)


def root_mean_norm(value_rows, gain):
    return (
        value_rows
        * lax.rsqrt(jnp.mean(value_rows * value_rows, axis=-1, keepdims=True) + 1e-06)
        * gain
    )


def apply_rotary(value_rows, token_positions):
    half_dim = value_rows.shape[-1] // 2
    frequency = jnp.exp(
        jnp.arange(half_dim, dtype=jnp.float32)
        * (-2.0 * math.log(1000000.0) / value_rows.shape[-1])
    )
    angles = token_positions[:, None] * frequency[None, :]
    cosine = jnp.cos(angles)[:, None, :]
    sine_part = jnp.sin(angles)[:, None, :]
    first = value_rows[..., :half_dim]
    second = value_rows[..., half_dim:]
    return jnp.concatenate(
        [first * cosine - second * sine_part, second * cosine + first * sine_part], axis=-1
    )


def general_body(
    tokens,
    seg_ids,
    expert_ids,
    gates,
    page_table,
    attn_gain,
    q_gain,
    key_norm_gain,
    w_query,
    w_keyval,
    w_out,
    moe_gain,
    w_gate_up,
    w_down,
):
    tok_rows, width = tokens.shape
    tp_count = lax.axis_size("tp")
    rep_count = lax.axis_size("rep")
    rep_index = lax.axis_index("rep")
    tp_index = lax.axis_index("tp")
    group_rows = tok_rows * tp_count
    head_dim = q_gain.shape[0]
    q_width = w_query.shape[1]
    heads_here = q_width // head_dim
    kv_heads = w_keyval.shape[1] // (2 * head_dim)
    kv_width = kv_heads * head_dim
    per_key_value = heads_here * tp_count // kv_heads
    own_head = tp_index * heads_here // per_key_value
    first_row = (rep_index * tp_count + tp_index) * tok_rows
    local_pos = (first_row + jnp.arange(tok_rows, dtype=jnp.int32)).astype(jnp.float32)
    normed = root_mean_norm(tokens.astype(jnp.float32), attn_gain).astype(jnp.bfloat16)
    key_value_rows = jnp.dot(normed, w_keyval, preferred_element_type=jnp.float32)
    rotary_output = apply_rotary(
        root_mean_norm(
            key_value_rows[:, :kv_width].reshape(tok_rows, kv_heads, head_dim), key_norm_gain
        ),
        local_pos,
    )
    stored_cache = jnp.concatenate(
        [rotary_output.reshape(tok_rows, kv_width), key_value_rows[:, kv_width:]], axis=1
    ).astype(jnp.bfloat16)
    page_count = page_table.shape[0]
    placement_matrix = (
        page_table[None, :] == jnp.arange(page_count, dtype=jnp.int32)[:, None]
    ).astype(jnp.bfloat16)
    cache = jnp.dot(
        placement_matrix, stored_cache.reshape(page_count, -1), preferred_element_type=jnp.float32
    )
    cache = cache.astype(jnp.bfloat16).reshape(page_count, tok_rows // page_count, 2 * kv_width)
    projected = jnp.dot(
        lax.all_gather(normed, "tp", axis=0, tiled=True),
        w_query,
        preferred_element_type=jnp.float32,
    )
    group_start = rep_index * group_rows
    group_pos = group_start + jnp.arange(group_rows, dtype=jnp.int32)
    group_posf = group_pos.astype(jnp.float32)
    query = root_mean_norm(projected.reshape(group_rows, heads_here, head_dim), q_gain)
    query = apply_rotary(query, group_posf).astype(jnp.bfloat16)
    gathered = lax.all_gather(stored_cache, "tp", axis=0, tiled=True)
    own_keys = lax.dynamic_slice_in_dim(gathered, own_head * head_dim, head_dim, 1)
    own_values = lax.dynamic_slice_in_dim(gathered, kv_width + own_head * head_dim, head_dim, 1)
    earlier_keys, earlier_values = passed_along((own_keys, own_values), "rep", 1)
    own_seg = lax.dynamic_slice_in_dim(seg_ids, group_start, group_rows, 0)
    earlier_seg = lax.dynamic_slice_in_dim(
        seg_ids, jnp.maximum(group_start - group_rows, 0), group_rows, 0
    )
    earlier_seg = jnp.where(rep_index > 0, earlier_seg, -1)
    keys_all = jnp.concatenate([earlier_keys, own_keys], axis=0)
    values_all = jnp.concatenate([earlier_values, own_values], axis=0)
    key_seg = jnp.concatenate([earlier_seg, own_seg], axis=0)
    key_pos = group_start - group_rows + jnp.arange(2 * group_rows, dtype=jnp.int32)
    block_rows = min(512, group_rows)
    block_count = group_rows // block_rows
    scale = head_dim ** (-0.5)

    def attend(inputs):
        block_query, block_pos, block_seg = inputs
        scores = (
            jnp.einsum("bhd,kd->hbk", block_query, keys_all, preferred_element_type=jnp.float32)
            * scale
        )
        allowed = (key_seg[None, :] == block_seg[:, None]) & (
            key_pos[None, :] <= block_pos[:, None]
        )
        scores = jnp.where(allowed[None], scores, -jnp.inf)
        largest = jnp.max(scores, axis=-1, keepdims=True)
        weights = jnp.exp(scores - largest)
        totals = jnp.sum(weights, axis=-1, keepdims=True)
        mixed = (
            jnp.einsum(
                "hbk,kd->hbd",
                weights.astype(jnp.bfloat16),
                values_all,
                preferred_element_type=jnp.float32,
            )
            / totals
        )
        return jnp.transpose(mixed.astype(jnp.bfloat16), (1, 0, 2)).reshape(
            block_rows, heads_here * head_dim
        )

    attended = lax.map(
        attend,
        (
            query.reshape(block_count, block_rows, heads_here, head_dim),
            group_pos.reshape(block_count, block_rows),
            own_seg.reshape(block_count, block_rows),
        ),
    )
    attended = attended.reshape(group_rows, heads_here * head_dim)
    rows = attended
    term = jnp.dot(rows, w_out, preferred_element_type=jnp.float32).astype(jnp.bfloat16)
    mixed_sum = lax.psum_scatter(
        lax.optimization_barrier(term).astype(jnp.float32).astype(jnp.bfloat16),
        "tp",
        scatter_dimension=0,
        tiled=True,
    ).astype(jnp.float32)
    residual = (tokens.astype(jnp.float32) + mixed_sum).astype(jnp.bfloat16)
    normed_moe = root_mean_norm(residual.astype(jnp.float32), moe_gain).astype(jnp.bfloat16)
    expert_count = rep_count * tp_count * w_gate_up.shape[0]
    top_count = expert_ids.shape[1]
    capacity = max(2, 3 * tok_rows * top_count // (2 * expert_count))
    hidden_units = w_down.shape[1]
    flat = expert_ids.reshape(-1)
    onehot = (flat[:, None] == jnp.arange(expert_count, dtype=jnp.int32)[None, :]).astype(jnp.int32)
    rank = jnp.sum((jnp.cumsum(onehot, axis=0) - 1) * onehot, axis=1)
    target = (flat * capacity + rank).reshape(tok_rows, top_count)
    match = (
        target[:, :, None] == jnp.arange(expert_count * capacity, dtype=jnp.int32)[None, None, :]
    )
    dispatch = jnp.any(match, axis=1).astype(jnp.bfloat16)
    combine = jnp.sum(jnp.where(match, gates[:, :, None].astype(jnp.float32), 0.0), axis=1).astype(
        jnp.bfloat16
    )
    outgoing = lax.dot_general(
        dispatch, normed_moe, (((0,), (0,)), ((), ())), preferred_element_type=jnp.float32
    )
    outgoing = outgoing.astype(jnp.bfloat16).reshape(expert_count, capacity, width)
    received = lax.all_to_all(outgoing, ("rep", "tp"), split_axis=0, concat_axis=0, tiled=True)
    rows = received.reshape(-1, width)
    gate_up = jnp.dot(rows, w_gate_up[0], preferred_element_type=jnp.float32)
    act = (jax.nn.silu(gate_up[:, :hidden_units]) * gate_up[:, hidden_units:]).astype(jnp.bfloat16)
    result = jnp.dot(act, w_down[0], preferred_element_type=jnp.float32).astype(jnp.bfloat16)
    returned = lax.all_to_all(
        result.reshape(received.shape), ("rep", "tp"), split_axis=0, concat_axis=0, tiled=True
    )
    combined = jnp.dot(
        combine,
        returned.reshape(expert_count * capacity, width),
        preferred_element_type=jnp.float32,
    )
    hidden_out = (residual.astype(jnp.float32) + combined).astype(jnp.bfloat16)
    return (hidden_out, cache)


KEY_BLOCK = 256
MASKED = -1e30


def moved(block, change):
    route = []
    for y in range(2):
        for core in range(2):
            for z in range(4):
                for x in range(2):
                    to_y, to_core, to_z, to_x = change(y, core, z, x)
                    route.append(
                        ((y * 2 + core) * 8 + z * 2 + x, (to_y * 2 + to_core) * 8 + to_z * 2 + to_x)
                    )
    return lax.ppermute(block, ("rep", "tp"), route)


def other_x(block):
    return moved(block, lambda y, core, z, x: (y, core, z, 1 - x))


def other_y(block):
    return moved(block, lambda y, core, z, x: (1 - y, core, z, x))


def other_core(block):
    return moved(block, lambda y, core, z, x: (y, 1 - core, z, x))


def across(block, over_y):
    if over_y:
        return moved(block, lambda y, core, z, x: (1 - y, 1 - core, z, x))
    return moved(block, lambda y, core, z, x: (y, 1 - core, z, 1 - x))


def other_z(block, k):
    return moved(block, lambda y, core, z, x: (y, core, z ^ k, x))


def sum_of(a, b):
    return (a.astype(jnp.float32) + b.astype(jnp.float32)).astype(jnp.bfloat16)


def after(value, earlier):
    return lax.optimization_barrier((value, earlier))[0]


def attention_kernel(
    place, low, projected, gain, cosine, sine, start, kv_here, kv_side, kv_before, kv_before_side, out,
    keys, values, acc, peak, total,
):
    z, x, slot = place[0], place[1], place[2] + pl.program_id(0)
    rows = projected.shape[0]
    head = gain.shape[1]
    heads = projected.shape[1] // head
    half = head // 2

    @pl.when(pl.program_id(0) == 0)
    def _():
        for first, near, far in ((0, kv_before, kv_before_side), (8, kv_here, kv_side)):
            for k in range(4):
                at = jnp.bitwise_xor(z, k) * 2
                for source, shift in ((near, x), (far, 1 - x)):
                    row = pl.multiple_of((first + at + shift) * rows, rows)
                    keys[pl.ds(row, rows), :] = source[k, :rows, :head]
                    values[:, pl.ds(row, rows)] = source[k, :rows, head:].astype(jnp.float32).T.astype(jnp.bfloat16)

    gain_column = jnp.broadcast_to(gain[...], (rows, head)).T
    turned = []
    for h in range(heads):
        q = projected[:, h * head : (h + 1) * head].T
        q = q * lax.rsqrt(jnp.mean(q * q, axis=0, keepdims=True) + 1e-06) * gain_column
        first, second = q[:half], q[half:]
        turned.append(
            jnp.concatenate(
                [first * cosine[0] - second * sine[0], second * cosine[0] + first * sine[0]], axis=0
            )
        )
    query = (jnp.concatenate(turned, axis=1) * (head**-0.5 * math.log2(math.e))).astype(jnp.bfloat16)
    acc[...] = jnp.zeros_like(acc)
    total[...] = jnp.zeros_like(total)
    peak[...] = jnp.full_like(peak, MASKED)
    position = (8 + jnp.bitwise_xor(z, slot) * 2 + x) * rows
    own_position = position + lax.broadcasted_iota(jnp.int32, (KEY_BLOCK, rows), 1)
    own_start = start[0]

    def step(j, _):
        row = pl.multiple_of(j * KEY_BLOCK, KEY_BLOCK)
        scores = jnp.dot(keys[pl.ds(row, KEY_BLOCK), :], query, preferred_element_type=jnp.float32)
        key_position = row + lax.broadcasted_iota(jnp.int32, (KEY_BLOCK, rows), 0)
        allowed = (key_position >= own_start) & (key_position <= own_position)
        scores = jnp.concatenate(
            [jnp.where(allowed, scores[:, h * rows : (h + 1) * rows], MASKED) for h in range(heads)], axis=1
        )
        largest = jnp.maximum(peak[...], jnp.max(scores, axis=0, keepdims=True))
        fade = jnp.exp2(peak[...] - largest)
        weights = jnp.exp2(scores - largest)
        total[...] = total[...] * fade + jnp.sum(weights, axis=0, keepdims=True)
        acc[...] = acc[...] * fade + jnp.dot(
            values[:, pl.ds(row, KEY_BLOCK)], weights.astype(jnp.bfloat16), preferred_element_type=jnp.float32
        )
        peak[...] = largest
        return 0

    lax.fori_loop(low[pl.program_id(0)], (position + rows - 1) // KEY_BLOCK + 1, step, 0)
    mixed = acc[...] / total[...]
    for h in range(heads):
        out[:, h * head : (h + 1) * head] = mixed[:, h * rows : (h + 1) * rows].T.astype(out.dtype)


def attend_slots(place, low, projected, q_gain, cosine, sine, start, kv):
    slots, rows = start.shape[0], start.shape[2]
    head = q_gain.shape[0]
    width = projected.shape[1]
    whole = lambda *shape: pl.BlockSpec(shape, lambda s, *_: (0,) * len(shape))
    return pl.pallas_call(
        attention_kernel,
        grid_spec=pltpu.PrefetchScalarGridSpec(
            num_scalar_prefetch=2,
            grid=(slots,),
            in_specs=[
                pl.BlockSpec((rows, width), lambda s, *_: (s, 0)),
                whole(1, head),
                pl.BlockSpec((1, head // 2, rows), lambda s, *_: (s, 0, 0)),
                pl.BlockSpec((1, head // 2, rows), lambda s, *_: (s, 0, 0)),
                pl.BlockSpec((1, 1, rows), lambda s, *_: (s, 0, 0)),
            ]
            + [whole(*part.shape) for part in kv],
            out_specs=pl.BlockSpec((rows, width), lambda s, *_: (s, 0)),
            scratch_shapes=[
                pltpu.VMEM((16 * rows, head), jnp.bfloat16),
                pltpu.VMEM((head, 16 * rows), jnp.bfloat16),
                pltpu.VMEM((head, width // head * rows), jnp.float32),
                pltpu.VMEM((1, width // head * rows), jnp.float32),
                pltpu.VMEM((1, width // head * rows), jnp.float32),
            ],
        ),
        out_shape=jax.ShapeDtypeStruct((slots * rows, width), jnp.bfloat16),
        compiler_params=pltpu.CompilerParams(vmem_limit_bytes=40 * 2**20),
        cost_estimate=pl.CostEstimate(
            flops=4 * slots * rows * width * 4 * rows,
            bytes_accessed=8 * 2**20,
            transcendentals=slots * width * rows,
        ),
        name="attention",
    )(place, low, projected, q_gain.reshape(1, head), cosine, sine, start, *kv)


def keyval_kernel(tokens, gain, key_gain, cosine, sine, w_key, w_value, out, normed):
    @pl.when(pl.program_id(0) == 0)
    def _():
        normed[...] = root_mean_norm(tokens[...].astype(jnp.float32), gain[...]).astype(jnp.bfloat16)

    head = key_gain.shape[1]
    half = head // 2
    k = jnp.dot(normed[...], w_key[...], preferred_element_type=jnp.float32).T
    k = k * lax.rsqrt(jnp.mean(k * k, axis=0, keepdims=True) + 1e-06)
    k = k * jnp.broadcast_to(key_gain[...], (normed.shape[0], head)).T
    first, second = k[:half], k[half:]
    k = jnp.concatenate(
        [first * cosine[0] - second * sine[0], second * cosine[0] + first * sine[0]], axis=0
    )
    out[0, :, :head] = k.T.astype(out.dtype)
    v = jnp.dot(normed[...], w_value[...], preferred_element_type=jnp.float32)
    out[0, :, head:] = v.astype(out.dtype)


def keyval_by_head(tokens, attn_gain, key_norm_gain, cosine, sine, w_keyval):
    rows, width = tokens.shape
    head = key_norm_gain.shape[0]
    heads = w_keyval.shape[1] // (2 * head)
    whole = lambda *shape: pl.BlockSpec(shape, lambda h: (0,) * len(shape))
    return pl.pallas_call(
        keyval_kernel,
        grid=(heads,),
        in_specs=[
            whole(rows, width),
            whole(1, width),
            whole(1, head),
            pl.BlockSpec((1, head // 2, rows), lambda h: (0, 0, 0)),
            pl.BlockSpec((1, head // 2, rows), lambda h: (0, 0, 0)),
            pl.BlockSpec((width, head), lambda h: (0, h)),
            pl.BlockSpec((width, head), lambda h: (0, heads + h)),
        ],
        out_specs=pl.BlockSpec((1, rows, 2 * head), lambda h: (h, 0, 0)),
        out_shape=jax.ShapeDtypeStruct((heads, rows, 2 * head), jnp.bfloat16),
        scratch_shapes=[pltpu.VMEM((rows, width), jnp.bfloat16)],
        compiler_params=pltpu.CompilerParams(vmem_limit_bytes=60 * 2**20),
        cost_estimate=pl.CostEstimate(
            flops=2 * rows * width * w_keyval.shape[1], bytes_accessed=5 * 2**20, transcendentals=0
        ),
        name="keyval",
    )(tokens, attn_gain.reshape(1, width), key_norm_gain.reshape(1, head), cosine, sine, w_keyval, w_keyval)


def grid_body(
    tokens,
    seg_ids,
    expert_ids,
    gates,
    page_table,
    attn_gain,
    q_gain,
    key_norm_gain,
    w_query,
    w_keyval,
    w_out,
    moe_gain,
    w_gate_up,
    w_down,
):
    rows, width = tokens.shape
    head = q_gain.shape[0]
    kv_heads = w_keyval.shape[1] // (2 * head)
    kv_width = kv_heads * head
    rep, tp = lax.axis_index("rep"), lax.axis_index("tp")
    y, core, z, x = rep // 2, rep % 2, tp // 2, tp % 2
    group_rows = 8 * rows
    group_start = rep * group_rows
    slots = range(4)

    slot_start = [group_start + ((z ^ k) * 2 + x) * rows for k in slots]
    slot_position = jnp.stack([at + jnp.arange(rows, dtype=jnp.int32) for at in slot_start])
    frequency = jnp.exp(
        jnp.arange(head // 2, dtype=jnp.float32) * (-2.0 * math.log(1000000.0) / head)
    )
    angles = frequency[None, :, None] * slot_position.astype(jnp.float32)[:, None, :]
    cosine, sine = jnp.cos(angles), jnp.sin(angles)

    by_head = keyval_by_head(tokens, attn_gain, key_norm_gain, cosine, sine, w_keyval)
    part = w_query.shape[1] // 4
    quarter = y * 2 + core
    far = other_z(tokens, 2)
    query_x = other_x(lax.dynamic_slice_in_dim(w_query, quarter * part, part, 1))
    by_head, late_segs, query_x, w_out = lax.optimization_barrier((by_head, seg_ids, query_x, w_out))
    out_x = other_x(lax.dynamic_slice_in_dim(w_out, quarter * part, part, 0))

    top = expert_ids.shape[1]
    routes = jnp.concatenate([expert_ids.T.astype(jnp.bfloat16), gates.T], axis=0)
    routes = jnp.pad(routes, ((0, 0), (0, 2 * head - rows)))
    pick = lambda h: jnp.concatenate(
        [lax.dynamic_index_in_dim(by_head, h, 0, keepdims=False), routes], axis=0
    )
    kv_parts = [other_z(pick(z ^ k), k) for k in (1, 2, 3)]
    query_y = other_y(after(query_x, kv_parts[0]))
    kv_here = jnp.stack([pick(z)] + kv_parts)
    kv_here, out_x, far, w_query, w_out = lax.optimization_barrier((kv_here, out_x, far, w_query, w_out))
    kv_before, kv_side = passed_along(kv_here, "rep", 1), other_x(kv_here)
    farther, out_y = other_z(far, 1), other_y(out_x)
    kv_side, query_y = lax.optimization_barrier((kv_side, query_y))
    kv_before_side = passed_along(kv_side, "rep", 1)
    query_two = jnp.concatenate([query_x, query_y], axis=1)
    query_far = other_core(query_two)
    kv_before, kv_before_side, query_far, farther, out_y = lax.optimization_barrier(
        (kv_before, kv_before_side, query_far, farther, out_y)
    )
    w_query_wide = jnp.concatenate([w_query, query_two, query_far], axis=1)
    out_two = jnp.concatenate([out_x, out_y], axis=0)
    near = other_z(after(tokens, farther), 1)
    w_out_wide = jnp.concatenate([w_out, out_two, other_core(out_two)], axis=0)
    raw = [tokens, near, far, farther]

    pages = page_table.shape[0]
    stored = jnp.transpose(by_head.reshape(kv_heads, rows, 2, head), (1, 2, 0, 3))
    placing = (page_table[None, :] == jnp.arange(pages, dtype=jnp.int32)[:, None]).astype(jnp.bfloat16)
    cache = jnp.dot(placing, stored.reshape(pages, -1), preferred_element_type=jnp.float32)
    cache = cache.astype(jnp.bfloat16).reshape(pages, rows // pages, 2 * kv_width)

    slot_seg = jnp.concatenate(
        [lax.dynamic_slice_in_dim(late_segs, at, rows, 0) for at in slot_start]
    )
    starts = jnp.sum((late_segs[None, :] < slot_seg[:, None]).astype(jnp.int32), axis=1)
    starts = (starts - (group_start - group_rows)).reshape(4, 1, rows)
    low = starts[:, 0, 0] // KEY_BLOCK

    def projection(first):
        lines = jnp.concatenate(raw[first : first + 2], axis=0).astype(jnp.float32)
        lines = root_mean_norm(lines, attn_gain).astype(jnp.bfloat16)
        return jnp.dot(lines, w_query_wide, preferred_element_type=jnp.float32)

    def attended(first, projected):
        two = slice(first, first + 2)
        return attend_slots(
            jnp.stack([z, x, jnp.int32(first)]),
            low[two],
            projected,
            q_gain,
            cosine[two],
            sine[two],
            starts[two],
            (kv_here, kv_side, kv_before, kv_before_side),
        )

    def term_of(part):
        term = jnp.dot(part, w_out_wide, preferred_element_type=jnp.float32).astype(jnp.bfloat16)
        return term[:rows], term[rows:]

    attended_far = attended(2, projection(2))
    raw[1] = after(near, attended_far)
    term_2, term_3 = term_of(attended_far)
    far_3 = other_z(term_3, 1)
    far = other_z(sum_of(term_2, far_3), 2)
    term_0, term_1 = term_of(attended(0, after(projection(0), term_3)))
    near = other_z(term_1, 1)
    mixed_sum = term_0.astype(jnp.float32) + near.astype(jnp.float32) + far.astype(jnp.float32)
    residual = (tokens.astype(jnp.float32) + mixed_sum).astype(jnp.bfloat16)
    normed_moe = root_mean_norm(residual.astype(jnp.float32), moe_gain).astype(jnp.bfloat16)

    turned = (False, True, False, True)
    routes = after(kv_here[:, rows:, :rows], term_3)
    over_x, over_y = kv_side[:, rows:, :rows], other_y(routes)
    routes = jnp.stack(
        [jnp.stack([routes[k], (over_y if turned[k] else over_x)[k]]) for k in slots]
    ).reshape(4, 2, 2, top, rows)
    capacity = max(2, 3 * rows * top // (2 * 32))
    mine = [rep * 8 + tp, (rep ^ 1) * 8 + tp]
    experts = jnp.stack(
        [jnp.stack(mine + [e ^ 1 if turned[k] else e ^ 16 for e in mine]) for k in slots]
    ).astype(jnp.bfloat16)
    hits = routes[:, :, 0][:, :, None] == experts[:, None, :, None, None]
    weight = jnp.sum(jnp.where(hits, routes[:, :, 1][:, :, None].astype(jnp.float32), 0.0), axis=3)
    hit = jnp.any(hits, axis=3)
    earlier = jnp.arange(rows)[:, None] < jnp.arange(rows)[None, :]
    place = jnp.dot(
        hit.reshape(-1, rows).astype(jnp.bfloat16),
        earlier.astype(jnp.bfloat16),
        preferred_element_type=jnp.float32,
    ).reshape(4, 2, 4, rows)
    chosen = (
        place[..., None, :].astype(jnp.int32) == jnp.arange(capacity, dtype=jnp.int32)[:, None]
    ) & hit[..., None, :]
    weighted = jnp.where(chosen, weight[..., None, :], 0.0).astype(jnp.bfloat16)
    weighted = weighted.reshape(4, 2, 4 * capacity, rows)
    chosen = chosen.astype(jnp.bfloat16).reshape(4, 2, 4 * capacity, rows)

    def experts_of(slot_rows_in):
        gate_up = jnp.dot(slot_rows_in, w_gate_up[0], preferred_element_type=jnp.float32)
        hidden = w_down.shape[1]
        act = (jax.nn.silu(gate_up[:, :hidden]) * gate_up[:, hidden:]).astype(jnp.bfloat16)
        return jnp.dot(act, w_down[0], preferred_element_type=jnp.float32).astype(jnp.bfloat16)

    pair = 2 * capacity
    together = lambda *values: lax.optimization_barrier(values)

    def picks(k, block, side):
        picked = lax.dot_general(
            chosen[k], jnp.stack([block, side]), (((2,), (1,)), ((0,), (0,))), preferred_element_type=jnp.float32
        ).astype(jnp.bfloat16)
        return picked[:, :pair], picked[:, pair:]

    def routed(mine, theirs):
        picked = jnp.concatenate([mine, theirs], axis=0)
        kept = picked[:, :capacity].reshape(-1, width)
        return jnp.concatenate([kept, other_core(picked[:, capacity:].reshape(-1, width))], axis=0)

    half = rows // 2
    near, far = other_z(normed_moe, 1), other_z(normed_moe, 2)
    mine_0, theirs_0 = picks(0, normed_moe, other_x(normed_moe))
    theirs_0 = other_y(theirs_0)
    near, far, mine_0 = together(near, far, mine_0)
    side_1, side_2, farther = other_y(near), other_x(far), other_z(far, 1)
    side_2, farther, theirs_0 = together(side_2, farther, theirs_0)
    mine_2, theirs_2 = picks(2, far, side_2)
    side_3 = other_y(farther)
    side_1, mine_2, theirs_2 = together(side_1, mine_2, theirs_2)
    mine_1, theirs_1 = picks(1, near, side_1)
    theirs_1 = other_x(theirs_1)

    def over_second(to_y, to_y_across, to_x, to_x_across):
        return together(
            other_y(to_y), across(to_y_across, True), other_x(to_x), across(to_x_across, False)
        )

    def experts_on(*parts):
        return experts_of(jnp.concatenate(parts, axis=0).reshape(-1, width)).reshape(-1, capacity, width)

    kept = lambda *parts: jnp.concatenate([part[:, :capacity] for part in parts], axis=0)
    traded = lambda *parts: other_core(jnp.concatenate([part[:, capacity:] for part in parts], axis=0))
    result_0 = experts_of(routed(mine_0, theirs_0))
    result_12 = experts_on(kept(mine_1, mine_2), traded(mine_1, mine_2))
    side_3, theirs_2, result_0, result_12, theirs_1 = together(side_3, theirs_2, result_0, result_12, theirs_1)
    mine_3, theirs_3 = picks(3, farther, side_3)
    late = traded(mine_3, theirs_1)
    got = over_second(
        theirs_2[:, :capacity], theirs_2[:, capacity:], theirs_3[:, :capacity], theirs_3[:, capacity:]
    )
    *got, late = together(*got, late)
    got, late = together(experts_on(*got), late)
    result_31 = experts_on(kept(mine_3, theirs_1), late)
    both = lambda result: jnp.concatenate([result[:4], other_core(result[4:])], axis=1)
    here_1, here_2 = jnp.split(both(result_12), 2)
    here_3, there_1 = jnp.split(both(result_31), 2)

    def back(result):
        traded = other_core(result[4 * capacity :])
        both = jnp.stack([result[: 4 * capacity], traded]).reshape(2, 4, capacity, width)
        both = jnp.transpose(both, (1, 0, 2, 3)).reshape(4, pair, width)
        return both[:2], both[2:]

    def summed(k, here, there):
        total = lax.dot_general(
            weighted[k],
            jnp.concatenate([here, there], axis=1),
            (((1,), (1,)), ((0,), (0,))),
            preferred_element_type=jnp.float32,
        ).astype(jnp.bfloat16)
        return total[0], total[1]

    here_0, there_0 = back(result_0)
    there = over_second(got[:2], got[2:4], got[4:6], got[6:])
    there_2, there_3 = jnp.concatenate(there[:2], axis=1), jnp.concatenate(there[2:], axis=1)
    (own_2, side_2), (own_3, side_3) = summed(2, here_2, there_2), summed(3, here_3, there_3)
    side_2, side_3, there_0, there_1 = together(other_x(side_2), other_y(side_3), there_0, there_1)
    far_3 = other_z(sum_of(own_3, side_3), 1)
    there_0, there_1 = together(other_y(there_0), other_x(there_1))
    (own_0, side_0), (own_1, side_1) = summed(0, here_0, there_0), summed(1, here_1, there_1)
    far = own_2.astype(jnp.float32) + side_2.astype(jnp.float32) + far_3.astype(jnp.float32)
    far = other_z(far.astype(jnp.bfloat16), 2)
    side_0 = other_x(side_0)
    near = [
        other_z(sum_of(own_1[part], other_y(side_1[part])), 1) for part in (slice(0, half), slice(half, rows))
    ]
    near = jnp.concatenate(near, axis=0)
    combined = residual.astype(jnp.float32)
    for value in (far, near, own_0, side_0):
        combined = combined + value.astype(jnp.float32)
    return (combined.astype(jnp.bfloat16), cache)


def solution(mesh):
    in_specs = (
        P(("rep", "tp"), None),
        P(),
        P(("rep", "tp"), None),
        P(("rep", "tp"), None),
        P(("rep", "tp")),
        P(),
        P(),
        P(),
        P(None, "tp"),
        P(),
        P("tp", None),
        P(),
        P(("rep", "tp"), None, None),
        P(("rep", "tp"), None, None),
    )
    out_specs = (P(("rep", "tp"), None), P(("rep", "tp"), None, None))
    body = grid_body if (mesh.shape["rep"], mesh.shape["tp"]) == (4, 8) else general_body
    return jax.shard_map(body, mesh=mesh, in_specs=in_specs, out_specs=out_specs, check_vma=False)
```

```python
import functools
import math

import jax
import jax.numpy as jnp
from jax import lax
from jax.experimental import pallas as pl
from jax.experimental.pallas import tpu as pltpu
from jax.sharding import PartitionSpec as P


def passed_along(block, axis, distance):
    devices = range(lax.axis_size(axis))
    route = [(i - distance, i) for i in devices if i - distance in devices]
    return lax.ppermute(block, axis, route)


def root_mean_norm(value_rows, gain):
    return (
        value_rows
        * lax.rsqrt(jnp.mean(value_rows * value_rows, axis=-1, keepdims=True) + 1e-06)
        * gain
    )


def apply_rotary(value_rows, token_positions):
    half_dim = value_rows.shape[-1] // 2
    frequency = jnp.exp(
        jnp.arange(half_dim, dtype=jnp.float32)
        * (-2.0 * math.log(1000000.0) / value_rows.shape[-1])
    )
    angles = token_positions[:, None] * frequency[None, :]
    cosine = jnp.cos(angles)[:, None, :]
    sine_part = jnp.sin(angles)[:, None, :]
    first = value_rows[..., :half_dim]
    second = value_rows[..., half_dim:]
    return jnp.concatenate(
        [first * cosine - second * sine_part, second * cosine + first * sine_part], axis=-1
    )


def general_body(
    tokens,
    seg_ids,
    expert_ids,
    gates,
    page_table,
    attn_gain,
    q_gain,
    key_norm_gain,
    w_query,
    w_keyval,
    w_out,
    moe_gain,
    w_gate_up,
    w_down,
):
    tok_rows, width = tokens.shape
    tp_count = lax.axis_size("tp")
    rep_count = lax.axis_size("rep")
    rep_index = lax.axis_index("rep")
    tp_index = lax.axis_index("tp")
    group_rows = tok_rows * tp_count
    head_dim = q_gain.shape[0]
    q_width = w_query.shape[1]
    heads_here = q_width // head_dim
    kv_heads = w_keyval.shape[1] // (2 * head_dim)
    kv_width = kv_heads * head_dim
    per_key_value = heads_here * tp_count // kv_heads
    own_head = tp_index * heads_here // per_key_value
    first_row = (rep_index * tp_count + tp_index) * tok_rows
    local_pos = (first_row + jnp.arange(tok_rows, dtype=jnp.int32)).astype(jnp.float32)
    normed = root_mean_norm(tokens.astype(jnp.float32), attn_gain).astype(jnp.bfloat16)
    key_value_rows = jnp.dot(normed, w_keyval, preferred_element_type=jnp.float32)
    rotary_output = apply_rotary(
        root_mean_norm(
            key_value_rows[:, :kv_width].reshape(tok_rows, kv_heads, head_dim), key_norm_gain
        ),
        local_pos,
    )
    stored_cache = jnp.concatenate(
        [rotary_output.reshape(tok_rows, kv_width), key_value_rows[:, kv_width:]], axis=1
    ).astype(jnp.bfloat16)
    page_count = page_table.shape[0]
    placement_matrix = (
        page_table[None, :] == jnp.arange(page_count, dtype=jnp.int32)[:, None]
    ).astype(jnp.bfloat16)
    cache = jnp.dot(
        placement_matrix, stored_cache.reshape(page_count, -1), preferred_element_type=jnp.float32
    )
    cache = cache.astype(jnp.bfloat16).reshape(page_count, tok_rows // page_count, 2 * kv_width)
    projected = jnp.dot(
        lax.all_gather(normed, "tp", axis=0, tiled=True),
        w_query,
        preferred_element_type=jnp.float32,
    )
    group_start = rep_index * group_rows
    group_pos = group_start + jnp.arange(group_rows, dtype=jnp.int32)
    group_posf = group_pos.astype(jnp.float32)
    query = root_mean_norm(projected.reshape(group_rows, heads_here, head_dim), q_gain)
    query = apply_rotary(query, group_posf).astype(jnp.bfloat16)
    gathered = lax.all_gather(stored_cache, "tp", axis=0, tiled=True)
    own_keys = lax.dynamic_slice_in_dim(gathered, own_head * head_dim, head_dim, 1)
    own_values = lax.dynamic_slice_in_dim(gathered, kv_width + own_head * head_dim, head_dim, 1)
    earlier_keys, earlier_values = passed_along((own_keys, own_values), "rep", 1)
    own_seg = lax.dynamic_slice_in_dim(seg_ids, group_start, group_rows, 0)
    earlier_seg = lax.dynamic_slice_in_dim(
        seg_ids, jnp.maximum(group_start - group_rows, 0), group_rows, 0
    )
    earlier_seg = jnp.where(rep_index > 0, earlier_seg, -1)
    keys_all = jnp.concatenate([earlier_keys, own_keys], axis=0)
    values_all = jnp.concatenate([earlier_values, own_values], axis=0)
    key_seg = jnp.concatenate([earlier_seg, own_seg], axis=0)
    key_pos = group_start - group_rows + jnp.arange(2 * group_rows, dtype=jnp.int32)
    block_rows = min(512, group_rows)
    block_count = group_rows // block_rows
    scale = head_dim ** (-0.5)

    def attend(inputs):
        block_query, block_pos, block_seg = inputs
        scores = (
            jnp.einsum("bhd,kd->hbk", block_query, keys_all, preferred_element_type=jnp.float32)
            * scale
        )
        allowed = (key_seg[None, :] == block_seg[:, None]) & (
            key_pos[None, :] <= block_pos[:, None]
        )
        scores = jnp.where(allowed[None], scores, -jnp.inf)
        largest = jnp.max(scores, axis=-1, keepdims=True)
        weights = jnp.exp(scores - largest)
        totals = jnp.sum(weights, axis=-1, keepdims=True)
        mixed = (
            jnp.einsum(
                "hbk,kd->hbd",
                weights.astype(jnp.bfloat16),
                values_all,
                preferred_element_type=jnp.float32,
            )
            / totals
        )
        return jnp.transpose(mixed.astype(jnp.bfloat16), (1, 0, 2)).reshape(
            block_rows, heads_here * head_dim
        )

    attended = lax.map(
        attend,
        (
            query.reshape(block_count, block_rows, heads_here, head_dim),
            group_pos.reshape(block_count, block_rows),
            own_seg.reshape(block_count, block_rows),
        ),
    )
    attended = attended.reshape(group_rows, heads_here * head_dim)
    rows = attended
    term = jnp.dot(rows, w_out, preferred_element_type=jnp.float32).astype(jnp.bfloat16)
    mixed_sum = lax.psum_scatter(
        lax.optimization_barrier(term).astype(jnp.float32).astype(jnp.bfloat16),
        "tp",
        scatter_dimension=0,
        tiled=True,
    ).astype(jnp.float32)
    residual = (tokens.astype(jnp.float32) + mixed_sum).astype(jnp.bfloat16)
    normed_moe = root_mean_norm(residual.astype(jnp.float32), moe_gain).astype(jnp.bfloat16)
    expert_count = rep_count * tp_count * w_gate_up.shape[0]
    top_count = expert_ids.shape[1]
    capacity = max(2, 3 * tok_rows * top_count // (2 * expert_count))
    hidden_units = w_down.shape[1]
    flat = expert_ids.reshape(-1)
    onehot = (flat[:, None] == jnp.arange(expert_count, dtype=jnp.int32)[None, :]).astype(jnp.int32)
    rank = jnp.sum((jnp.cumsum(onehot, axis=0) - 1) * onehot, axis=1)
    target = (flat * capacity + rank).reshape(tok_rows, top_count)
    match = (
        target[:, :, None] == jnp.arange(expert_count * capacity, dtype=jnp.int32)[None, None, :]
    )
    dispatch = jnp.any(match, axis=1).astype(jnp.bfloat16)
    combine = jnp.sum(jnp.where(match, gates[:, :, None].astype(jnp.float32), 0.0), axis=1).astype(
        jnp.bfloat16
    )
    outgoing = lax.dot_general(
        dispatch, normed_moe, (((0,), (0,)), ((), ())), preferred_element_type=jnp.float32
    )
    outgoing = outgoing.astype(jnp.bfloat16).reshape(expert_count, capacity, width)
    received = lax.all_to_all(outgoing, ("rep", "tp"), split_axis=0, concat_axis=0, tiled=True)
    rows = received.reshape(-1, width)
    gate_up = jnp.dot(rows, w_gate_up[0], preferred_element_type=jnp.float32)
    act = (jax.nn.silu(gate_up[:, :hidden_units]) * gate_up[:, hidden_units:]).astype(jnp.bfloat16)
    result = jnp.dot(act, w_down[0], preferred_element_type=jnp.float32).astype(jnp.bfloat16)
    returned = lax.all_to_all(
        result.reshape(received.shape), ("rep", "tp"), split_axis=0, concat_axis=0, tiled=True
    )
    combined = jnp.dot(
        combine,
        returned.reshape(expert_count * capacity, width),
        preferred_element_type=jnp.float32,
    )
    hidden_out = (residual.astype(jnp.float32) + combined).astype(jnp.bfloat16)
    return (hidden_out, cache)


KEY_BLOCK = 256
MASKED = -1e30


def moved(block, change):
    route = []
    for y in range(2):
        for core in range(2):
            for z in range(4):
                for x in range(2):
                    to_y, to_core, to_z, to_x = change(y, core, z, x)
                    route.append(
                        ((y * 2 + core) * 8 + z * 2 + x, (to_y * 2 + to_core) * 8 + to_z * 2 + to_x)
                    )
    return lax.ppermute(block, ("rep", "tp"), route)


def other_x(block):
    return moved(block, lambda y, core, z, x: (y, core, z, 1 - x))


def other_y(block):
    return moved(block, lambda y, core, z, x: (1 - y, core, z, x))


def other_core(block):
    return moved(block, lambda y, core, z, x: (y, 1 - core, z, x))


def across(block, over_y):
    if over_y:
        return moved(block, lambda y, core, z, x: (1 - y, 1 - core, z, x))
    return moved(block, lambda y, core, z, x: (y, 1 - core, z, 1 - x))


def other_z(block, k):
    return moved(block, lambda y, core, z, x: (y, core, z ^ k, x))


def sum_of(a, b):
    return (a.astype(jnp.float32) + b.astype(jnp.float32)).astype(jnp.bfloat16)


def after(value, earlier):
    return lax.optimization_barrier((value, earlier))[0]


def attention_kernel(
    place, low, projected, gain, cosine, sine, start, kv_here, kv_side, kv_before, kv_before_side, out,
    keys, values, acc, peak, total,
):
    z, x, slot = place[0], place[1], place[2] + pl.program_id(0)
    rows = projected.shape[0]
    head = gain.shape[1]
    heads = projected.shape[1] // head
    half = head // 2

    @pl.when(pl.program_id(0) == 0)
    def _():
        for first, near, far in ((0, kv_before, kv_before_side), (8, kv_here, kv_side)):
            for k in range(4):
                at = jnp.bitwise_xor(z, k) * 2
                for source, shift in ((near, x), (far, 1 - x)):
                    row = pl.multiple_of((first + at + shift) * rows, rows)
                    keys[pl.ds(row, rows), :] = source[k, :rows, :head]
                    values[:, pl.ds(row, rows)] = source[k, :rows, head:].astype(jnp.float32).T.astype(jnp.bfloat16)

    gain_column = jnp.broadcast_to(gain[...], (rows, head)).T
    turned = []
    for h in range(heads):
        q = projected[:, h * head : (h + 1) * head].T
        q = q * lax.rsqrt(jnp.mean(q * q, axis=0, keepdims=True) + 1e-06) * gain_column
        first, second = q[:half], q[half:]
        turned.append(
            jnp.concatenate(
                [first * cosine[0] - second * sine[0], second * cosine[0] + first * sine[0]], axis=0
            )
        )
    query = (jnp.concatenate(turned, axis=1) * (head**-0.5 * math.log2(math.e))).astype(jnp.bfloat16)
    acc[...] = jnp.zeros_like(acc)
    total[...] = jnp.zeros_like(total)
    peak[...] = jnp.full_like(peak, MASKED)
    position = (8 + jnp.bitwise_xor(z, slot) * 2 + x) * rows
    own_position = position + lax.broadcasted_iota(jnp.int32, (KEY_BLOCK, rows), 1)
    own_start = start[0]

    def step(j, _):
        row = pl.multiple_of(j * KEY_BLOCK, KEY_BLOCK)
        scores = jnp.dot(keys[pl.ds(row, KEY_BLOCK), :], query, preferred_element_type=jnp.float32)
        key_position = row + lax.broadcasted_iota(jnp.int32, (KEY_BLOCK, rows), 0)
        allowed = (key_position >= own_start) & (key_position <= own_position)
        scores = jnp.concatenate(
            [jnp.where(allowed, scores[:, h * rows : (h + 1) * rows], MASKED) for h in range(heads)], axis=1
        )
        largest = jnp.maximum(peak[...], jnp.max(scores, axis=0, keepdims=True))
        fade = jnp.exp2(peak[...] - largest)
        weights = jnp.exp2(scores - largest)
        total[...] = total[...] * fade + jnp.sum(weights, axis=0, keepdims=True)
        acc[...] = acc[...] * fade + jnp.dot(
            values[:, pl.ds(row, KEY_BLOCK)], weights.astype(jnp.bfloat16), preferred_element_type=jnp.float32
        )
        peak[...] = largest
        return 0

    lax.fori_loop(low[pl.program_id(0)], (position + rows - 1) // KEY_BLOCK + 1, step, 0)
    mixed = acc[...] / total[...]
    for h in range(heads):
        out[:, h * head : (h + 1) * head] = mixed[:, h * rows : (h + 1) * rows].T.astype(out.dtype)


def attend_slots(place, low, projected, q_gain, cosine, sine, start, kv):
    slots, rows = start.shape[0], start.shape[2]
    head = q_gain.shape[0]
    width = projected.shape[1]
    whole = lambda *shape: pl.BlockSpec(shape, lambda s, *_: (0,) * len(shape))
    return pl.pallas_call(
        attention_kernel,
        grid_spec=pltpu.PrefetchScalarGridSpec(
            num_scalar_prefetch=2,
            grid=(slots,),
            in_specs=[
                pl.BlockSpec((rows, width), lambda s, *_: (s, 0)),
                whole(1, head),
                pl.BlockSpec((1, head // 2, rows), lambda s, *_: (s, 0, 0)),
                pl.BlockSpec((1, head // 2, rows), lambda s, *_: (s, 0, 0)),
                pl.BlockSpec((1, 1, rows), lambda s, *_: (s, 0, 0)),
            ]
            + [whole(*part.shape) for part in kv],
            out_specs=pl.BlockSpec((rows, width), lambda s, *_: (s, 0)),
            scratch_shapes=[
                pltpu.VMEM((16 * rows, head), jnp.bfloat16),
                pltpu.VMEM((head, 16 * rows), jnp.bfloat16),
                pltpu.VMEM((head, width // head * rows), jnp.float32),
                pltpu.VMEM((1, width // head * rows), jnp.float32),
                pltpu.VMEM((1, width // head * rows), jnp.float32),
            ],
        ),
        out_shape=jax.ShapeDtypeStruct((slots * rows, width), jnp.bfloat16),
        compiler_params=pltpu.CompilerParams(vmem_limit_bytes=40 * 2**20),
        cost_estimate=pl.CostEstimate(
            flops=4 * slots * rows * width * 4 * rows,
            bytes_accessed=8 * 2**20,
            transcendentals=slots * width * rows,
        ),
        name="attention",
    )(place, low, projected, q_gain.reshape(1, head), cosine, sine, start, *kv)


def keyval_kernel(tokens, gain, key_gain, cosine, sine, w_key, w_value, out, normed):
    @pl.when(pl.program_id(0) == 0)
    def _():
        normed[...] = root_mean_norm(tokens[...].astype(jnp.float32), gain[...]).astype(jnp.bfloat16)

    head = key_gain.shape[1]
    half = head // 2
    k = jnp.dot(normed[...], w_key[...], preferred_element_type=jnp.float32).T
    k = k * lax.rsqrt(jnp.mean(k * k, axis=0, keepdims=True) + 1e-06)
    k = k * jnp.broadcast_to(key_gain[...], (normed.shape[0], head)).T
    first, second = k[:half], k[half:]
    k = jnp.concatenate(
        [first * cosine[0] - second * sine[0], second * cosine[0] + first * sine[0]], axis=0
    )
    out[0, :, :head] = k.T.astype(out.dtype)
    v = jnp.dot(normed[...], w_value[...], preferred_element_type=jnp.float32)
    out[0, :, head:] = v.astype(out.dtype)


def keyval_by_head(tokens, attn_gain, key_norm_gain, cosine, sine, w_keyval):
    rows, width = tokens.shape
    head = key_norm_gain.shape[0]
    heads = w_keyval.shape[1] // (2 * head)
    whole = lambda *shape: pl.BlockSpec(shape, lambda h: (0,) * len(shape))
    return pl.pallas_call(
        keyval_kernel,
        grid=(heads,),
        in_specs=[
            whole(rows, width),
            whole(1, width),
            whole(1, head),
            pl.BlockSpec((1, head // 2, rows), lambda h: (0, 0, 0)),
            pl.BlockSpec((1, head // 2, rows), lambda h: (0, 0, 0)),
            pl.BlockSpec((width, head), lambda h: (0, h)),
            pl.BlockSpec((width, head), lambda h: (0, heads + h)),
        ],
        out_specs=pl.BlockSpec((1, rows, 2 * head), lambda h: (h, 0, 0)),
        out_shape=jax.ShapeDtypeStruct((heads, rows, 2 * head), jnp.bfloat16),
        scratch_shapes=[pltpu.VMEM((rows, width), jnp.bfloat16)],
        compiler_params=pltpu.CompilerParams(vmem_limit_bytes=60 * 2**20),
        cost_estimate=pl.CostEstimate(
            flops=2 * rows * width * w_keyval.shape[1], bytes_accessed=5 * 2**20, transcendentals=0
        ),
        name="keyval",
    )(tokens, attn_gain.reshape(1, width), key_norm_gain.reshape(1, head), cosine, sine, w_keyval, w_keyval)


def grid_body(
    tokens,
    seg_ids,
    expert_ids,
    gates,
    page_table,
    attn_gain,
    q_gain,
    key_norm_gain,
    w_query,
    w_keyval,
    w_out,
    moe_gain,
    w_gate_up,
    w_down,
):
    rows, width = tokens.shape
    head = q_gain.shape[0]
    kv_heads = w_keyval.shape[1] // (2 * head)
    kv_width = kv_heads * head
    rep, tp = lax.axis_index("rep"), lax.axis_index("tp")
    y, core, z, x = rep // 2, rep % 2, tp // 2, tp % 2
    group_rows = 8 * rows
    group_start = rep * group_rows
    slots = range(4)

    slot_start = [group_start + ((z ^ k) * 2 + x) * rows for k in slots]
    slot_position = jnp.stack([at + jnp.arange(rows, dtype=jnp.int32) for at in slot_start])
    frequency = jnp.exp(
        jnp.arange(head // 2, dtype=jnp.float32) * (-2.0 * math.log(1000000.0) / head)
    )
    angles = frequency[None, :, None] * slot_position.astype(jnp.float32)[:, None, :]
    cosine, sine = jnp.cos(angles), jnp.sin(angles)

    by_head = keyval_by_head(tokens, attn_gain, key_norm_gain, cosine, sine, w_keyval)
    part = w_query.shape[1] // 4
    quarter = y * 2 + core
    far = other_z(tokens, 2)
    query_x = other_x(lax.dynamic_slice_in_dim(w_query, quarter * part, part, 1))
    by_head, late_segs, query_x, w_out = lax.optimization_barrier((by_head, seg_ids, query_x, w_out))
    out_x = other_x(lax.dynamic_slice_in_dim(w_out, quarter * part, part, 0))

    top = expert_ids.shape[1]
    routes = jnp.concatenate([expert_ids.T.astype(jnp.bfloat16), gates.T], axis=0)
    routes = jnp.concatenate([routes, other_y(routes)], axis=1)
    pick = lambda h: jnp.concatenate(
        [lax.dynamic_index_in_dim(by_head, h, 0, keepdims=False), routes], axis=0
    )
    kv_parts = [other_z(pick(z ^ k), k) for k in (1, 2, 3)]
    query_y = other_y(after(query_x, kv_parts[0]))
    kv_here = jnp.stack([pick(z)] + kv_parts)
    kv_here, out_x, far, w_query, w_out = lax.optimization_barrier((kv_here, out_x, far, w_query, w_out))
    kv_before, kv_side = passed_along(kv_here, "rep", 1), other_x(kv_here)
    farther, out_y = other_z(far, 1), other_y(out_x)
    kv_side, query_y = lax.optimization_barrier((kv_side, query_y))
    kv_before_side = passed_along(kv_side, "rep", 1)
    query_two = jnp.concatenate([query_x, query_y], axis=1)
    query_far = other_core(query_two)
    kv_before, query_far, farther, out_y = lax.optimization_barrier(
        (kv_before, query_far, farther, out_y)
    )
    w_query_wide = jnp.concatenate([w_query, query_two, query_far], axis=1)
    out_two = jnp.concatenate([out_x, out_y], axis=0)
    near = other_z(after(tokens, farther), 1)
    w_out_wide = jnp.concatenate([w_out, out_two, other_core(out_two)], axis=0)
    raw = [tokens, near, far, farther]

    pages = page_table.shape[0]
    stored = jnp.transpose(by_head.reshape(kv_heads, rows, 2, head), (1, 2, 0, 3))
    placing = (page_table[None, :] == jnp.arange(pages, dtype=jnp.int32)[:, None]).astype(jnp.bfloat16)
    cache = jnp.dot(placing, stored.reshape(pages, -1), preferred_element_type=jnp.float32)
    cache = cache.astype(jnp.bfloat16).reshape(pages, rows // pages, 2 * kv_width)

    slot_seg = jnp.concatenate(
        [lax.dynamic_slice_in_dim(late_segs, at, rows, 0) for at in slot_start]
    )
    starts = jnp.sum((late_segs[None, :] < slot_seg[:, None]).astype(jnp.int32), axis=1)
    starts = (starts - (group_start - group_rows)).reshape(4, 1, rows)
    low = starts[:, 0, 0] // KEY_BLOCK

    def projection(first):
        lines = jnp.concatenate(raw[first : first + 2], axis=0).astype(jnp.float32)
        lines = root_mean_norm(lines, attn_gain).astype(jnp.bfloat16)
        return jnp.dot(lines, w_query_wide, preferred_element_type=jnp.float32)

    def attended(first, projected):
        two = slice(first, first + 2)
        return attend_slots(
            jnp.stack([z, x, jnp.int32(first)]),
            low[two],
            projected,
            q_gain,
            cosine[two],
            sine[two],
            starts[two],
            (kv_here, kv_side, kv_before, kv_before_side),
        )

    def term_of(part):
        term = jnp.dot(part, w_out_wide, preferred_element_type=jnp.float32).astype(jnp.bfloat16)
        return term[:rows], term[rows:]

    attended_far = attended(2, projection(2))
    term_2, term_3 = term_of(attended_far)
    term_2, raw[1] = lax.optimization_barrier((term_2, near))
    far_3 = other_z(term_3, 1)
    far = other_z(sum_of(term_2, far_3), 2)
    term_0, term_1 = term_of(attended(0, after(projection(0), term_3)))
    near = other_z(term_1, 1)
    mixed_sum = term_0.astype(jnp.float32) + near.astype(jnp.float32) + far.astype(jnp.float32)
    residual = (tokens.astype(jnp.float32) + mixed_sum).astype(jnp.bfloat16)
    normed_moe = root_mean_norm(residual.astype(jnp.float32), moe_gain).astype(jnp.bfloat16)

    turned = (False, True, False, True)
    routes, over_y = kv_here[:, rows:, :rows], kv_here[:, rows:, rows:]
    over_x, corner_routes = kv_side[:, rows:, :rows], kv_side[0, rows:, rows:]
    capacity = max(2, 3 * rows * top // (2 * 32))
    pair = 2 * capacity
    mine = [rep * 8 + tp, (rep ^ 1) * 8 + tp]
    earlier = (jnp.arange(rows)[:, None] < jnp.arange(rows)[None, :]).astype(jnp.bfloat16)

    def matrices(blocks, experts):
        blocks = blocks.reshape(blocks.shape[:2] + (2, top, rows))
        experts = experts.astype(jnp.bfloat16)
        hits = blocks[:, :, 0][:, :, None] == experts[:, None, :, None, None]
        weight = jnp.sum(jnp.where(hits, blocks[:, :, 1][:, :, None].astype(jnp.float32), 0.0), axis=3)
        hit = jnp.any(hits, axis=3)
        place = jnp.dot(
            hit.reshape(-1, rows).astype(jnp.bfloat16), earlier, preferred_element_type=jnp.float32
        ).reshape(hit.shape)
        chosen = (
            place[..., None, :].astype(jnp.int32) == jnp.arange(capacity, dtype=jnp.int32)[:, None]
        ) & hit[..., None, :]
        weighted = jnp.where(chosen, weight[..., None, :], 0.0).astype(jnp.bfloat16)
        flat = hit.shape[:2] + (-1, rows)
        return chosen.astype(jnp.bfloat16).reshape(flat), weighted.reshape(flat)

    chosen, weighted = matrices(
        jnp.stack([jnp.stack([routes[k], (over_y if turned[k] else over_x)[k]]) for k in slots]),
        jnp.stack([jnp.stack(mine + [e ^ 1 if turned[k] else e ^ 16 for e in mine]) for k in slots]),
    )
    chosen_second, _ = matrices(jnp.stack([over_y[0], corner_routes])[None], jnp.stack(mine)[None])
    chosen_0 = jnp.concatenate([chosen[0, :, :pair], chosen_second[0]], axis=0)

    def experts_of(slot_rows_in):
        gate_up = jnp.dot(slot_rows_in, w_gate_up[0], preferred_element_type=jnp.float32)
        hidden = w_down.shape[1]
        act = (jax.nn.silu(gate_up[:, :hidden]) * gate_up[:, hidden:]).astype(jnp.bfloat16)
        return jnp.dot(act, w_down[0], preferred_element_type=jnp.float32).astype(jnp.bfloat16)

    together = lambda *values: lax.optimization_barrier(values)

    def picks(k, block, side):
        picked = lax.dot_general(
            chosen[k], jnp.stack([block, side]), (((2,), (1,)), ((0,), (0,))), preferred_element_type=jnp.float32
        ).astype(jnp.bfloat16)
        return picked[:, :pair], picked[:, pair:]

    def routed(picked):
        kept = picked[:, :capacity].reshape(-1, width)
        return jnp.concatenate([kept, other_core(picked[:, capacity:].reshape(-1, width))], axis=0)

    half = rows // 2
    near, far = other_z(normed_moe, 1), other_z(normed_moe, 2)
    side_x, side_y = together(other_x(normed_moe), other_y(normed_moe))
    near, far, *corner = together(near, far, other_y(side_x[:half]), other_x(side_y[half:]))
    side_1, side_2, farther = other_y(near), other_x(far), other_z(far, 1)
    corner = jnp.concatenate(corner, axis=0)
    picked_0 = lax.dot_general(
        chosen_0,
        jnp.stack([normed_moe, side_x, side_y, corner]),
        (((2,), (1,)), ((0,), (0,))),
        preferred_element_type=jnp.float32,
    ).astype(jnp.bfloat16)
    side_2, farther, picked_0 = together(side_2, farther, picked_0)
    mine_2, theirs_2 = picks(2, far, side_2)
    side_3 = other_y(farther)
    side_1, mine_2, theirs_2 = together(side_1, mine_2, theirs_2)
    mine_1, theirs_1 = picks(1, near, side_1)
    theirs_1 = other_x(theirs_1)

    def over_second(to_y, to_y_across, to_x, to_x_across):
        return together(
            other_y(to_y), across(to_y_across, True), other_x(to_x), across(to_x_across, False)
        )

    def experts_on(*parts):
        return experts_of(jnp.concatenate(parts, axis=0).reshape(-1, width)).reshape(-1, capacity, width)

    kept = lambda *parts: jnp.concatenate([part[:, :capacity] for part in parts], axis=0)
    traded = lambda *parts: other_core(jnp.concatenate([part[:, capacity:] for part in parts], axis=0))
    result_0 = experts_of(routed(picked_0))
    result_12 = experts_on(kept(mine_1, mine_2), traded(mine_1, mine_2))
    side_3, theirs_2, result_0, result_12 = together(side_3, theirs_2, result_0, result_12)
    mine_3, theirs_3 = picks(3, farther, side_3)
    theirs_3, theirs_1 = together(theirs_3, theirs_1)
    late = traded(mine_3, theirs_1)
    got = over_second(
        theirs_2[:, :capacity], theirs_2[:, capacity:], theirs_3[:, :capacity], theirs_3[:, capacity:]
    )
    *got, late = together(*got, late)
    got, late = together(experts_on(*got), late)
    result_31 = experts_on(kept(mine_3, theirs_1), late)
    both = lambda result: jnp.concatenate([result[:4], other_core(result[4:])], axis=1)
    here_1, here_2 = jnp.split(both(result_12), 2)
    here_3, there_1 = jnp.split(both(result_31), 2)

    def back(result):
        traded = other_core(result[4 * capacity :])
        both = jnp.stack([result[: 4 * capacity], traded]).reshape(2, 4, capacity, width)
        both = jnp.transpose(both, (1, 0, 2, 3)).reshape(4, pair, width)
        return both[:2], both[2:]

    def summed(k, here, there):
        total = lax.dot_general(
            weighted[k],
            jnp.concatenate([here, there], axis=1),
            (((1,), (1,)), ((0,), (0,))),
            preferred_element_type=jnp.float32,
        ).astype(jnp.bfloat16)
        return total[0], total[1]

    here_0, there_0 = back(result_0)
    there = over_second(got[:2], got[2:4], got[4:6], got[6:])
    there_2, there_3 = jnp.concatenate(there[:2], axis=1), jnp.concatenate(there[2:], axis=1)
    (own_2, side_2), (own_3, side_3) = summed(2, here_2, there_2), summed(3, here_3, there_3)
    side_2, side_3, there_0, there_1 = together(other_x(side_2), other_y(side_3), there_0, there_1)
    far_3 = other_z(sum_of(own_3, side_3), 1)
    there_0, there_1 = together(other_y(there_0), other_x(there_1))
    (own_0, side_0), (own_1, side_1) = summed(0, here_0, there_0), summed(1, here_1, there_1)
    far = own_2.astype(jnp.float32) + side_2.astype(jnp.float32) + far_3.astype(jnp.float32)
    far = other_z(far.astype(jnp.bfloat16), 2)
    side_0 = other_x(side_0)
    near = [
        other_z(sum_of(own_1[part], other_y(side_1[part])), 1) for part in (slice(0, half), slice(half, rows))
    ]
    near = jnp.concatenate(near, axis=0)
    combined = residual.astype(jnp.float32)
    for value in (far, near, own_0, side_0):
        combined = combined + value.astype(jnp.float32)
    return (combined.astype(jnp.bfloat16), cache)


def solution(mesh):
    in_specs = (
        P(("rep", "tp"), None),
        P(),
        P(("rep", "tp"), None),
        P(("rep", "tp"), None),
        P(("rep", "tp")),
        P(),
        P(),
        P(),
        P(None, "tp"),
        P(),
        P("tp", None),
        P(),
        P(("rep", "tp"), None, None),
        P(("rep", "tp"), None, None),
    )
    out_specs = (P(("rep", "tp"), None), P(("rep", "tp"), None, None))
    body = grid_body if (mesh.shape["rep"], mesh.shape["tp"]) == (4, 8) else general_body
    return jax.shard_map(body, mesh=mesh, in_specs=in_specs, out_specs=out_specs, check_vma=False)
```

```python
import functools
import math

import jax
import jax.numpy as jnp
from jax import lax
from jax.experimental import pallas as pl
from jax.experimental.pallas import tpu as pltpu
from jax.sharding import PartitionSpec as P


def passed_along(block, axis, distance):
    devices = range(lax.axis_size(axis))
    route = [(i - distance, i) for i in devices if i - distance in devices]
    return lax.ppermute(block, axis, route)


def root_mean_norm(value_rows, gain):
    return (
        value_rows
        * lax.rsqrt(jnp.mean(value_rows * value_rows, axis=-1, keepdims=True) + 1e-06)
        * gain
    )


def apply_rotary(value_rows, token_positions):
    half_dim = value_rows.shape[-1] // 2
    frequency = jnp.exp(
        jnp.arange(half_dim, dtype=jnp.float32)
        * (-2.0 * math.log(1000000.0) / value_rows.shape[-1])
    )
    angles = token_positions[:, None] * frequency[None, :]
    cosine = jnp.cos(angles)[:, None, :]
    sine_part = jnp.sin(angles)[:, None, :]
    first = value_rows[..., :half_dim]
    second = value_rows[..., half_dim:]
    return jnp.concatenate(
        [first * cosine - second * sine_part, second * cosine + first * sine_part], axis=-1
    )


def general_body(
    tokens,
    seg_ids,
    expert_ids,
    gates,
    page_table,
    attn_gain,
    q_gain,
    key_norm_gain,
    w_query,
    w_keyval,
    w_out,
    moe_gain,
    w_gate_up,
    w_down,
):
    tok_rows, width = tokens.shape
    tp_count = lax.axis_size("tp")
    rep_count = lax.axis_size("rep")
    rep_index = lax.axis_index("rep")
    tp_index = lax.axis_index("tp")
    group_rows = tok_rows * tp_count
    head_dim = q_gain.shape[0]
    q_width = w_query.shape[1]
    heads_here = q_width // head_dim
    kv_heads = w_keyval.shape[1] // (2 * head_dim)
    kv_width = kv_heads * head_dim
    per_key_value = heads_here * tp_count // kv_heads
    own_head = tp_index * heads_here // per_key_value
    first_row = (rep_index * tp_count + tp_index) * tok_rows
    local_pos = (first_row + jnp.arange(tok_rows, dtype=jnp.int32)).astype(jnp.float32)
    normed = root_mean_norm(tokens.astype(jnp.float32), attn_gain).astype(jnp.bfloat16)
    key_value_rows = jnp.dot(normed, w_keyval, preferred_element_type=jnp.float32)
    rotary_output = apply_rotary(
        root_mean_norm(
            key_value_rows[:, :kv_width].reshape(tok_rows, kv_heads, head_dim), key_norm_gain
        ),
        local_pos,
    )
    stored_cache = jnp.concatenate(
        [rotary_output.reshape(tok_rows, kv_width), key_value_rows[:, kv_width:]], axis=1
    ).astype(jnp.bfloat16)
    page_count = page_table.shape[0]
    placement_matrix = (
        page_table[None, :] == jnp.arange(page_count, dtype=jnp.int32)[:, None]
    ).astype(jnp.bfloat16)
    cache = jnp.dot(
        placement_matrix, stored_cache.reshape(page_count, -1), preferred_element_type=jnp.float32
    )
    cache = cache.astype(jnp.bfloat16).reshape(page_count, tok_rows // page_count, 2 * kv_width)
    projected = jnp.dot(
        lax.all_gather(normed, "tp", axis=0, tiled=True),
        w_query,
        preferred_element_type=jnp.float32,
    )
    group_start = rep_index * group_rows
    group_pos = group_start + jnp.arange(group_rows, dtype=jnp.int32)
    group_posf = group_pos.astype(jnp.float32)
    query = root_mean_norm(projected.reshape(group_rows, heads_here, head_dim), q_gain)
    query = apply_rotary(query, group_posf).astype(jnp.bfloat16)
    gathered = lax.all_gather(stored_cache, "tp", axis=0, tiled=True)
    own_keys = lax.dynamic_slice_in_dim(gathered, own_head * head_dim, head_dim, 1)
    own_values = lax.dynamic_slice_in_dim(gathered, kv_width + own_head * head_dim, head_dim, 1)
    earlier_keys, earlier_values = passed_along((own_keys, own_values), "rep", 1)
    own_seg = lax.dynamic_slice_in_dim(seg_ids, group_start, group_rows, 0)
    earlier_seg = lax.dynamic_slice_in_dim(
        seg_ids, jnp.maximum(group_start - group_rows, 0), group_rows, 0
    )
    earlier_seg = jnp.where(rep_index > 0, earlier_seg, -1)
    keys_all = jnp.concatenate([earlier_keys, own_keys], axis=0)
    values_all = jnp.concatenate([earlier_values, own_values], axis=0)
    key_seg = jnp.concatenate([earlier_seg, own_seg], axis=0)
    key_pos = group_start - group_rows + jnp.arange(2 * group_rows, dtype=jnp.int32)
    block_rows = min(512, group_rows)
    block_count = group_rows // block_rows
    scale = head_dim ** (-0.5)

    def attend(inputs):
        block_query, block_pos, block_seg = inputs
        scores = (
            jnp.einsum("bhd,kd->hbk", block_query, keys_all, preferred_element_type=jnp.float32)
            * scale
        )
        allowed = (key_seg[None, :] == block_seg[:, None]) & (
            key_pos[None, :] <= block_pos[:, None]
        )
        scores = jnp.where(allowed[None], scores, -jnp.inf)
        largest = jnp.max(scores, axis=-1, keepdims=True)
        weights = jnp.exp(scores - largest)
        totals = jnp.sum(weights, axis=-1, keepdims=True)
        mixed = (
            jnp.einsum(
                "hbk,kd->hbd",
                weights.astype(jnp.bfloat16),
                values_all,
                preferred_element_type=jnp.float32,
            )
            / totals
        )
        return jnp.transpose(mixed.astype(jnp.bfloat16), (1, 0, 2)).reshape(
            block_rows, heads_here * head_dim
        )

    attended = lax.map(
        attend,
        (
            query.reshape(block_count, block_rows, heads_here, head_dim),
            group_pos.reshape(block_count, block_rows),
            own_seg.reshape(block_count, block_rows),
        ),
    )
    attended = attended.reshape(group_rows, heads_here * head_dim)
    rows = attended
    term = jnp.dot(rows, w_out, preferred_element_type=jnp.float32).astype(jnp.bfloat16)
    mixed_sum = lax.psum_scatter(
        lax.optimization_barrier(term).astype(jnp.float32).astype(jnp.bfloat16),
        "tp",
        scatter_dimension=0,
        tiled=True,
    ).astype(jnp.float32)
    residual = (tokens.astype(jnp.float32) + mixed_sum).astype(jnp.bfloat16)
    normed_moe = root_mean_norm(residual.astype(jnp.float32), moe_gain).astype(jnp.bfloat16)
    expert_count = rep_count * tp_count * w_gate_up.shape[0]
    top_count = expert_ids.shape[1]
    capacity = max(2, 3 * tok_rows * top_count // (2 * expert_count))
    hidden_units = w_down.shape[1]
    flat = expert_ids.reshape(-1)
    onehot = (flat[:, None] == jnp.arange(expert_count, dtype=jnp.int32)[None, :]).astype(jnp.int32)
    rank = jnp.sum((jnp.cumsum(onehot, axis=0) - 1) * onehot, axis=1)
    target = (flat * capacity + rank).reshape(tok_rows, top_count)
    match = (
        target[:, :, None] == jnp.arange(expert_count * capacity, dtype=jnp.int32)[None, None, :]
    )
    dispatch = jnp.any(match, axis=1).astype(jnp.bfloat16)
    combine = jnp.sum(jnp.where(match, gates[:, :, None].astype(jnp.float32), 0.0), axis=1).astype(
        jnp.bfloat16
    )
    outgoing = lax.dot_general(
        dispatch, normed_moe, (((0,), (0,)), ((), ())), preferred_element_type=jnp.float32
    )
    outgoing = outgoing.astype(jnp.bfloat16).reshape(expert_count, capacity, width)
    received = lax.all_to_all(outgoing, ("rep", "tp"), split_axis=0, concat_axis=0, tiled=True)
    rows = received.reshape(-1, width)
    gate_up = jnp.dot(rows, w_gate_up[0], preferred_element_type=jnp.float32)
    act = (jax.nn.silu(gate_up[:, :hidden_units]) * gate_up[:, hidden_units:]).astype(jnp.bfloat16)
    result = jnp.dot(act, w_down[0], preferred_element_type=jnp.float32).astype(jnp.bfloat16)
    returned = lax.all_to_all(
        result.reshape(received.shape), ("rep", "tp"), split_axis=0, concat_axis=0, tiled=True
    )
    combined = jnp.dot(
        combine,
        returned.reshape(expert_count * capacity, width),
        preferred_element_type=jnp.float32,
    )
    hidden_out = (residual.astype(jnp.float32) + combined).astype(jnp.bfloat16)
    return (hidden_out, cache)


KEY_BLOCK = 256
MASKED = -1e30


def moved(block, change):
    route = []
    for y in range(2):
        for core in range(2):
            for z in range(4):
                for x in range(2):
                    to_y, to_core, to_z, to_x = change(y, core, z, x)
                    route.append(
                        ((y * 2 + core) * 8 + z * 2 + x, (to_y * 2 + to_core) * 8 + to_z * 2 + to_x)
                    )
    return lax.ppermute(block, ("rep", "tp"), route)


def other_x(block):
    return moved(block, lambda y, core, z, x: (y, core, z, 1 - x))


def other_y(block):
    return moved(block, lambda y, core, z, x: (1 - y, core, z, x))


def other_core(block):
    return moved(block, lambda y, core, z, x: (y, 1 - core, z, x))


def across(block, over_y):
    if over_y:
        return moved(block, lambda y, core, z, x: (1 - y, 1 - core, z, x))
    return moved(block, lambda y, core, z, x: (y, 1 - core, z, 1 - x))


def other_z(block, k):
    return moved(block, lambda y, core, z, x: (y, core, z ^ k, x))


def sum_of(a, b):
    return (a.astype(jnp.float32) + b.astype(jnp.float32)).astype(jnp.bfloat16)


def after(value, earlier):
    return lax.optimization_barrier((value, earlier))[0]


def attention_kernel(
    first_slot, place, low, projected, gain, cosine, sine, start, kv_here, kv_side, kv_before, kv_before_side, out,
    keys, values, acc, peak, total,
):
    z, x, slot = place[0], place[1], first_slot + pl.program_id(0)
    rows = projected.shape[0]
    head = gain.shape[1]
    heads = projected.shape[1] // head
    half = head // 2

    @pl.when(pl.program_id(0) == 0)
    def _():
        for first, near, far in ((0, kv_before, kv_before_side), (8, kv_here, kv_side)):
            for k in range(4):
                at = jnp.bitwise_xor(z, k) * 2
                for source, shift in ((near, x), (far, 1 - x)):
                    row = pl.multiple_of((first + at + shift) * rows, rows)
                    keys[pl.ds(row, rows), :] = source[k, :rows, :head]
                    values[:, pl.ds(row, rows)] = source[k, :rows, head:].astype(jnp.float32).T.astype(jnp.bfloat16)

    gain_column = jnp.broadcast_to(gain[...], (rows, head)).T
    turned = []
    for h in range(heads):
        q = projected[:, h * head : (h + 1) * head].T
        q = q * lax.rsqrt(jnp.mean(q * q, axis=0, keepdims=True) + 1e-06) * gain_column
        first, second = q[:half], q[half:]
        turned.append(
            jnp.concatenate(
                [first * cosine[0] - second * sine[0], second * cosine[0] + first * sine[0]], axis=0
            )
        )
    query = (jnp.concatenate(turned, axis=1) * (head**-0.5 * math.log2(math.e))).astype(jnp.bfloat16)
    acc[...] = jnp.zeros_like(acc)
    total[...] = jnp.zeros_like(total)
    peak[...] = jnp.full_like(peak, MASKED)
    position = (8 + jnp.bitwise_xor(z, slot) * 2 + x) * rows
    own_position = position + lax.broadcasted_iota(jnp.int32, (KEY_BLOCK, rows), 1)
    own_start = start[0]

    def step(j, _):
        row = pl.multiple_of(j * KEY_BLOCK, KEY_BLOCK)
        scores = jnp.dot(keys[pl.ds(row, KEY_BLOCK), :], query, preferred_element_type=jnp.float32)
        key_position = row + lax.broadcasted_iota(jnp.int32, (KEY_BLOCK, rows), 0)
        allowed = (key_position >= own_start) & (key_position <= own_position)
        scores = jnp.concatenate(
            [jnp.where(allowed, scores[:, h * rows : (h + 1) * rows], MASKED) for h in range(heads)], axis=1
        )
        largest = jnp.maximum(peak[...], jnp.max(scores, axis=0, keepdims=True))
        fade = jnp.exp2(peak[...] - largest)
        weights = jnp.exp2(scores - largest)
        total[...] = total[...] * fade + jnp.sum(weights, axis=0, keepdims=True)
        acc[...] = acc[...] * fade + jnp.dot(
            values[:, pl.ds(row, KEY_BLOCK)], weights.astype(jnp.bfloat16), preferred_element_type=jnp.float32
        )
        peak[...] = largest
        return 0

    lax.fori_loop(low[slot], (position + rows - 1) // KEY_BLOCK + 1, step, 0)
    mixed = acc[...] / total[...]
    for h in range(heads):
        out[:, h * head : (h + 1) * head] = mixed[:, h * rows : (h + 1) * rows].T.astype(out.dtype)


def attend_slots(first_slot, place, low, projected, q_gain, cosine, sine, start, kv):
    rows = start.shape[2]
    slots = projected.shape[0] // rows
    head = q_gain.shape[0]
    width = projected.shape[1]
    whole = lambda *shape: pl.BlockSpec(shape, lambda s, *_: (0,) * len(shape))
    return pl.pallas_call(
        functools.partial(attention_kernel, first_slot),
        grid_spec=pltpu.PrefetchScalarGridSpec(
            num_scalar_prefetch=2,
            grid=(slots,),
            in_specs=[
                pl.BlockSpec((rows, width), lambda s, *_: (s, 0)),
                whole(1, head),
                pl.BlockSpec((1, head // 2, rows), lambda s, *_: (first_slot + s, 0, 0)),
                pl.BlockSpec((1, head // 2, rows), lambda s, *_: (first_slot + s, 0, 0)),
                pl.BlockSpec((1, 1, rows), lambda s, *_: (first_slot + s, 0, 0)),
            ]
            + [whole(*part.shape) for part in kv],
            out_specs=pl.BlockSpec((rows, width), lambda s, *_: (s, 0)),
            scratch_shapes=[
                pltpu.VMEM((16 * rows, head), jnp.bfloat16),
                pltpu.VMEM((head, 16 * rows), jnp.bfloat16),
                pltpu.VMEM((head, width // head * rows), jnp.float32),
                pltpu.VMEM((1, width // head * rows), jnp.float32),
                pltpu.VMEM((1, width // head * rows), jnp.float32),
            ],
        ),
        out_shape=jax.ShapeDtypeStruct((slots * rows, width), jnp.bfloat16),
        compiler_params=pltpu.CompilerParams(vmem_limit_bytes=40 * 2**20),
        cost_estimate=pl.CostEstimate(
            flops=4 * slots * rows * width * 4 * rows,
            bytes_accessed=8 * 2**20,
            transcendentals=slots * width * rows,
        ),
        name="attention",
    )(place, low, projected, q_gain.reshape(1, head), cosine, sine, start, *kv)


def keyval_kernel(tokens, gain, key_gain, cosine, sine, w_key, w_value, out, normed):
    @pl.when(pl.program_id(0) == 0)
    def _():
        normed[...] = root_mean_norm(tokens[...].astype(jnp.float32), gain[...]).astype(jnp.bfloat16)

    head = key_gain.shape[1]
    half = head // 2
    k = jnp.dot(normed[...], w_key[...], preferred_element_type=jnp.float32).T
    k = k * lax.rsqrt(jnp.mean(k * k, axis=0, keepdims=True) + 1e-06)
    k = k * jnp.broadcast_to(key_gain[...], (normed.shape[0], head)).T
    first, second = k[:half], k[half:]
    k = jnp.concatenate(
        [first * cosine[0] - second * sine[0], second * cosine[0] + first * sine[0]], axis=0
    )
    out[0, :, :head] = k.T.astype(out.dtype)
    v = jnp.dot(normed[...], w_value[...], preferred_element_type=jnp.float32)
    out[0, :, head:] = v.astype(out.dtype)


def keyval_by_head(tokens, attn_gain, key_norm_gain, cosine, sine, w_keyval):
    rows, width = tokens.shape
    head = key_norm_gain.shape[0]
    heads = w_keyval.shape[1] // (2 * head)
    whole = lambda *shape: pl.BlockSpec(shape, lambda h: (0,) * len(shape))
    return pl.pallas_call(
        keyval_kernel,
        grid=(heads,),
        in_specs=[
            whole(rows, width),
            whole(1, width),
            whole(1, head),
            pl.BlockSpec((1, head // 2, rows), lambda h: (0, 0, 0)),
            pl.BlockSpec((1, head // 2, rows), lambda h: (0, 0, 0)),
            pl.BlockSpec((width, head), lambda h: (0, h)),
            pl.BlockSpec((width, head), lambda h: (0, heads + h)),
        ],
        out_specs=pl.BlockSpec((1, rows, 2 * head), lambda h: (h, 0, 0)),
        out_shape=jax.ShapeDtypeStruct((heads, rows, 2 * head), jnp.bfloat16),
        scratch_shapes=[pltpu.VMEM((rows, width), jnp.bfloat16)],
        compiler_params=pltpu.CompilerParams(vmem_limit_bytes=60 * 2**20),
        cost_estimate=pl.CostEstimate(
            flops=2 * rows * width * w_keyval.shape[1], bytes_accessed=5 * 2**20, transcendentals=0
        ),
        name="keyval",
    )(tokens, attn_gain.reshape(1, width), key_norm_gain.reshape(1, head), cosine, sine, w_keyval, w_keyval)


def grid_body(
    tokens,
    seg_ids,
    expert_ids,
    gates,
    page_table,
    attn_gain,
    q_gain,
    key_norm_gain,
    w_query,
    w_keyval,
    w_out,
    moe_gain,
    w_gate_up,
    w_down,
):
    rows, width = tokens.shape
    head = q_gain.shape[0]
    kv_heads = w_keyval.shape[1] // (2 * head)
    kv_width = kv_heads * head
    rep, tp = lax.axis_index("rep"), lax.axis_index("tp")
    y, core, z, x = rep // 2, rep % 2, tp // 2, tp % 2
    group_rows = 8 * rows
    group_start = rep * group_rows
    slots = range(4)

    slot_start = [group_start + ((z ^ k) * 2 + x) * rows for k in slots]
    slot_position = jnp.stack([at + jnp.arange(rows, dtype=jnp.int32) for at in slot_start])
    frequency = jnp.exp(
        jnp.arange(head // 2, dtype=jnp.float32) * (-2.0 * math.log(1000000.0) / head)
    )
    angles = frequency[None, :, None] * slot_position.astype(jnp.float32)[:, None, :]
    cosine, sine = jnp.cos(angles), jnp.sin(angles)

    by_head = keyval_by_head(tokens, attn_gain, key_norm_gain, cosine, sine, w_keyval)
    part = w_query.shape[1] // 4
    quarter = y * 2 + core
    far = other_z(tokens, 2)
    query_x = other_x(lax.dynamic_slice_in_dim(w_query, quarter * part, part, 1))
    by_head, late_segs, query_x, w_out = lax.optimization_barrier((by_head, seg_ids, query_x, w_out))
    out_x = other_x(lax.dynamic_slice_in_dim(w_out, quarter * part, part, 0))

    top = expert_ids.shape[1]
    routes = jnp.concatenate([expert_ids.T.astype(jnp.bfloat16), gates.T], axis=0)
    routes = jnp.concatenate([routes, other_y(routes)], axis=1)
    pick = lambda h: jnp.concatenate(
        [lax.dynamic_index_in_dim(by_head, h, 0, keepdims=False), routes], axis=0
    )
    kv_parts = [other_z(pick(z ^ k), k) for k in (1, 2, 3)]
    query_y = other_y(after(query_x, kv_parts[0]))
    kv_here = jnp.stack([pick(z)] + kv_parts)
    kv_here, out_x, far, w_query, w_out = lax.optimization_barrier((kv_here, out_x, far, w_query, w_out))
    kv_before, kv_side = passed_along(kv_here, "rep", 1), other_x(kv_here)
    farther, out_y = other_z(far, 1), other_y(out_x)
    kv_side, query_y = lax.optimization_barrier((kv_side, query_y))
    kv_before_side = passed_along(kv_side, "rep", 1)
    query_two = jnp.concatenate([query_x, query_y], axis=1)
    query_far = other_core(query_two)
    kv_before, query_far, farther, out_y = lax.optimization_barrier(
        (kv_before, query_far, farther, out_y)
    )
    w_query_wide = jnp.concatenate([w_query, query_two, query_far], axis=1)
    out_two = jnp.concatenate([out_x, out_y], axis=0)
    near = other_z(after(tokens, farther), 1)
    w_out_wide = jnp.concatenate([w_out, out_two, other_core(out_two)], axis=0)
    raw = [tokens, near, far, farther]

    pages = page_table.shape[0]
    stored = jnp.transpose(by_head.reshape(kv_heads, rows, 2, head), (1, 2, 0, 3))
    placing = (page_table[None, :] == jnp.arange(pages, dtype=jnp.int32)[:, None]).astype(jnp.bfloat16)
    cache = jnp.dot(placing, stored.reshape(pages, -1), preferred_element_type=jnp.float32)
    cache = cache.astype(jnp.bfloat16).reshape(pages, rows // pages, 2 * kv_width)

    slot_seg = jnp.concatenate(
        [lax.dynamic_slice_in_dim(late_segs, at, rows, 0) for at in slot_start]
    )
    starts = jnp.sum((late_segs[None, :] < slot_seg[:, None]).astype(jnp.int32), axis=1)
    starts = (starts - (group_start - group_rows)).reshape(4, 1, rows)
    low = starts[:, 0, 0] // KEY_BLOCK

    def projection(first):
        lines = jnp.concatenate(raw[first : first + 2], axis=0).astype(jnp.float32)
        lines = root_mean_norm(lines, attn_gain).astype(jnp.bfloat16)
        return jnp.dot(lines, w_query_wide, preferred_element_type=jnp.float32)

    def attended(first, projected):
        return attend_slots(
            first,
            jnp.stack([z, x]),
            low,
            projected,
            q_gain,
            cosine,
            sine,
            starts,
            (kv_here, kv_side, kv_before, kv_before_side),
        )

    def term_of(part):
        term = jnp.dot(part, w_out_wide, preferred_element_type=jnp.float32).astype(jnp.bfloat16)
        return term[:rows], term[rows:]

    attended_far = attended(2, projection(2))
    term_2, term_3 = term_of(attended_far)
    term_2, raw[1] = lax.optimization_barrier((term_2, near))
    far_3 = other_z(term_3, 1)
    far = other_z(sum_of(term_2, far_3), 2)
    term_0, term_1 = term_of(attended(0, after(projection(0), term_3)))
    near = other_z(term_1, 1)
    mixed_sum = term_0.astype(jnp.float32) + near.astype(jnp.float32) + far.astype(jnp.float32)
    residual = (tokens.astype(jnp.float32) + mixed_sum).astype(jnp.bfloat16)
    normed_moe = root_mean_norm(residual.astype(jnp.float32), moe_gain).astype(jnp.bfloat16)

    turned = (False, True, False, True)
    routes, over_y = kv_here[:, rows:, :rows], kv_here[:, rows:, rows:]
    over_x, corner_routes = kv_side[:, rows:, :rows], kv_side[0, rows:, rows:]
    capacity = max(2, 3 * rows * top // (2 * 32))
    pair = 2 * capacity
    mine = [rep * 8 + tp, (rep ^ 1) * 8 + tp]
    earlier = (jnp.arange(rows)[:, None] < jnp.arange(rows)[None, :]).astype(jnp.bfloat16)

    def matrices(blocks, experts):
        blocks = blocks.reshape(blocks.shape[:2] + (2, top, rows))
        experts = experts.astype(jnp.bfloat16)
        hits = blocks[:, :, 0][:, :, None] == experts[:, None, :, None, None]
        weight = jnp.sum(jnp.where(hits, blocks[:, :, 1][:, :, None].astype(jnp.float32), 0.0), axis=3)
        hit = jnp.any(hits, axis=3)
        place = jnp.dot(
            hit.reshape(-1, rows).astype(jnp.bfloat16), earlier, preferred_element_type=jnp.float32
        ).reshape(hit.shape)
        chosen = (
            place[..., None, :].astype(jnp.int32) == jnp.arange(capacity, dtype=jnp.int32)[:, None]
        ) & hit[..., None, :]
        weighted = jnp.where(chosen, weight[..., None, :], 0.0).astype(jnp.bfloat16)
        flat = hit.shape[:2] + (-1, rows)
        return chosen.astype(jnp.bfloat16).reshape(flat), weighted.reshape(flat)

    pairs = [jnp.stack([routes[k], (over_y if turned[k] else over_x)[k]]) for k in slots]
    theirs = [[e ^ 1 if turned[k] else e ^ 16 for e in mine] for k in slots]
    chosen, weighted = matrices(
        jnp.stack(pairs + [jnp.stack([over_y[0], corner_routes])]),
        jnp.stack([jnp.stack(mine + others) for others in theirs + [mine]]),
    )
    chosen_0 = jnp.concatenate([chosen[0, :, :pair], chosen[4, :, :pair]], axis=0)

    def experts_of(slot_rows_in):
        gate_up = jnp.dot(slot_rows_in, w_gate_up[0], preferred_element_type=jnp.float32)
        hidden = w_down.shape[1]
        act = (jax.nn.silu(gate_up[:, :hidden]) * gate_up[:, hidden:]).astype(jnp.bfloat16)
        return jnp.dot(act, w_down[0], preferred_element_type=jnp.float32).astype(jnp.bfloat16)

    together = lambda *values: lax.optimization_barrier(values)

    def picks(k, block, side):
        picked = lax.dot_general(
            chosen[k], jnp.stack([block, side]), (((2,), (1,)), ((0,), (0,))), preferred_element_type=jnp.float32
        ).astype(jnp.bfloat16)
        return picked[:, :pair], picked[:, pair:]

    half = rows // 2
    near, far = other_z(normed_moe, 1), other_z(normed_moe, 2)
    side_x, side_y = together(other_x(normed_moe), other_y(normed_moe))
    near, far, *corner = together(near, far, other_y(side_x[:half]), other_x(side_y[half:]))
    side_1, side_2, farther = other_y(near), other_x(far), other_z(far, 1)
    corner = jnp.concatenate(corner, axis=0)
    picked_0 = lax.dot_general(
        chosen_0,
        jnp.stack([normed_moe, side_x, side_y, corner]),
        (((2,), (1,)), ((0,), (0,))),
        preferred_element_type=jnp.float32,
    ).astype(jnp.bfloat16)
    side_2, farther, picked_0 = together(side_2, farther, picked_0)
    mine_2, theirs_2 = picks(2, far, side_2)
    side_3 = other_y(farther)
    side_1, mine_2, theirs_2 = together(side_1, mine_2, theirs_2)
    mine_1, theirs_1 = picks(1, near, side_1)
    theirs_1 = other_x(theirs_1)

    def over_second(to_y, to_y_across, to_x, to_x_across):
        return together(
            other_y(to_y), across(to_y_across, True), other_x(to_x), across(to_x_across, False)
        )

    def experts_on(*parts):
        return experts_of(jnp.concatenate(parts, axis=0).reshape(-1, width)).reshape(-1, capacity, width)

    kept = lambda *parts: jnp.concatenate([part[:, :capacity] for part in parts], axis=0)
    traded = lambda *parts: other_core(jnp.concatenate([part[:, capacity:] for part in parts], axis=0))
    result_0 = experts_on(kept(picked_0), traded(picked_0))
    result_12 = experts_on(kept(mine_1, mine_2), traded(mine_1, mine_2))
    side_3, theirs_2, result_0, result_12 = together(side_3, theirs_2, result_0, result_12)
    mine_3, theirs_3 = picks(3, farther, side_3)
    theirs_3, theirs_1 = together(theirs_3, theirs_1)
    late = traded(mine_3, theirs_1)
    got = over_second(
        theirs_2[:, :capacity], theirs_2[:, capacity:], theirs_3[:, :capacity], theirs_3[:, capacity:]
    )
    *got, late = together(*got, late)
    got, late = together(experts_on(*got), late)
    result_31 = experts_on(kept(mine_3, theirs_1), late)
    both = lambda result: jnp.concatenate([result[:4], other_core(result[4:])], axis=1)
    here_1, here_2 = jnp.split(both(result_12), 2)
    here_3, there_1 = jnp.split(both(result_31), 2)

    def summed(k, here, there):
        total = lax.dot_general(
            weighted[k],
            jnp.concatenate([here, there], axis=1),
            (((1,), (1,)), ((0,), (0,))),
            preferred_element_type=jnp.float32,
        ).astype(jnp.bfloat16)
        return total[0], total[1]

    here_0, there_0 = jnp.split(both(result_0), 2)
    there = over_second(got[:2], got[2:4], got[4:6], got[6:])
    there_2, there_3 = jnp.concatenate(there[:2], axis=1), jnp.concatenate(there[2:], axis=1)
    (own_2, side_2), (own_3, side_3) = summed(2, here_2, there_2), summed(3, here_3, there_3)
    side_2, side_3, there_0, there_1 = together(other_x(side_2), other_y(side_3), there_0, there_1)
    far_3 = other_z(sum_of(own_3, side_3), 1)
    there_0, there_1 = together(other_y(there_0), other_x(there_1))
    (own_0, side_0), (own_1, side_1) = summed(0, here_0, there_0), summed(1, here_1, there_1)
    far = own_2.astype(jnp.float32) + side_2.astype(jnp.float32) + far_3.astype(jnp.float32)
    far = other_z(far.astype(jnp.bfloat16), 2)
    side_0 = other_x(side_0)
    near = [
        other_z(sum_of(own_1[part], other_y(side_1[part])), 1) for part in (slice(0, half), slice(half, rows))
    ]
    near = jnp.concatenate(near, axis=0)
    combined = residual.astype(jnp.float32)
    for value in (far, near, own_0, side_0):
        combined = combined + value.astype(jnp.float32)
    return (combined.astype(jnp.bfloat16), cache)


def solution(mesh):
    in_specs = (
        P(("rep", "tp"), None),
        P(),
        P(("rep", "tp"), None),
        P(("rep", "tp"), None),
        P(("rep", "tp")),
        P(),
        P(),
        P(),
        P(None, "tp"),
        P(),
        P("tp", None),
        P(),
        P(("rep", "tp"), None, None),
        P(("rep", "tp"), None, None),
    )
    out_specs = (P(("rep", "tp"), None), P(("rep", "tp"), None, None))
    body = grid_body if (mesh.shape["rep"], mesh.shape["tp"]) == (4, 8) else general_body
    return jax.shard_map(body, mesh=mesh, in_specs=in_specs, out_specs=out_specs, check_vma=False)
```

```python
import functools
import math

import jax
import jax.numpy as jnp
from jax import lax
from jax.experimental import pallas as pl
from jax.experimental.pallas import tpu as pltpu
from jax.sharding import PartitionSpec as P


def passed_along(block, axis, distance):
    devices = range(lax.axis_size(axis))
    route = [(i - distance, i) for i in devices if i - distance in devices]
    return lax.ppermute(block, axis, route)


def root_mean_norm(value_rows, gain):
    return (
        value_rows
        * lax.rsqrt(jnp.mean(value_rows * value_rows, axis=-1, keepdims=True) + 1e-06)
        * gain
    )


def apply_rotary(value_rows, token_positions):
    half_dim = value_rows.shape[-1] // 2
    frequency = jnp.exp(
        jnp.arange(half_dim, dtype=jnp.float32)
        * (-2.0 * math.log(1000000.0) / value_rows.shape[-1])
    )
    angles = token_positions[:, None] * frequency[None, :]
    cosine = jnp.cos(angles)[:, None, :]
    sine_part = jnp.sin(angles)[:, None, :]
    first = value_rows[..., :half_dim]
    second = value_rows[..., half_dim:]
    return jnp.concatenate(
        [first * cosine - second * sine_part, second * cosine + first * sine_part], axis=-1
    )


def general_body(
    tokens,
    seg_ids,
    expert_ids,
    gates,
    page_table,
    attn_gain,
    q_gain,
    key_norm_gain,
    w_query,
    w_keyval,
    w_out,
    moe_gain,
    w_gate_up,
    w_down,
):
    tok_rows, width = tokens.shape
    tp_count = lax.axis_size("tp")
    rep_count = lax.axis_size("rep")
    rep_index = lax.axis_index("rep")
    tp_index = lax.axis_index("tp")
    group_rows = tok_rows * tp_count
    head_dim = q_gain.shape[0]
    q_width = w_query.shape[1]
    heads_here = q_width // head_dim
    kv_heads = w_keyval.shape[1] // (2 * head_dim)
    kv_width = kv_heads * head_dim
    per_key_value = heads_here * tp_count // kv_heads
    own_head = tp_index * heads_here // per_key_value
    first_row = (rep_index * tp_count + tp_index) * tok_rows
    local_pos = (first_row + jnp.arange(tok_rows, dtype=jnp.int32)).astype(jnp.float32)
    normed = root_mean_norm(tokens.astype(jnp.float32), attn_gain).astype(jnp.bfloat16)
    key_value_rows = jnp.dot(normed, w_keyval, preferred_element_type=jnp.float32)
    rotary_output = apply_rotary(
        root_mean_norm(
            key_value_rows[:, :kv_width].reshape(tok_rows, kv_heads, head_dim), key_norm_gain
        ),
        local_pos,
    )
    stored_cache = jnp.concatenate(
        [rotary_output.reshape(tok_rows, kv_width), key_value_rows[:, kv_width:]], axis=1
    ).astype(jnp.bfloat16)
    page_count = page_table.shape[0]
    placement_matrix = (
        page_table[None, :] == jnp.arange(page_count, dtype=jnp.int32)[:, None]
    ).astype(jnp.bfloat16)
    cache = jnp.dot(
        placement_matrix, stored_cache.reshape(page_count, -1), preferred_element_type=jnp.float32
    )
    cache = cache.astype(jnp.bfloat16).reshape(page_count, tok_rows // page_count, 2 * kv_width)
    projected = jnp.dot(
        lax.all_gather(normed, "tp", axis=0, tiled=True),
        w_query,
        preferred_element_type=jnp.float32,
    )
    group_start = rep_index * group_rows
    group_pos = group_start + jnp.arange(group_rows, dtype=jnp.int32)
    group_posf = group_pos.astype(jnp.float32)
    query = root_mean_norm(projected.reshape(group_rows, heads_here, head_dim), q_gain)
    query = apply_rotary(query, group_posf).astype(jnp.bfloat16)
    gathered = lax.all_gather(stored_cache, "tp", axis=0, tiled=True)
    own_keys = lax.dynamic_slice_in_dim(gathered, own_head * head_dim, head_dim, 1)
    own_values = lax.dynamic_slice_in_dim(gathered, kv_width + own_head * head_dim, head_dim, 1)
    earlier_keys, earlier_values = passed_along((own_keys, own_values), "rep", 1)
    own_seg = lax.dynamic_slice_in_dim(seg_ids, group_start, group_rows, 0)
    earlier_seg = lax.dynamic_slice_in_dim(
        seg_ids, jnp.maximum(group_start - group_rows, 0), group_rows, 0
    )
    earlier_seg = jnp.where(rep_index > 0, earlier_seg, -1)
    keys_all = jnp.concatenate([earlier_keys, own_keys], axis=0)
    values_all = jnp.concatenate([earlier_values, own_values], axis=0)
    key_seg = jnp.concatenate([earlier_seg, own_seg], axis=0)
    key_pos = group_start - group_rows + jnp.arange(2 * group_rows, dtype=jnp.int32)
    block_rows = min(512, group_rows)
    block_count = group_rows // block_rows
    scale = head_dim ** (-0.5)

    def attend(inputs):
        block_query, block_pos, block_seg = inputs
        scores = (
            jnp.einsum("bhd,kd->hbk", block_query, keys_all, preferred_element_type=jnp.float32)
            * scale
        )
        allowed = (key_seg[None, :] == block_seg[:, None]) & (
            key_pos[None, :] <= block_pos[:, None]
        )
        scores = jnp.where(allowed[None], scores, -jnp.inf)
        largest = jnp.max(scores, axis=-1, keepdims=True)
        weights = jnp.exp(scores - largest)
        totals = jnp.sum(weights, axis=-1, keepdims=True)
        mixed = (
            jnp.einsum(
                "hbk,kd->hbd",
                weights.astype(jnp.bfloat16),
                values_all,
                preferred_element_type=jnp.float32,
            )
            / totals
        )
        return jnp.transpose(mixed.astype(jnp.bfloat16), (1, 0, 2)).reshape(
            block_rows, heads_here * head_dim
        )

    attended = lax.map(
        attend,
        (
            query.reshape(block_count, block_rows, heads_here, head_dim),
            group_pos.reshape(block_count, block_rows),
            own_seg.reshape(block_count, block_rows),
        ),
    )
    attended = attended.reshape(group_rows, heads_here * head_dim)
    rows = attended
    term = jnp.dot(rows, w_out, preferred_element_type=jnp.float32).astype(jnp.bfloat16)
    mixed_sum = lax.psum_scatter(
        lax.optimization_barrier(term).astype(jnp.float32).astype(jnp.bfloat16),
        "tp",
        scatter_dimension=0,
        tiled=True,
    ).astype(jnp.float32)
    residual = (tokens.astype(jnp.float32) + mixed_sum).astype(jnp.bfloat16)
    normed_moe = root_mean_norm(residual.astype(jnp.float32), moe_gain).astype(jnp.bfloat16)
    expert_count = rep_count * tp_count * w_gate_up.shape[0]
    top_count = expert_ids.shape[1]
    capacity = max(2, 3 * tok_rows * top_count // (2 * expert_count))
    hidden_units = w_down.shape[1]
    flat = expert_ids.reshape(-1)
    onehot = (flat[:, None] == jnp.arange(expert_count, dtype=jnp.int32)[None, :]).astype(jnp.int32)
    rank = jnp.sum((jnp.cumsum(onehot, axis=0) - 1) * onehot, axis=1)
    target = (flat * capacity + rank).reshape(tok_rows, top_count)
    match = (
        target[:, :, None] == jnp.arange(expert_count * capacity, dtype=jnp.int32)[None, None, :]
    )
    dispatch = jnp.any(match, axis=1).astype(jnp.bfloat16)
    combine = jnp.sum(jnp.where(match, gates[:, :, None].astype(jnp.float32), 0.0), axis=1).astype(
        jnp.bfloat16
    )
    outgoing = lax.dot_general(
        dispatch, normed_moe, (((0,), (0,)), ((), ())), preferred_element_type=jnp.float32
    )
    outgoing = outgoing.astype(jnp.bfloat16).reshape(expert_count, capacity, width)
    received = lax.all_to_all(outgoing, ("rep", "tp"), split_axis=0, concat_axis=0, tiled=True)
    rows = received.reshape(-1, width)
    gate_up = jnp.dot(rows, w_gate_up[0], preferred_element_type=jnp.float32)
    act = (jax.nn.silu(gate_up[:, :hidden_units]) * gate_up[:, hidden_units:]).astype(jnp.bfloat16)
    result = jnp.dot(act, w_down[0], preferred_element_type=jnp.float32).astype(jnp.bfloat16)
    returned = lax.all_to_all(
        result.reshape(received.shape), ("rep", "tp"), split_axis=0, concat_axis=0, tiled=True
    )
    combined = jnp.dot(
        combine,
        returned.reshape(expert_count * capacity, width),
        preferred_element_type=jnp.float32,
    )
    hidden_out = (residual.astype(jnp.float32) + combined).astype(jnp.bfloat16)
    return (hidden_out, cache)


KEY_BLOCK = 256
MASKED = -1e30


def moved(block, change):
    route = []
    for y in range(2):
        for core in range(2):
            for z in range(4):
                for x in range(2):
                    to_y, to_core, to_z, to_x = change(y, core, z, x)
                    route.append(
                        ((y * 2 + core) * 8 + z * 2 + x, (to_y * 2 + to_core) * 8 + to_z * 2 + to_x)
                    )
    return lax.ppermute(block, ("rep", "tp"), route)


def other_x(block):
    return moved(block, lambda y, core, z, x: (y, core, z, 1 - x))


def other_y(block):
    return moved(block, lambda y, core, z, x: (1 - y, core, z, x))


def other_core(block):
    return moved(block, lambda y, core, z, x: (y, 1 - core, z, x))


def across(block, over_y):
    if over_y:
        return moved(block, lambda y, core, z, x: (1 - y, 1 - core, z, x))
    return moved(block, lambda y, core, z, x: (y, 1 - core, z, 1 - x))


def other_z(block, k):
    return moved(block, lambda y, core, z, x: (y, core, z ^ k, x))


def sum_of(a, b):
    return (a.astype(jnp.float32) + b.astype(jnp.float32)).astype(jnp.bfloat16)


def after(value, earlier):
    return lax.optimization_barrier((value, earlier))[0]


def attention_kernel(
    first_slot, place, low, projected, gain, cosine, sine, start, kv_here, kv_side, kv_before, kv_before_side, out,
    keys, values, acc, peak, total,
):
    z, x, slot = place[0], place[1], first_slot + pl.program_id(0)
    rows = projected.shape[0]
    head = gain.shape[1]
    heads = projected.shape[1] // head
    half = head // 2

    @pl.when(pl.program_id(0) == 0)
    def _():
        for first, near, far in ((0, kv_before, kv_before_side), (8, kv_here, kv_side)):
            for k in range(4):
                at = jnp.bitwise_xor(z, k) * 2
                for source, shift in ((near, x), (far, 1 - x)):
                    row = pl.multiple_of((first + at + shift) * rows, rows)
                    keys[pl.ds(row, rows), :] = source[k, :rows, :head]
                    values[:, pl.ds(row, rows)] = source[k, :rows, head:].astype(jnp.float32).T.astype(jnp.bfloat16)

    gain_column = jnp.broadcast_to(gain[...], (rows, head)).T
    turned = []
    for h in range(heads):
        q = projected[:, h * head : (h + 1) * head].T
        q = q * lax.rsqrt(jnp.mean(q * q, axis=0, keepdims=True) + 1e-06) * gain_column
        first, second = q[:half], q[half:]
        turned.append(
            jnp.concatenate(
                [first * cosine[0] - second * sine[0], second * cosine[0] + first * sine[0]], axis=0
            )
        )
    query = (jnp.concatenate(turned, axis=1) * (head**-0.5 * math.log2(math.e))).astype(jnp.bfloat16)
    acc[...] = jnp.zeros_like(acc)
    total[...] = jnp.zeros_like(total)
    peak[...] = jnp.full_like(peak, MASKED)
    position = (8 + jnp.bitwise_xor(z, slot) * 2 + x) * rows
    own_position = position + lax.broadcasted_iota(jnp.int32, (KEY_BLOCK, rows), 1)
    own_start = start[0]

    def step(j, _):
        row = pl.multiple_of(j * KEY_BLOCK, KEY_BLOCK)
        scores = jnp.dot(keys[pl.ds(row, KEY_BLOCK), :], query, preferred_element_type=jnp.float32)
        key_position = row + lax.broadcasted_iota(jnp.int32, (KEY_BLOCK, rows), 0)
        allowed = (key_position >= own_start) & (key_position <= own_position)
        scores = jnp.concatenate(
            [jnp.where(allowed, scores[:, h * rows : (h + 1) * rows], MASKED) for h in range(heads)], axis=1
        )
        largest = jnp.maximum(peak[...], jnp.max(scores, axis=0, keepdims=True))
        fade = jnp.exp2(peak[...] - largest)
        weights = jnp.exp2(scores - largest)
        total[...] = total[...] * fade + jnp.sum(weights, axis=0, keepdims=True)
        acc[...] = acc[...] * fade + jnp.dot(
            values[:, pl.ds(row, KEY_BLOCK)], weights.astype(jnp.bfloat16), preferred_element_type=jnp.float32
        )
        peak[...] = largest
        return 0

    lax.fori_loop(low[slot], (position + rows - 1) // KEY_BLOCK + 1, step, 0)
    mixed = acc[...] / total[...]
    for h in range(heads):
        out[:, h * head : (h + 1) * head] = mixed[:, h * rows : (h + 1) * rows].T.astype(out.dtype)


def attend_slots(first_slot, place, low, projected, q_gain, cosine, sine, start, kv):
    rows = start.shape[2]
    slots = projected.shape[0] // rows
    head = q_gain.shape[0]
    width = projected.shape[1]
    whole = lambda *shape: pl.BlockSpec(shape, lambda s, *_: (0,) * len(shape))
    return pl.pallas_call(
        functools.partial(attention_kernel, first_slot),
        grid_spec=pltpu.PrefetchScalarGridSpec(
            num_scalar_prefetch=2,
            grid=(slots,),
            in_specs=[
                pl.BlockSpec((rows, width), lambda s, *_: (s, 0)),
                whole(1, head),
                pl.BlockSpec((1, head // 2, rows), lambda s, *_: (first_slot + s, 0, 0)),
                pl.BlockSpec((1, head // 2, rows), lambda s, *_: (first_slot + s, 0, 0)),
                pl.BlockSpec((1, 1, rows), lambda s, *_: (first_slot + s, 0, 0)),
            ]
            + [whole(*part.shape) for part in kv],
            out_specs=pl.BlockSpec((rows, width), lambda s, *_: (s, 0)),
            scratch_shapes=[
                pltpu.VMEM((16 * rows, head), jnp.bfloat16),
                pltpu.VMEM((head, 16 * rows), jnp.bfloat16),
                pltpu.VMEM((head, width // head * rows), jnp.float32),
                pltpu.VMEM((1, width // head * rows), jnp.float32),
                pltpu.VMEM((1, width // head * rows), jnp.float32),
            ],
        ),
        out_shape=jax.ShapeDtypeStruct((slots * rows, width), jnp.bfloat16),
        compiler_params=pltpu.CompilerParams(vmem_limit_bytes=40 * 2**20),
        cost_estimate=pl.CostEstimate(
            flops=4 * slots * rows * width * 4 * rows,
            bytes_accessed=8 * 2**20,
            transcendentals=slots * width * rows,
        ),
        name="attention",
    )(place, low, projected, q_gain.reshape(1, head), cosine, sine, start, *kv)


def keyval_kernel(tokens, gain, key_gain, cosine, sine, w_key, w_value, out, normed):
    @pl.when(pl.program_id(0) == 0)
    def _():
        normed[...] = root_mean_norm(tokens[...].astype(jnp.float32), gain[...]).astype(jnp.bfloat16)

    head = key_gain.shape[1]
    half = head // 2
    k = jnp.dot(normed[...], w_key[...], preferred_element_type=jnp.float32).T
    k = k * lax.rsqrt(jnp.mean(k * k, axis=0, keepdims=True) + 1e-06)
    k = k * jnp.broadcast_to(key_gain[...], (normed.shape[0], head)).T
    first, second = k[:half], k[half:]
    k = jnp.concatenate(
        [first * cosine[0] - second * sine[0], second * cosine[0] + first * sine[0]], axis=0
    )
    out[0, :, :head] = k.T.astype(out.dtype)
    v = jnp.dot(normed[...], w_value[...], preferred_element_type=jnp.float32)
    out[0, :, head:] = v.astype(out.dtype)


def keyval_by_head(tokens, attn_gain, key_norm_gain, cosine, sine, w_keyval):
    rows, width = tokens.shape
    head = key_norm_gain.shape[0]
    heads = w_keyval.shape[1] // (2 * head)
    whole = lambda *shape: pl.BlockSpec(shape, lambda h: (0,) * len(shape))
    return pl.pallas_call(
        keyval_kernel,
        grid=(heads,),
        in_specs=[
            whole(rows, width),
            whole(1, width),
            whole(1, head),
            pl.BlockSpec((1, head // 2, rows), lambda h: (0, 0, 0)),
            pl.BlockSpec((1, head // 2, rows), lambda h: (0, 0, 0)),
            pl.BlockSpec((width, head), lambda h: (0, h)),
            pl.BlockSpec((width, head), lambda h: (0, heads + h)),
        ],
        out_specs=pl.BlockSpec((1, rows, 2 * head), lambda h: (h, 0, 0)),
        out_shape=jax.ShapeDtypeStruct((heads, rows, 2 * head), jnp.bfloat16),
        scratch_shapes=[pltpu.VMEM((rows, width), jnp.bfloat16)],
        compiler_params=pltpu.CompilerParams(vmem_limit_bytes=60 * 2**20),
        cost_estimate=pl.CostEstimate(
            flops=2 * rows * width * w_keyval.shape[1], bytes_accessed=5 * 2**20, transcendentals=0
        ),
        name="keyval",
    )(tokens, attn_gain.reshape(1, width), key_norm_gain.reshape(1, head), cosine, sine, w_keyval, w_keyval)


def grid_body(
    tokens,
    seg_ids,
    expert_ids,
    gates,
    page_table,
    attn_gain,
    q_gain,
    key_norm_gain,
    w_query,
    w_keyval,
    w_out,
    moe_gain,
    w_gate_up,
    w_down,
):
    rows, width = tokens.shape
    head = q_gain.shape[0]
    kv_heads = w_keyval.shape[1] // (2 * head)
    kv_width = kv_heads * head
    rep, tp = lax.axis_index("rep"), lax.axis_index("tp")
    y, core, z, x = rep // 2, rep % 2, tp // 2, tp % 2
    group_rows = 8 * rows
    group_start = rep * group_rows
    slots = range(4)

    slot_start = [group_start + ((z ^ k) * 2 + x) * rows for k in slots]
    slot_position = jnp.stack([at + jnp.arange(rows, dtype=jnp.int32) for at in slot_start])
    frequency = jnp.exp(
        jnp.arange(head // 2, dtype=jnp.float32) * (-2.0 * math.log(1000000.0) / head)
    )
    angles = frequency[None, :, None] * slot_position.astype(jnp.float32)[:, None, :]
    cosine, sine = jnp.cos(angles), jnp.sin(angles)

    by_head = keyval_by_head(tokens, attn_gain, key_norm_gain, cosine, sine, w_keyval)
    part = w_query.shape[1] // 4
    quarter = y * 2 + core
    far = other_z(tokens, 2)
    query_x = other_x(lax.dynamic_slice_in_dim(w_query, quarter * part, part, 1))
    by_head, late_segs, query_x, w_out = lax.optimization_barrier((by_head, seg_ids, query_x, w_out))
    out_x = other_x(lax.dynamic_slice_in_dim(w_out, quarter * part, part, 0))

    top = expert_ids.shape[1]
    routes = jnp.concatenate([expert_ids.T.astype(jnp.bfloat16), gates.T], axis=0)
    routes = jnp.concatenate([routes, other_y(routes)], axis=1)
    pick = lambda h: jnp.concatenate(
        [lax.dynamic_index_in_dim(by_head, h, 0, keepdims=False), routes], axis=0
    )
    kv_parts = [other_z(pick(z ^ k), k) for k in (1, 2, 3)]
    query_y = other_y(after(query_x, kv_parts[0]))
    kv_here = jnp.stack([pick(z)] + kv_parts)
    kv_here, out_x, far, w_query, w_out = lax.optimization_barrier((kv_here, out_x, far, w_query, w_out))
    kv_before, kv_side = passed_along(kv_here, "rep", 1), other_x(kv_here)
    farther, out_y = other_z(far, 1), other_y(out_x)
    kv_side, query_y = lax.optimization_barrier((kv_side, query_y))
    kv_before_side = passed_along(kv_side, "rep", 1)
    query_two = jnp.concatenate([query_x, query_y], axis=1)
    query_far = other_core(query_two)
    kv_before, query_far, farther, out_y = lax.optimization_barrier(
        (kv_before, query_far, farther, out_y)
    )
    w_query_wide = jnp.concatenate([w_query, query_two, query_far], axis=1)
    out_two = jnp.concatenate([out_x, out_y], axis=0)
    near = other_z(after(tokens, farther), 1)
    w_out_wide = jnp.concatenate([w_out, out_two, other_core(out_two)], axis=0)
    raw = [tokens, near, far, farther]

    pages = page_table.shape[0]
    stored = jnp.transpose(by_head.reshape(kv_heads, rows, 2, head), (1, 2, 0, 3))
    placing = (page_table[None, :] == jnp.arange(pages, dtype=jnp.int32)[:, None]).astype(jnp.bfloat16)
    cache = jnp.dot(placing, stored.reshape(pages, -1), preferred_element_type=jnp.float32)
    cache = cache.astype(jnp.bfloat16).reshape(pages, rows // pages, 2 * kv_width)

    slot_seg = jnp.concatenate(
        [lax.dynamic_slice_in_dim(late_segs, at, rows, 0) for at in slot_start]
    )
    starts = jnp.sum((late_segs[None, :] < slot_seg[:, None]).astype(jnp.int32), axis=1)
    starts = (starts - (group_start - group_rows)).reshape(4, 1, rows)
    low = starts[:, 0, 0] // KEY_BLOCK

    def projection(first):
        lines = jnp.concatenate(raw[first : first + 2], axis=0).astype(jnp.float32)
        lines = root_mean_norm(lines, attn_gain).astype(jnp.bfloat16)
        return jnp.dot(lines, w_query_wide, preferred_element_type=jnp.float32)

    def attended(first, projected):
        return attend_slots(
            first,
            jnp.stack([z, x]),
            low,
            projected,
            q_gain,
            cosine,
            sine,
            starts,
            (kv_here, kv_side, kv_before, kv_before_side),
        )

    def term_of(part):
        term = jnp.dot(part, w_out_wide, preferred_element_type=jnp.float32).astype(jnp.bfloat16)
        return term[:rows], term[rows:]

    attended_far = attended(2, projection(2))
    term_2, term_3 = term_of(attended_far)
    term_2, raw[1] = lax.optimization_barrier((term_2, near))
    far_3 = other_z(term_3, 1)
    far = other_z(sum_of(term_2, far_3), 2)
    term_0, term_1 = term_of(attended(0, after(projection(0), term_3)))
    near = other_z(term_1, 1)
    mixed_sum = term_0.astype(jnp.float32) + near.astype(jnp.float32) + far.astype(jnp.float32)
    residual = (tokens.astype(jnp.float32) + mixed_sum).astype(jnp.bfloat16)
    normed_moe = root_mean_norm(residual.astype(jnp.float32), moe_gain).astype(jnp.bfloat16)

    turned = (False, True, False, True)
    routes, over_y = kv_here[:, rows:, :rows], kv_here[:, rows:, rows:]
    over_x, corner_routes = kv_side[:, rows:, :rows], kv_side[0, rows:, rows:]
    capacity = max(2, 3 * rows * top // (2 * 32))
    pair = 2 * capacity
    mine = [rep * 8 + tp, (rep ^ 1) * 8 + tp]
    earlier = (jnp.arange(rows)[:, None] < jnp.arange(rows)[None, :]).astype(jnp.bfloat16)

    def matrices(blocks, experts):
        blocks = blocks.reshape(blocks.shape[:2] + (2, top, rows))
        experts = experts.astype(jnp.bfloat16)
        hits = blocks[:, :, 0][:, :, None] == experts[:, None, :, None, None]
        weight = jnp.sum(jnp.where(hits, blocks[:, :, 1][:, :, None].astype(jnp.float32), 0.0), axis=3)
        hit = jnp.any(hits, axis=3)
        place = jnp.dot(
            hit.reshape(-1, rows).astype(jnp.bfloat16), earlier, preferred_element_type=jnp.float32
        ).reshape(hit.shape)
        chosen = (
            place[..., None, :].astype(jnp.int32) == jnp.arange(capacity, dtype=jnp.int32)[:, None]
        ) & hit[..., None, :]
        weighted = jnp.where(chosen, weight[..., None, :], 0.0).astype(jnp.bfloat16)
        flat = hit.shape[:2] + (-1, rows)
        return chosen.astype(jnp.bfloat16).reshape(flat), weighted.reshape(flat)

    pairs = [jnp.stack([routes[k], (over_y if turned[k] else over_x)[k]]) for k in slots]
    theirs = [[e ^ 1 if turned[k] else e ^ 16 for e in mine] for k in slots]
    chosen, weighted = matrices(
        jnp.stack(pairs + [jnp.stack([over_y[0], corner_routes])]),
        jnp.stack([jnp.stack(mine + others) for others in theirs + [mine]]),
    )
    chosen_0 = jnp.concatenate([chosen[0, :, :pair], chosen[4, :, :pair]], axis=0)

    def experts_of(slot_rows_in):
        gate_up = jnp.dot(slot_rows_in, w_gate_up[0], preferred_element_type=jnp.float32)
        hidden = w_down.shape[1]
        act = (jax.nn.silu(gate_up[:, :hidden]) * gate_up[:, hidden:]).astype(jnp.bfloat16)
        return jnp.dot(act, w_down[0], preferred_element_type=jnp.float32).astype(jnp.bfloat16)

    together = lambda *values: lax.optimization_barrier(values)

    def picks(k, block, side):
        picked = lax.dot_general(
            chosen[k], jnp.stack([block, side]), (((2,), (1,)), ((0,), (0,))), preferred_element_type=jnp.float32
        ).astype(jnp.bfloat16)
        return picked[:, :pair], picked[:, pair:]

    half = rows // 2
    near, far = other_z(normed_moe, 1), other_z(normed_moe, 2)
    side_x, side_y = together(other_x(normed_moe), other_y(normed_moe))
    near, far, *corner = together(near, far, other_y(side_x[:half]), other_x(side_y[half:]))
    side_1, side_2, farther = other_y(near), other_x(far), other_z(far, 1)
    corner = jnp.concatenate(corner, axis=0)
    picked_0 = lax.dot_general(
        chosen_0,
        jnp.stack([normed_moe, side_x, side_y, corner]),
        (((2,), (1,)), ((0,), (0,))),
        preferred_element_type=jnp.float32,
    ).astype(jnp.bfloat16)
    side_2, farther, picked_0 = together(side_2, farther, picked_0)
    mine_2, theirs_2 = picks(2, far, side_2)
    side_3 = other_y(farther)
    side_1, mine_2, theirs_2 = together(side_1, mine_2, theirs_2)
    mine_1, theirs_1 = picks(1, near, side_1)
    theirs_1 = other_x(theirs_1)

    def over_second(to_y, to_y_across, to_x, to_x_across):
        return together(
            other_y(to_y), across(to_y_across, True), other_x(to_x), across(to_x_across, False)
        )

    def experts_on(*parts):
        return experts_of(jnp.concatenate(parts, axis=0).reshape(-1, width)).reshape(-1, capacity, width)

    kept = lambda *parts: jnp.concatenate([part[:, :capacity] for part in parts], axis=0)
    traded = lambda *parts: other_core(jnp.concatenate([part[:, capacity:] for part in parts], axis=0))
    result_0 = experts_on(kept(picked_0), traded(picked_0))
    result_12 = experts_on(kept(mine_1, mine_2), traded(mine_1, mine_2))
    side_3, theirs_2, result_0, result_12 = together(side_3, theirs_2, result_0, result_12)
    mine_3, theirs_3 = picks(3, farther, side_3)
    theirs_3, theirs_1 = together(theirs_3, theirs_1)
    late = traded(mine_3, theirs_1)
    got = over_second(
        theirs_2[:, :capacity], theirs_2[:, capacity:], theirs_3[:, :capacity], theirs_3[:, capacity:]
    )
    *got, late = together(*got, late)
    got, late = together(experts_on(*got), late)
    result_31 = experts_on(kept(mine_3, theirs_1), late)
    both = lambda result: jnp.concatenate([result[:4], other_core(result[4:])], axis=1)
    here_1, here_2 = jnp.split(both(result_12), 2)
    here_3, there_1 = jnp.split(both(result_31), 2)

    def summed(k, here, there):
        total = lax.dot_general(
            weighted[k],
            jnp.concatenate([here, there], axis=1),
            (((1,), (1,)), ((0,), (0,))),
            preferred_element_type=jnp.float32,
        ).astype(jnp.bfloat16)
        return total[0], total[1]

    here_0, there_0 = jnp.split(both(result_0), 2)
    there = over_second(got[:2], got[2:4], got[4:6], got[6:])
    there_2, there_3 = jnp.concatenate(there[:2], axis=1), jnp.concatenate(there[2:], axis=1)
    (own_2, side_2), (own_3, side_3) = summed(2, here_2, there_2), summed(3, here_3, there_3)
    side_2, side_3, there_0, there_1 = together(other_x(side_2), other_y(side_3), there_0, there_1)
    far_3 = other_z(sum_of(own_3, side_3), 1)
    there_0, there_1 = together(other_y(there_0), other_x(there_1))
    (own_0, side_0), (own_1, side_1) = summed(0, here_0, there_0), summed(1, here_1, there_1)
    far = own_2.astype(jnp.float32) + side_2.astype(jnp.float32) + far_3.astype(jnp.float32)
    far = other_z(far.astype(jnp.bfloat16), 2)
    side_0 = other_x(side_0)
    near, later = sum_of(own_1[:half], other_y(side_1[:half])), other_y(side_1[half:])
    near, later = together(near, later)
    near = [other_z(near, 1), other_z(sum_of(own_1[half:], later), 1)]
    near = jnp.concatenate(near, axis=0)
    combined = residual.astype(jnp.float32)
    for value in (far, near, own_0, side_0):
        combined = combined + value.astype(jnp.float32)
    return (combined.astype(jnp.bfloat16), cache)


def solution(mesh):
    in_specs = (
        P(("rep", "tp"), None),
        P(),
        P(("rep", "tp"), None),
        P(("rep", "tp"), None),
        P(("rep", "tp")),
        P(),
        P(),
        P(),
        P(None, "tp"),
        P(),
        P("tp", None),
        P(),
        P(("rep", "tp"), None, None),
        P(("rep", "tp"), None, None),
    )
    out_specs = (P(("rep", "tp"), None), P(("rep", "tp"), None, None))
    body = grid_body if (mesh.shape["rep"], mesh.shape["tp"]) == (4, 8) else general_body
    return jax.shard_map(body, mesh=mesh, in_specs=in_specs, out_specs=out_specs, check_vma=False)
```
